32 devices in a mesh: blk: 8 (over y, x, core), head: 4 (over z).
Axes of the slice: x: 2, y: 2, z: 4, core: 2. Of those that a mesh axis runs over, the one named last changes fastest.
Arguments:
- queries: bfloat16 [4096, 8192], P('blk', 'head'), may hold values from -120 to 120
- keys: bfloat16 [4096, 1024], P('blk', 'head'), may hold values from -6.5 to 6.5
- values: bfloat16 [4096, 1024], P('blk', 'head'), may hold values from -6 to 6
- w_out: bfloat16 [8192, 8192], P('head'), may hold values from -0.09375 to 0.09375
- order: int32 [16], replicated, may hold values from 0 to 15, each once
Outputs:
- mixed: bfloat16 [4096, 8192], P('blk', 'head')
The draws below stay inside these ranges and needn't reach their ends.
Inputs may be any that keep to these rules, and one draw needn't show every extreme that they name: `order`: A permutation of 0 to 15.
All inputs are finite; a program needn't handle non-finite values.
Results may differ from the reference program's by a relative error of at most 0.015.
Values may be sent and summed in bfloat16 or wider, within the bound.
No kernel may reach another device: no remote copies, remote signals or barrier semaphores. Data moves between devices by JAX's collectives and lax.ppermute only.
A program may use at most 128 MiB of HBM per device.

```python
import math
import jax
import jax.numpy as jnp
from jax import lax

D = 8192
H = 64
KVH = 8
HD = 128
TOK_DEV = 512
SEQ = 4096
BLOCKS = 16


def draw_keys(key, part):
    drawn = jnp.clip(jax.random.normal(jax.random.fold_in(key, 13), (SEQ, KVH * HD), jnp.float32), -6.0, 6.0)
    return drawn.astype(jnp.bfloat16)


def draw_queries(key, part):
    drawn = jnp.clip(jax.random.normal(jax.random.fold_in(key, 31), (SEQ, H * HD), jnp.float32), -6.0, 6.0)
    return drawn.astype(jnp.bfloat16)


def with_spikes(array, rng, source, target, parts, factor):
    owner, partner = [(jnp.arange(array.shape[dim]) // (array.shape[dim] // parts)).reshape([-1 if axis == dim else 1 for axis in range(array.ndim)]) for dim in (source, target)]
    chosen = jax.random.permutation(rng, parts)[partner]
    strong = (owner == chosen) | (owner == (partner + parts // 2) % parts)
    return jnp.where(strong, factor * array, array)


def levels(own_key, extent, cuts, smallest, largest):
    gain = 1.0
    for axis_at, parts in cuts:
        draws = jax.random.uniform(jax.random.fold_in(jax.random.fold_in(own_key, 6), axis_at), (parts,), jnp.float32, smallest / len(cuts), largest / len(cuts))
        gain = gain * jnp.repeat(jnp.exp(draws), extent[axis_at] // parts).reshape((-1,) + (1,) * (len(extent) - 1 - axis_at))
    return gain


def normal_values(stream_key, dims, scale, most, cuts=(), kind=jnp.bfloat16):
    entries = scale * jax.random.normal(stream_key, dims, jnp.float32)
    if cuts:
        entries = entries * levels(stream_key, dims, cuts, -0.22, 0.18)
    return jnp.clip(entries, -most, most).astype(kind)


def gaussian_with(own_key, dims, deviation, reach, shards, heavy, kind=jnp.bfloat16):
    values = deviation * jax.random.normal(own_key, dims, jnp.float32)
    if shards:
        values = values * levels(own_key, dims, shards, -0.22, 0.18)
    return jnp.clip(with_spikes(values, jax.random.fold_in(own_key, 3), *heavy), -reach, reach).astype(kind)


def setup_inputs(seed: int = 0) -> dict:
    key_list = jax.random.split(jax.random.key(seed), 6)
    queries = draw_queries(jax.random.fold_in(key_list[5], 71), 0)
    keys = draw_keys(jax.random.fold_in(key_list[5], 71), 0)
    values = normal_values(key_list[2], (SEQ, KVH * HD), 1.0, 6.0, ((0, 8), (1, 4)))
    w_out = gaussian_with(key_list[3], (H * HD, D), (H * HD) ** -0.5, 0.09375, ((0, 4),), (0, 1, 4, 2.0))
    order = jax.random.permutation(key_list[4], BLOCKS).astype(jnp.int32)
    return {"queries": queries, "keys": keys, "values": values, "w_out": w_out, "order": order}


def reference(queries, keys, values, w_out, order):
    seq = queries.shape[0]
    half = TOK_DEV // 2
    group = H // KVH
    scale = HD ** -0.5
    rows = jnp.arange(seq, dtype=jnp.int32)
    position = (order[rows // half] * half + rows % half).astype(jnp.int32)
    qb = math.gcd(seq, 512)
    nq = seq // qb
    q_all = queries.reshape(nq, qb, KVH, group, HD)
    k_all = keys.reshape(seq, KVH, HD)
    v_all = values.reshape(seq, KVH, HD)
    qpos_all = position.reshape(nq, qb)

    def per_head(kv_index):
        k_head = lax.dynamic_index_in_dim(k_all, kv_index, 1, keepdims=False).astype(jnp.float32)
        v_head = lax.dynamic_index_in_dim(v_all, kv_index, 1, keepdims=False).astype(jnp.float32)

        def per_block(block):
            q_block = lax.dynamic_index_in_dim(q_all[block], kv_index, 1, keepdims=False).astype(jnp.float32)
            qpos = qpos_all[block]
            score = jnp.einsum("tgd,nd->tgn", q_block, k_head) * scale
            visible = position[None, None, :] <= qpos[:, None, None]
            score = jnp.where(visible, score, -1e30)
            top = jnp.max(score, axis=-1, keepdims=True)
            weight = jnp.where(visible, jnp.exp(score - top), 0.0)
            total = jnp.sum(weight, axis=-1)
            weight_low = weight.astype(jnp.bfloat16).astype(jnp.float32)
            summed = jnp.einsum("tgn,nd->tgd", weight_low, v_head)
            return (summed / total[:, :, None]).astype(jnp.bfloat16)

        return lax.map(per_block, jnp.arange(nq))

    heads = lax.map(per_head, jnp.arange(KVH))
    attended = jnp.transpose(heads, (1, 2, 0, 3, 4)).reshape(seq, H * HD)
    return jnp.dot(attended, w_out, preferred_element_type=jnp.float32).astype(jnp.bfloat16)
```

```python
import functools
import math

import jax
import jax.numpy as jnp
from jax import lax
from jax.experimental import pallas as pl
from jax.experimental.pallas import tpu as pltpu
from jax.sharding import PartitionSpec as P

HD = 128
NT = (((1,), (1,)), ((), ()))


def attend_kernel(half, tile, chunk, order_ref, me_ref, q_ref, k_ref, v_ref, o_ref,
                  inv, q_rows, v_wide, acc, top):
    blocks = order_ref.shape[0]
    tok = q_ref.shape[0]
    group = q_ref.shape[1] // HD
    rows = group * tok
    factor = HD ** (-0.5) * math.log2(math.e)
    start = chunk * tok
    offset = start % half
    own = me_ref[0] + start // half

    def invert(b, _):
        inv[order_ref[b]] = b
        return 0

    lax.fori_loop(0, blocks, invert, 0)
    for g in range(group):
        q_rows[g * tok:(g + 1) * tok, :] = q_ref[:, g * HD:(g + 1) * HD]
    v_wide[:, :HD] = v_ref[...]
    v_wide[:, HD:] = jnp.ones((v_wide.shape[0], HD), v_wide.dtype)
    earlier = order_ref[own]

    def block_of(ref, b):
        return ref[pl.ds(pl.multiple_of(b * half, half), half), :]

    def first(blocks_in):
        k_cat = jnp.concatenate([block_of(k_ref, b) for b in blocks_in], axis=0)
        v_cat = jnp.concatenate([block_of(v_wide, b) for b in blocks_in], axis=0)
        width = k_cat.shape[0]
        query = lax.rem(lax.broadcasted_iota(jnp.int32, (tile, width), 0), tok) + offset
        key = lax.broadcasted_iota(jnp.int32, (tile, width), 1) - (width - half)
        seen = key <= query
        for r in range(0, rows, tile):
            score = lax.dot_general(q_rows[r:r + tile, :], k_cat, NT,
                                    preferred_element_type=jnp.float32)
            score = jnp.where(seen, score, -1e30)
            peak = jnp.max(score, axis=1, keepdims=True)
            weight = jnp.exp2((score - peak) * factor)
            top[r:r + tile, :] = jnp.broadcast_to(peak, (tile, HD))
            acc[r:r + tile, :] = jnp.dot(weight.astype(jnp.bfloat16), v_cat,
                                         preferred_element_type=jnp.float32)

    odd = lax.rem(earlier, 2) == 1

    @pl.when(odd)
    def _():
        first([inv[jnp.maximum(earlier - 1, 0)], own])

    @pl.when(jnp.logical_not(odd))
    def _():
        first([own])

    def step(n, _):
        pair = [inv[2 * n], inv[2 * n + 1]]
        k_cat = jnp.concatenate([block_of(k_ref, b) for b in pair], axis=0)
        v_cat = jnp.concatenate([block_of(v_wide, b) for b in pair], axis=0)
        for r in range(0, rows, tile):
            score = lax.dot_general(q_rows[r:r + tile, :], k_cat, NT,
                                    preferred_element_type=jnp.float32)
            old = top[r:r + tile, :]
            peak = jnp.maximum(old, jnp.max(score, axis=1, keepdims=True))
            top[r:r + tile, :] = peak
            wide = jnp.concatenate([peak] * (2 * half // HD), axis=1)
            weight = jnp.exp2((score - wide) * factor)
            shrink = jnp.exp2((old - peak) * factor)
            acc[r:r + tile, :] = acc[r:r + tile, :] * jnp.concatenate(
                [shrink, shrink], axis=1) + jnp.dot(
                    weight.astype(jnp.bfloat16), v_cat, preferred_element_type=jnp.float32)
        return 0

    lax.fori_loop(0, earlier // 2, step, 0)
    for g in range(group):
        part = acc[g * tok:(g + 1) * tok, :]
        o_ref[:, g * HD:(g + 1) * HD] = (part[:, :HD] / part[:, HD:]).astype(o_ref.dtype)


def attend(queries, k_all, v_all, order, me, chunk, tok, half):
    kv_local = k_all.shape[1] // HD
    width = queries.shape[1] // kv_local
    group = width // HD
    keys = k_all.shape[0]
    rows = group * tok
    tile = min(rows, 256)
    work = rows * keys * kv_local
    return pl.pallas_call(
        functools.partial(attend_kernel, half, tile, chunk),
        out_shape=jax.ShapeDtypeStruct((tok, queries.shape[1]), jnp.bfloat16),
        grid_spec=pltpu.PrefetchScalarGridSpec(
            num_scalar_prefetch=2,
            grid=(kv_local,),
            in_specs=[
                pl.BlockSpec((tok, width), lambda h, *_: (chunk, h)),
                pl.BlockSpec((keys, HD), lambda h, *_: (0, h)),
                pl.BlockSpec((keys, HD), lambda h, *_: (0, h)),
            ],
            out_specs=pl.BlockSpec((tok, width), lambda h, *_: (0, h)),
            scratch_shapes=[
                pltpu.SMEM((order.shape[0],), jnp.int32),
                pltpu.VMEM((rows, HD), jnp.bfloat16),
                pltpu.VMEM((keys, 2 * HD), jnp.bfloat16),
                pltpu.VMEM((rows, 2 * HD), jnp.float32),
                pltpu.VMEM((rows, HD), jnp.float32),
            ],
        ),
        compiler_params=pltpu.CompilerParams(vmem_limit_bytes=40 * 2 ** 20),
        cost_estimate=pl.CostEstimate(
            flops=4 * work * HD, bytes_accessed=4 * keys * HD * kv_local, transcendentals=work),
    )(order, me, queries, k_all, v_all)


def per_device(queries, keys, values, w_out, order):
    tok = queries.shape[0]
    half = tok // 2
    part = tok // 4
    me = (lax.axis_index("blk") * 2).astype(jnp.int32).reshape(1)
    k_all = lax.all_gather(keys, "blk", axis=0, tiled=True)
    v_all = lax.all_gather(values, "blk", axis=0, tiled=True)
    outs = []
    for c in range(tok // part):
        attended = attend(queries, k_all, v_all, order, me, c, part, half)
        share = jnp.dot(attended, w_out, preferred_element_type=jnp.float32).astype(jnp.bfloat16)
        outs.append(lax.psum_scatter(share, "head", scatter_dimension=1, tiled=True))
    return jnp.concatenate(outs, axis=0)


def solution(mesh):
    return jax.shard_map(
        per_device,
        mesh=mesh,
        in_specs=(P("blk", "head"), P("blk", "head"), P("blk", "head"), P("head", None), P()),
        out_specs=P("blk", "head"),
        check_vma=False,
    )
```

```python
import functools
import math

import jax
import jax.numpy as jnp
from jax import lax
from jax.experimental import pallas as pl
from jax.experimental.pallas import tpu as pltpu
from jax.sharding import PartitionSpec as P

HD = 128
NT = (((1,), (1,)), ((), ()))
MIB = 2 ** 20


def attend_kernel(half, tile, chunk, pieces, order_ref, me_ref, q_ref, *refs):
    k_refs, v_refs = refs[:pieces], refs[pieces:2 * pieces]
    o_ref, inv, q_rows, k_all, v_wide, acc, top = refs[2 * pieces:]
    blocks = order_ref.shape[0]
    per = blocks // pieces
    tok = q_ref.shape[0]
    group = q_ref.shape[1] // HD
    rows = group * tok
    shard = per * half
    factor = HD ** (-0.5) * math.log2(math.e)
    start = chunk * tok
    offset = start % half
    own = start // half
    me = me_ref[0]

    def invert(b, _):
        inv[order_ref[b]] = jnp.bitwise_xor(b // per, me) * per + lax.rem(b, per)
        return 0

    lax.fori_loop(0, blocks, invert, 0)
    for g in range(group):
        q_rows[g * tok:(g + 1) * tok, :] = q_ref[:, g * HD:(g + 1) * HD]
    for r in range(pieces):
        k_all[r * shard:(r + 1) * shard, :] = k_refs[r][...]
        v_wide[r * shard:(r + 1) * shard, :HD] = v_refs[r][...]
    v_wide[:, HD:] = jnp.ones((v_wide.shape[0], HD), v_wide.dtype)
    earlier = order_ref[me * per + own]

    def block_of(ref, b):
        return ref[pl.ds(pl.multiple_of(b * half, half), half), :]

    def first(blocks_in):
        k_cat = jnp.concatenate([block_of(k_all, b) for b in blocks_in], axis=0)
        v_cat = jnp.concatenate([block_of(v_wide, b) for b in blocks_in], axis=0)
        width = k_cat.shape[0]
        query = lax.rem(lax.broadcasted_iota(jnp.int32, (tile, width), 0), tok) + offset
        key = lax.broadcasted_iota(jnp.int32, (tile, width), 1) - (width - half)
        seen = key <= query
        for r in range(0, rows, tile):
            score = lax.dot_general(q_rows[r:r + tile, :], k_cat, NT,
                                    preferred_element_type=jnp.float32)
            score = jnp.where(seen, score, -1e30)
            peak = jnp.max(score, axis=1, keepdims=True)
            weight = jnp.exp2((score - peak) * factor)
            top[r:r + tile, :] = jnp.broadcast_to(peak, (tile, HD))
            acc[r:r + tile, :] = jnp.dot(weight.astype(jnp.bfloat16), v_cat,
                                         preferred_element_type=jnp.float32)

    odd = lax.rem(earlier, 2) == 1

    @pl.when(odd)
    def _():
        first([inv[jnp.maximum(earlier - 1, 0)], own])

    @pl.when(jnp.logical_not(odd))
    def _():
        first([own])

    def step(n, _):
        pair = [inv[2 * n], inv[2 * n + 1]]
        k_cat = jnp.concatenate([block_of(k_all, b) for b in pair], axis=0)
        v_cat = jnp.concatenate([block_of(v_wide, b) for b in pair], axis=0)
        for r in range(0, rows, tile):
            score = lax.dot_general(q_rows[r:r + tile, :], k_cat, NT,
                                    preferred_element_type=jnp.float32)
            old = top[r:r + tile, :]
            peak = jnp.maximum(old, jnp.max(score, axis=1, keepdims=True))
            top[r:r + tile, :] = peak
            wide = jnp.concatenate([peak] * (2 * half // HD), axis=1)
            weight = jnp.exp2((score - wide) * factor)
            shrink = jnp.exp2((old - peak) * factor)
            acc[r:r + tile, :] = acc[r:r + tile, :] * jnp.concatenate(
                [shrink, shrink], axis=1) + jnp.dot(
                    weight.astype(jnp.bfloat16), v_cat, preferred_element_type=jnp.float32)
        return 0

    lax.fori_loop(0, earlier // 2, step, 0)
    for g in range(group):
        part = acc[g * tok:(g + 1) * tok, :]
        o_ref[:, g * HD:(g + 1) * HD] = (part[:, :HD] / part[:, HD:]).astype(o_ref.dtype)


def attend(queries, k_pieces, v_pieces, order, me, chunk, tok, half):
    pieces = len(k_pieces)
    shard, kv_width = k_pieces[0].shape
    kv_local = kv_width // HD
    width = queries.shape[1] // kv_local
    keys = shard * pieces
    rows = width // HD * tok
    tile = min(rows, 256)
    work = rows * keys * kv_local
    piece_spec = pl.BlockSpec((shard, HD), lambda h, *_: (0, h))
    return pl.pallas_call(
        functools.partial(attend_kernel, half, tile, chunk, pieces),
        out_shape=jax.ShapeDtypeStruct((tok, queries.shape[1]), jnp.bfloat16),
        grid_spec=pltpu.PrefetchScalarGridSpec(
            num_scalar_prefetch=2,
            grid=(kv_local,),
            in_specs=[pl.BlockSpec((tok, width), lambda h, *_: (chunk, h))]
            + [piece_spec] * (2 * pieces),
            out_specs=pl.BlockSpec((tok, width), lambda h, *_: (0, h)),
            scratch_shapes=[
                pltpu.SMEM((order.shape[0],), jnp.int32),
                pltpu.VMEM((rows, HD), jnp.bfloat16),
                pltpu.VMEM((keys, HD), jnp.bfloat16),
                pltpu.VMEM((keys, 2 * HD), jnp.bfloat16),
                pltpu.VMEM((rows, 2 * HD), jnp.float32),
                pltpu.VMEM((rows, HD), jnp.float32),
            ],
        ),
        compiler_params=pltpu.CompilerParams(vmem_limit_bytes=40 * MIB),
        cost_estimate=pl.CostEstimate(
            flops=4 * work * HD, bytes_accessed=4 * keys * HD * kv_local, transcendentals=work),
        name="attend",
    )(order, me, queries, *k_pieces, *v_pieces)


def exchange(arrays, axis, bits):
    count = lax.axis_size(axis)
    held = {0: arrays}
    for bit in bits:
        pairs = [(i, i ^ (1 << bit)) for i in range(count)]
        held.update({r ^ (1 << bit): lax.ppermute(a, axis, pairs) for r, a in held.items()})
    return [held[r] for r in range(count)]


def share_kernel(extra, meta_ref, a_ref, w_ref, *refs):
    went, sums = refs[:extra], refs[extra:]
    way = pl.program_id(0)
    for side in range(2):
        @pl.when(jnp.logical_and(way == side, meta_ref[2 * side + 1] == 1))
        def _():
            total = jnp.dot(a_ref[...], w_ref[...], preferred_element_type=jnp.float32)
            if extra:
                total = total + went[side][...].astype(jnp.float32)
            sums[side][...] = total.astype(jnp.bfloat16)


def shares(attended, w_out, arrived, meta, columns):
    tok, depth = attended.shape
    wide = min(columns, 512)
    tiles = columns // wide

    def w_index(way, j, meta):
        up, has_up, down, has_down = meta[0], meta[1], meta[2], meta[3]
        first = jnp.where(has_up == 1, up * tiles + j, jnp.where(has_down == 1, down * tiles, 0))
        second = jnp.where(has_down == 1, down * tiles + j,
                           jnp.where(has_up == 1, up * tiles + tiles - 1, 0))
        return (0, jnp.where(way == 0, first, second))

    up_spec = pl.BlockSpec((tok, wide), lambda way, j, meta: (0, jnp.where(way == 0, j, tiles - 1)))
    down_spec = pl.BlockSpec((tok, wide), lambda way, j, meta: (0, jnp.where(way == 0, 0, j)))
    extra = len(arrived)
    return pl.pallas_call(
        functools.partial(share_kernel, extra),
        out_shape=[jax.ShapeDtypeStruct((tok, columns), jnp.bfloat16)] * 2,
        grid_spec=pltpu.PrefetchScalarGridSpec(
            num_scalar_prefetch=1,
            grid=(2, tiles),
            in_specs=[
                pl.BlockSpec((tok, depth), lambda way, j, meta: (0, 0)),
                pl.BlockSpec((depth, wide), w_index),
            ] + [up_spec, down_spec][:extra],
            out_specs=[up_spec, down_spec],
        ),
        compiler_params=pltpu.CompilerParams(vmem_limit_bytes=24 * MIB),
        cost_estimate=pl.CostEstimate(
            flops=2 * tok * depth * columns, bytes_accessed=2 * depth * columns, transcendentals=0),
        name="shares",
    )(meta, attended, w_out, *arrived)


def finish_kernel(extra, here_ref, a_ref, w_ref, *refs):
    total = jnp.dot(a_ref[...], w_ref[...], preferred_element_type=jnp.float32)
    for ref in refs[:extra]:
        total = total + ref[...].astype(jnp.float32)
    refs[-1][...] = total.astype(jnp.bfloat16)


def finish(attended, w_out, arrived, here, columns, chunk, whole_tok, out):
    tok, depth = attended.shape
    wide = min(columns, 512)
    tiles = columns // wide
    extra = len(arrived)
    operands = [attended, w_out, *arrived]
    specs = [
        pl.BlockSpec((tok, depth), lambda j, here: (0, 0)),
        pl.BlockSpec((depth, wide), lambda j, here: (0, here[0] * tiles + j)),
    ] + [pl.BlockSpec((tok, wide), lambda j, here: (0, j))] * extra
    aliases = {}
    if out is not None:
        operands.append(out)
        specs.append(pl.BlockSpec(memory_space=pl.ANY))
        aliases = {len(operands): 0}
    return pl.pallas_call(
        functools.partial(finish_kernel, extra),
        out_shape=jax.ShapeDtypeStruct((whole_tok, columns), jnp.bfloat16),
        grid_spec=pltpu.PrefetchScalarGridSpec(
            num_scalar_prefetch=1,
            grid=(tiles,),
            in_specs=specs,
            out_specs=pl.BlockSpec((tok, wide), lambda j, here: (chunk, j)),
        ),
        input_output_aliases=aliases,
        compiler_params=pltpu.CompilerParams(vmem_limit_bytes=24 * MIB),
        cost_estimate=pl.CostEstimate(
            flops=2 * tok * depth * columns, bytes_accessed=2 * depth * columns, transcendentals=0),
        name="finish",
    )(here, *operands)


def per_device(queries, keys, values, w_out, order):
    tok = queries.shape[0]
    half = tok // 2
    part = tok // 4
    line = lax.axis_size("head")
    columns = w_out.shape[1] // line
    me = lax.axis_index("blk").astype(jnp.int32).reshape(1)
    z = lax.axis_index("head").astype(jnp.int32)
    bits = list(range(1, lax.axis_size("blk").bit_length() - 1))
    k_pieces = exchange(keys, "blk", bits + [0])
    v_pieces = exchange(values, "blk", bits[::-1] + [0])
    metas = [
        jnp.stack([
            jnp.where(z < s, line - s + z, 0), (z < s).astype(jnp.int32),
            jnp.where(z >= line - s, z + s - line, 0), (z >= line - s).astype(jnp.int32),
        ]).astype(jnp.int32)
        for s in range(1, line)
    ]
    out = None
    for c in range(tok // part):
        attended = attend(queries, k_pieces, v_pieces, order, me, c, part, half)
        arrived = []
        for s in range(1, line):
            up, down = shares(attended, w_out, arrived, metas[s - 1], columns)
            arrived = [
                lax.ppermute(up, "head", [(i, i + 1) for i in range(s)]),
                lax.ppermute(down, "head", [(i, i - 1) for i in range(line - s, line)]),
            ]
        out = finish(attended, w_out, arrived, z.reshape(1), columns, c, tok, out)
    return out


def solution(mesh):
    return jax.shard_map(
        per_device,
        mesh=mesh,
        in_specs=(P("blk", "head"), P("blk", "head"), P("blk", "head"), P("head", None), P()),
        out_specs=P("blk", "head"),
        check_vma=False,
    )
```

```python
import functools
import math

import jax
import jax.numpy as jnp
from jax import lax
from jax.experimental import pallas as pl
from jax.experimental.pallas import tpu as pltpu
from jax.sharding import PartitionSpec as P

HD = 128
NT = (((1,), (1,)), ((), ()))
MIB = 2 ** 20


def attend_kernel(half, tile, chunk, pieces, order_ref, me_ref, q_ref, *refs):
    k_refs, v_refs = refs[:pieces], refs[pieces:2 * pieces]
    o_ref, inv, q_rows, k_all, v_wide, acc, top = refs[2 * pieces:]
    blocks = order_ref.shape[0]
    per = blocks // pieces
    tok = q_ref.shape[0]
    group = q_ref.shape[1] // HD
    rows = group * tok
    shard = per * half
    factor = HD ** (-0.5) * math.log2(math.e)
    start = chunk * tok
    offset = start % half
    own = start // half
    me = me_ref[0]

    def invert(b, _):
        inv[order_ref[b]] = jnp.bitwise_xor(b // per, me) * per + lax.rem(b, per)
        return 0

    lax.fori_loop(0, blocks, invert, 0)
    for g in range(group):
        q_rows[g * tok:(g + 1) * tok, :] = q_ref[:, g * HD:(g + 1) * HD]
    for r in range(pieces):
        k_all[r * shard:(r + 1) * shard, :] = k_refs[r][...]
        v_wide[r * shard:(r + 1) * shard, :HD] = v_refs[r][...]
    v_wide[:, HD:] = jnp.ones((v_wide.shape[0], HD), v_wide.dtype)
    earlier = order_ref[me * per + own]

    def block_of(ref, b):
        return ref[pl.ds(pl.multiple_of(b * half, half), half), :]

    def first(blocks_in):
        k_cat = jnp.concatenate([block_of(k_all, b) for b in blocks_in], axis=0)
        v_cat = jnp.concatenate([block_of(v_wide, b) for b in blocks_in], axis=0)
        width = k_cat.shape[0]
        query = lax.rem(lax.broadcasted_iota(jnp.int32, (tile, width), 0), tok) + offset
        key = lax.broadcasted_iota(jnp.int32, (tile, width), 1) - (width - half)
        seen = key <= query
        for r in range(0, rows, tile):
            score = lax.dot_general(q_rows[r:r + tile, :], k_cat, NT,
                                    preferred_element_type=jnp.float32)
            score = jnp.where(seen, score, -1e30)
            peak = jnp.max(score, axis=1, keepdims=True)
            weight = jnp.exp2((score - peak) * factor)
            top[r:r + tile, :] = jnp.broadcast_to(peak, (tile, HD))
            acc[r:r + tile, :] = jnp.dot(weight.astype(jnp.bfloat16), v_cat,
                                         preferred_element_type=jnp.float32)

    odd = lax.rem(earlier, 2) == 1

    @pl.when(odd)
    def _():
        first([inv[jnp.maximum(earlier - 1, 0)], own])

    @pl.when(jnp.logical_not(odd))
    def _():
        first([own])

    def step(n, _):
        pair = [inv[2 * n], inv[2 * n + 1]]
        k_cat = jnp.concatenate([block_of(k_all, b) for b in pair], axis=0)
        v_cat = jnp.concatenate([block_of(v_wide, b) for b in pair], axis=0)
        for r in range(0, rows, tile):
            score = lax.dot_general(q_rows[r:r + tile, :], k_cat, NT,
                                    preferred_element_type=jnp.float32)
            old = top[r:r + tile, :]
            peak = jnp.maximum(old, jnp.max(score, axis=1, keepdims=True))
            top[r:r + tile, :] = peak
            wide = jnp.concatenate([peak] * (2 * half // HD), axis=1)
            weight = jnp.exp2((score - wide) * factor)
            shrink = jnp.exp2((old - peak) * factor)
            acc[r:r + tile, :] = acc[r:r + tile, :] * jnp.concatenate(
                [shrink, shrink], axis=1) + jnp.dot(
                    weight.astype(jnp.bfloat16), v_cat, preferred_element_type=jnp.float32)
        return 0

    lax.fori_loop(0, earlier // 2, step, 0)
    for g in range(group):
        part = acc[g * tok:(g + 1) * tok, :]
        o_ref[:, g * HD:(g + 1) * HD] = (part[:, :HD] / part[:, HD:]).astype(o_ref.dtype)


def attend(queries, k_pieces, v_pieces, order, me, chunk, tok, half):
    pieces = len(k_pieces)
    shard, kv_width = k_pieces[0].shape
    kv_local = kv_width // HD
    width = queries.shape[1] // kv_local
    keys = shard * pieces
    rows = width // HD * tok
    tile = min(rows, 256)
    work = rows * keys * kv_local
    piece_spec = pl.BlockSpec((shard, HD), lambda h, *_: (0, h))
    return pl.pallas_call(
        functools.partial(attend_kernel, half, tile, chunk, pieces),
        out_shape=jax.ShapeDtypeStruct((tok, queries.shape[1]), jnp.bfloat16),
        grid_spec=pltpu.PrefetchScalarGridSpec(
            num_scalar_prefetch=2,
            grid=(kv_local,),
            in_specs=[pl.BlockSpec((tok, width), lambda h, *_: (chunk, h))]
            + [piece_spec] * (2 * pieces),
            out_specs=pl.BlockSpec((tok, width), lambda h, *_: (0, h)),
            scratch_shapes=[
                pltpu.SMEM((order.shape[0],), jnp.int32),
                pltpu.VMEM((rows, HD), jnp.bfloat16),
                pltpu.VMEM((keys, HD), jnp.bfloat16),
                pltpu.VMEM((keys, 2 * HD), jnp.bfloat16),
                pltpu.VMEM((rows, 2 * HD), jnp.float32),
                pltpu.VMEM((rows, HD), jnp.float32),
            ],
        ),
        compiler_params=pltpu.CompilerParams(vmem_limit_bytes=40 * MIB),
        cost_estimate=pl.CostEstimate(
            flops=4 * work * HD, bytes_accessed=4 * keys * HD * kv_local, transcendentals=work),
        name="attend",
    )(order, me, queries, *k_pieces, *v_pieces)


def exchange(arrays, axis, bits):
    count = lax.axis_size(axis)
    held = {0: arrays}
    for bit in bits:
        pairs = [(i, i ^ (1 << bit)) for i in range(count)]
        held.update({r ^ (1 << bit): lax.ppermute(a, axis, pairs) for r, a in held.items()})
    return [held[r] for r in range(count)]


def pick(z, options):
    value = jnp.int32(options[-1])
    for i in range(len(options) - 1):
        value = jnp.where(z == i, jnp.int32(options[i]), value)
    return value


def share_kernel(extra, blocks, z_ref, a_ref, w_ref, *refs):
    @pl.when(pick(z_ref[0], blocks) >= 0)
    def _():
        total = jnp.dot(a_ref[...], w_ref[...], preferred_element_type=jnp.float32)
        for ref in refs[:extra]:
            total = total + ref[...].astype(jnp.float32)
        refs[-1][...] = total.astype(jnp.bfloat16)


def share(attended, w_out, arrived, z, blocks, columns, chunk=0, whole_tok=None, out=None):
    tok, depth = attended.shape
    wide = min(columns, 512)
    tiles = columns // wide
    extra = len(arrived)

    def at(j, z_ref):
        block = pick(z_ref[0], blocks)
        return jnp.maximum(block, 0) * tiles + jnp.where(block >= 0, j, 0)

    def inside(j, z_ref):
        return jnp.where(pick(z_ref[0], blocks) >= 0, j, 0)

    operands = [attended, w_out, *arrived]
    specs = [
        pl.BlockSpec((tok, depth), lambda j, z_ref: (0, 0)),
        pl.BlockSpec((depth, wide), lambda j, z_ref: (0, at(j, z_ref))),
    ] + [pl.BlockSpec((tok, wide), lambda j, z_ref: (0, inside(j, z_ref)))] * extra
    aliases = {}
    if out is not None:
        operands.append(out)
        specs.append(pl.BlockSpec(memory_space=pl.ANY))
        aliases = {len(operands): 0}
    return pl.pallas_call(
        functools.partial(share_kernel, extra, blocks),
        out_shape=jax.ShapeDtypeStruct((whole_tok or tok, columns), jnp.bfloat16),
        grid_spec=pltpu.PrefetchScalarGridSpec(
            num_scalar_prefetch=1,
            grid=(tiles,),
            in_specs=specs,
            out_specs=pl.BlockSpec((tok, wide), lambda j, z_ref: (chunk, inside(j, z_ref))),
        ),
        input_output_aliases=aliases,
        compiler_params=pltpu.CompilerParams(vmem_limit_bytes=40 * MIB),
        cost_estimate=pl.CostEstimate(
            flops=2 * tok * depth * columns // 8, bytes_accessed=0, transcendentals=0),
        name="share",
    )(z, *operands)


def swap(array, pairs):
    return lax.ppermute(array, "head", pairs)


def line_of_four(parts, w_out, z, columns, tok):
    outer, inner = [(0, 1), (3, 2)], [(1, 2), (2, 1)]
    both = outer + [(1, 0), (2, 3)]
    out = None
    for c, a in enumerate(parts):
        far = swap(share(a, w_out, [], z, (3, -1, -1, 0), columns), outer)
        near = swap(share(a, w_out, [], z, (2, -1, -1, 1), columns), outer)
        far = swap(share(a, w_out, [far], z, (-1, 3, 0, -1), columns), inner)
        near = swap(share(a, w_out, [near], z, (-1, 2, 1, -1), columns), inner)
        last = swap(share(a, w_out, [far], z, (1, 0, 3, 2), columns), both)
        out = share(a, w_out, [near, last], z, (0, 1, 2, 3), columns, c, tok, out)
    return out


def per_device(queries, keys, values, w_out, order):
    tok = queries.shape[0]
    half = tok // 2
    line = lax.axis_size("head")
    columns = w_out.shape[1] // line
    me = lax.axis_index("blk").astype(jnp.int32).reshape(1)
    z = lax.axis_index("head").astype(jnp.int32).reshape(1)
    bits = list(range(1, lax.axis_size("blk").bit_length() - 1))
    k_pieces = exchange(keys, "blk", bits + [0])
    v_pieces = exchange(values, "blk", bits[::-1] + [0])
    parts = [attend(queries, k_pieces, v_pieces, order, me, c, half, half) for c in range(2)]
    if line == 4:
        return line_of_four(parts, w_out, z, columns, tok)
    outs = []
    for a in parts:
        sums = jnp.dot(a, w_out, preferred_element_type=jnp.float32).astype(jnp.bfloat16)
        outs.append(lax.psum_scatter(sums, "head", scatter_dimension=1, tiled=True))
    return jnp.concatenate(outs, axis=0)


def solution(mesh):
    return jax.shard_map(
        per_device,
        mesh=mesh,
        in_specs=(P("blk", "head"), P("blk", "head"), P("blk", "head"), P("head", None), P()),
        out_specs=P("blk", "head"),
        check_vma=False,
    )
```

```python
import functools
import math

import jax
import jax.numpy as jnp
from jax import lax
from jax.experimental import pallas as pl
from jax.experimental.pallas import tpu as pltpu
from jax.sharding import PartitionSpec as P

HD = 128
NT = (((1,), (1,)), ((), ()))
MIB = 2 ** 20
STREAMS = 4


def in_hbm(array):
    return pltpu.with_memory_space_constraint(array, pltpu.HBM)


def block_place(chunk, order_ref, me_ref):
    own = 2 * me_ref[0]
    return jnp.where(order_ref[own] > order_ref[own + 1], 1 - chunk, chunk)


def attend_kernel(half, tile, chunk, pieces, order_ref, me_ref, q_ref, *refs):
    k_refs, v_refs = refs[:pieces], refs[pieces:2 * pieces]
    o_ref, inv, q_rows, k_all, v_wide, acc, top = refs[2 * pieces:]
    blocks = order_ref.shape[0]
    per = blocks // pieces
    tok = q_ref.shape[0]
    group = q_ref.shape[1] // HD
    rows = group * tok
    shard = per * half
    factor = HD ** (-0.5) * math.log2(math.e)
    own = block_place(chunk, order_ref, me_ref)
    me = me_ref[0]

    def invert(b, _):
        inv[order_ref[b]] = jnp.bitwise_xor(b // per, me) * per + lax.rem(b, per)
        return 0

    lax.fori_loop(0, blocks, invert, 0)
    for g in range(group):
        q_rows[g * tok:(g + 1) * tok, :] = q_ref[:, g * HD:(g + 1) * HD]
    for r in range(pieces):
        k_all[r * shard:(r + 1) * shard, :] = k_refs[r][...]
        v_wide[r * shard:(r + 1) * shard, :HD] = v_refs[r][...]
    v_wide[:, HD:] = jnp.ones((v_wide.shape[0], HD), v_wide.dtype)
    earlier = order_ref[me * per + own]

    def block_of(ref, b):
        return ref[pl.ds(pl.multiple_of(b * half, half), half), :]

    def first(blocks_in):
        k_cat = jnp.concatenate([block_of(k_all, b) for b in blocks_in], axis=0)
        v_cat = jnp.concatenate([block_of(v_wide, b) for b in blocks_in], axis=0)
        width = k_cat.shape[0]
        query = lax.rem(lax.broadcasted_iota(jnp.int32, (tile, width), 0), tok)
        key = lax.broadcasted_iota(jnp.int32, (tile, width), 1) - (width - half)
        seen = key <= query
        for r in range(0, rows, tile):
            score = lax.dot_general(q_rows[r:r + tile, :], k_cat, NT,
                                    preferred_element_type=jnp.float32)
            score = jnp.where(seen, score, -1e30)
            peak = jnp.max(score, axis=1, keepdims=True)
            weight = jnp.exp2((score - peak) * factor)
            top[r:r + tile, :] = jnp.broadcast_to(peak, (tile, HD))
            acc[r:r + tile, :] = jnp.dot(weight.astype(jnp.bfloat16), v_cat,
                                         preferred_element_type=jnp.float32)

    odd = lax.rem(earlier, 2) == 1

    @pl.when(odd)
    def _():
        first([inv[jnp.maximum(earlier - 1, 0)], own])

    @pl.when(jnp.logical_not(odd))
    def _():
        first([own])

    def step(n, _):
        pair = [inv[2 * n], inv[2 * n + 1]]
        k_cat = jnp.concatenate([block_of(k_all, b) for b in pair], axis=0)
        v_cat = jnp.concatenate([block_of(v_wide, b) for b in pair], axis=0)
        for r in range(0, rows, tile):
            score = lax.dot_general(q_rows[r:r + tile, :], k_cat, NT,
                                    preferred_element_type=jnp.float32)
            old = top[r:r + tile, :]
            peak = jnp.maximum(old, jnp.max(score, axis=1, keepdims=True))
            top[r:r + tile, :] = peak
            wide = jnp.concatenate([peak] * (2 * half // HD), axis=1)
            weight = jnp.exp2((score - wide) * factor)
            shrink = jnp.exp2((old - peak) * factor)
            acc[r:r + tile, :] = acc[r:r + tile, :] * jnp.concatenate(
                [shrink, shrink], axis=1) + jnp.dot(
                    weight.astype(jnp.bfloat16), v_cat, preferred_element_type=jnp.float32)
        return 0

    lax.fori_loop(0, earlier // 2, step, 0)
    for g in range(group):
        part = acc[g * tok:(g + 1) * tok, :]
        o_ref[:, g * HD:(g + 1) * HD] = (part[:, :HD] / part[:, HD:]).astype(o_ref.dtype)


def attend(queries, k_pieces, v_pieces, order, me, chunk, half):
    tok = half
    pieces = len(k_pieces)
    shard, kv_width = k_pieces[0].shape
    kv_local = kv_width // HD
    width = queries.shape[1] // kv_local
    keys = shard * pieces
    rows = width // HD * tok
    tile = min(rows, 256)
    work = rows * keys * kv_local
    piece_spec = pl.BlockSpec((shard, HD), lambda h, *_: (0, h))
    return pl.pallas_call(
        functools.partial(attend_kernel, half, tile, chunk, pieces),
        out_shape=jax.ShapeDtypeStruct((tok, queries.shape[1]), jnp.bfloat16),
        grid_spec=pltpu.PrefetchScalarGridSpec(
            num_scalar_prefetch=2,
            grid=(kv_local,),
            in_specs=[pl.BlockSpec((tok, width), lambda h, *refs: (block_place(chunk, *refs), h))]
            + [piece_spec] * (2 * pieces),
            out_specs=pl.BlockSpec((tok, width), lambda h, *_: (0, h)),
            scratch_shapes=[
                pltpu.SMEM((order.shape[0],), jnp.int32),
                pltpu.VMEM((rows, HD), jnp.bfloat16),
                pltpu.VMEM((keys, HD), jnp.bfloat16),
                pltpu.VMEM((keys, 2 * HD), jnp.bfloat16),
                pltpu.VMEM((rows, 2 * HD), jnp.float32),
                pltpu.VMEM((rows, HD), jnp.float32),
            ],
        ),
        compiler_params=pltpu.CompilerParams(vmem_limit_bytes=40 * MIB),
        cost_estimate=pl.CostEstimate(
            flops=4 * work * HD, bytes_accessed=4 * keys * HD * kv_local, transcendentals=work),
        name="attend",
    )(order, me, in_hbm(queries), in_hbm(k_pieces[0]), *k_pieces[1:], in_hbm(v_pieces[0]), *v_pieces[1:])


def exchange(arrays, axis, bits):
    count = lax.axis_size(axis)
    held = {0: arrays}
    for bit in bits:
        pairs = [(i, i ^ (1 << bit)) for i in range(count)]
        held.update({r ^ (1 << bit): lax.ppermute(a, axis, pairs) for r, a in held.items()})
    return [held[r] for r in range(count)]


def pick(z, options):
    value = jnp.int32(options[-1])
    for i in range(len(options) - 1):
        value = jnp.where(z == i, jnp.int32(options[i]), value)
    return value


def share_kernel(extra, blocks, z_ref, order_ref, me_ref, a_ref, *refs):
    w_refs, arrived, out = refs[:STREAMS], refs[STREAMS:STREAMS + extra], refs[-1]

    @pl.when(pick(z_ref[0], blocks) >= 0)
    def _():
        w = jnp.concatenate([ref[...] for ref in w_refs], axis=0)
        total = jnp.dot(a_ref[...], w, preferred_element_type=jnp.float32)
        for ref in arrived:
            total = total + ref[...].astype(jnp.float32)
        out[...] = total.astype(jnp.bfloat16)


def share(attended, w_out, arrived, place, blocks, columns, chunk=None, whole_tok=None, out=None):
    tok, depth = attended.shape
    wide = min(columns, 512)
    tiles = columns // wide
    extra = len(arrived)

    def at(j, z_ref):
        block = pick(z_ref[0], blocks)
        return jnp.maximum(block, 0) * tiles + jnp.where(block >= 0, j, 0)

    def inside(j, z_ref):
        return jnp.where(pick(z_ref[0], blocks) >= 0, j, 0)

    def target(j, z_ref, order_ref, me_ref):
        row = 0 if chunk is None else block_place(chunk, order_ref, me_ref)
        return (row, inside(j, z_ref))

    def stream(i):
        return pl.BlockSpec((depth // STREAMS, wide), lambda j, z_ref, *_: (i, at(j, z_ref)))

    operands = [attended] + [in_hbm(w_out)] * STREAMS + arrived
    specs = [pl.BlockSpec((tok, depth), lambda j, *_: (0, 0))]
    specs += [stream(i) for i in range(STREAMS)]
    specs += [pl.BlockSpec((tok, wide), lambda j, z_ref, *_: (0, inside(j, z_ref)))] * extra
    aliases = {}
    if out is not None:
        operands.append(out)
        specs.append(pl.BlockSpec(memory_space=pl.ANY))
        aliases = {2 + len(operands): 0}
    return pl.pallas_call(
        functools.partial(share_kernel, extra, blocks),
        out_shape=jax.ShapeDtypeStruct((whole_tok or tok, columns), jnp.bfloat16),
        grid_spec=pltpu.PrefetchScalarGridSpec(
            num_scalar_prefetch=3,
            grid=(tiles,),
            in_specs=specs,
            out_specs=pl.BlockSpec((tok, wide), target),
        ),
        input_output_aliases=aliases,
        compiler_params=pltpu.CompilerParams(vmem_limit_bytes=40 * MIB),
        cost_estimate=pl.CostEstimate(
            flops=2 * tok * depth * columns // 8, bytes_accessed=0, transcendentals=0),
        name="share",
    )(*place, *operands)


def swap(array, pairs):
    return lax.ppermute(array, "head", pairs)


def line_of_four(parts, w_out, place, columns, tok):
    outer, inner, back = [(0, 1), (3, 2)], [(1, 2), (2, 1)], [(1, 0), (2, 3)]
    far, near, last, home = [], [], [], []
    for a in parts:
        far.append(swap(share(a, w_out, [], place, (3, -1, -1, 0), columns), outer))
        near.append(swap(share(a, w_out, [], place, (2, -1, -1, 1), columns), outer))
    for a in parts:
        last.append(swap(share(a, w_out, [], place, (1, -1, -1, 2), columns), outer))
    for c, a in enumerate(parts):
        far[c] = swap(share(a, w_out, [far[c]], place, (-1, 3, 0, -1), columns), inner)
        near[c] = swap(share(a, w_out, [near[c]], place, (-1, 2, 1, -1), columns), inner)
        home.append(swap(share(a, w_out, [far[c]], place, (-1, 0, 3, -1), columns), back))
    out = None
    for c, a in enumerate(parts):
        out = share(a, w_out, [near[c], last[c], home[c]], place, (0, 1, 2, 3), columns, c, tok, out)
    return out


def per_device(queries, keys, values, w_out, order):
    tok = queries.shape[0]
    half = tok // 2
    line = lax.axis_size("head")
    columns = w_out.shape[1] // line
    me = lax.axis_index("blk").astype(jnp.int32).reshape(1)
    z = lax.axis_index("head").astype(jnp.int32).reshape(1)
    bits = list(range(1, lax.axis_size("blk").bit_length() - 1))
    k_pieces = exchange(keys, "blk", bits + [0])
    v_pieces = exchange(values, "blk", bits[::-1] + [0])
    parts = [attend(queries, k_pieces, v_pieces, order, me, c, half) for c in range(2)]
    if line == 4:
        return line_of_four(parts, w_out, (z, order, me), columns, tok)
    outs = []
    for a in parts:
        sums = jnp.dot(a, w_out, preferred_element_type=jnp.float32).astype(jnp.bfloat16)
        outs.append(lax.psum_scatter(sums, "head", scatter_dimension=1, tiled=True))
    swapped = block_place(0, order, me) == 1
    outs = [jnp.where(swapped, outs[1 - c], outs[c]) for c in range(2)]
    return jnp.concatenate(outs, axis=0)


def solution(mesh):
    return jax.shard_map(
        per_device,
        mesh=mesh,
        in_specs=(P("blk", "head"), P("blk", "head"), P("blk", "head"), P("head", None), P()),
        out_specs=P("blk", "head"),
        check_vma=False,
    )
```

```python
import functools
import math

import jax
import jax.numpy as jnp
from jax import lax
from jax.experimental import pallas as pl
from jax.experimental.pallas import tpu as pltpu
from jax.sharding import PartitionSpec as P

HD = 128
NT = (((1,), (1,)), ((), ()))
MIB = 2 ** 20
STEP = 4


def in_hbm(array):
    return pltpu.with_memory_space_constraint(array, pltpu.HBM)


def block_place(chunk, order_ref, me_ref):
    own = 2 * me_ref[0]
    return jnp.where(order_ref[own] > order_ref[own + 1], 1 - chunk, chunk)


def attend_kernel(half, tile, chunk, pieces, waited, order_ref, me_ref, q_ref, *refs):
    k_refs, v_refs = refs[:pieces], refs[pieces:2 * pieces]
    o_ref, inv, q_rows, k_all, v_wide, acc, top = refs[2 * pieces + waited:]
    blocks = order_ref.shape[0]
    per = blocks // pieces
    tok = q_ref.shape[0]
    group = q_ref.shape[1] // HD
    rows = group * tok
    shard = per * half
    factor = HD ** (-0.5) * math.log2(math.e)
    own = block_place(chunk, order_ref, me_ref)
    me = me_ref[0]

    def invert(b, _):
        inv[order_ref[b]] = jnp.bitwise_xor(b // per, me) * per + lax.rem(b, per)
        return 0

    lax.fori_loop(0, blocks, invert, 0)
    for g in range(group):
        q_rows[g * tok:(g + 1) * tok, :] = q_ref[:, g * HD:(g + 1) * HD]
    for r in range(pieces):
        k_all[r * shard:(r + 1) * shard, :] = k_refs[r][...]
        v_wide[r * shard:(r + 1) * shard, :HD] = v_refs[r][...]
    v_wide[:, HD:] = jnp.ones((v_wide.shape[0], HD), v_wide.dtype)
    earlier = order_ref[me * per + own]

    def block_of(ref, b):
        return ref[pl.ds(pl.multiple_of(b * half, half), half), :]

    def first(blocks_in):
        k_cat = jnp.concatenate([block_of(k_all, b) for b in blocks_in], axis=0)
        v_cat = jnp.concatenate([block_of(v_wide, b) for b in blocks_in], axis=0)
        width = k_cat.shape[0]
        query = lax.rem(lax.broadcasted_iota(jnp.int32, (tile, width), 0), tok)
        key = lax.broadcasted_iota(jnp.int32, (tile, width), 1) - (width - half)
        seen = key <= query
        for r in range(0, rows, tile):
            score = lax.dot_general(q_rows[r:r + tile, :], k_cat, NT,
                                    preferred_element_type=jnp.float32)
            score = jnp.where(seen, score, -1e30)
            peak = jnp.max(score, axis=1, keepdims=True)
            weight = jnp.exp2((score - peak) * factor)
            top[r:r + tile, :] = jnp.broadcast_to(peak, (tile, HD))
            acc[r:r + tile, :] = jnp.dot(weight.astype(jnp.bfloat16), v_cat,
                                         preferred_element_type=jnp.float32)

    def keys_of(blocks_in):
        return (jnp.concatenate([block_of(k_all, b) for b in blocks_in], axis=0),
                jnp.concatenate([block_of(v_wide, b) for b in blocks_in], axis=0))

    def over_tiles(k_cat, use):
        def scores(r):
            return lax.dot_general(q_rows[r:r + tile, :], k_cat, NT,
                                   preferred_element_type=jnp.float32)

        score = scores(0)
        for r in range(0, rows, tile):
            ahead = scores(r + tile) if r + tile < rows else None
            use(r, score)
            score = ahead

    def first(rest):
        k_cat, v_cat = keys_of([inv[earlier - rest + i] for i in range(rest)] + [own])
        query = lax.rem(lax.broadcasted_iota(jnp.int32, (tile, half), 0), tok)
        seen = lax.broadcasted_iota(jnp.int32, (tile, half), 1) <= query

        def use(r, score):
            masked = jnp.where(seen, score[:, rest * half:], -1e30)
            score = jnp.concatenate([score[:, :rest * half], masked], axis=1) if rest else masked
            peak = jnp.max(score, axis=1, keepdims=True)
            weight = jnp.exp2((score - peak) * factor)
            top[r:r + tile, :] = jnp.broadcast_to(peak, (tile, HD))
            acc[r:r + tile, :] = jnp.dot(weight.astype(jnp.bfloat16), v_cat,
                                         preferred_element_type=jnp.float32)

        over_tiles(k_cat, use)

    for rest in range(STEP):
        pl.when(lax.rem(earlier, STEP) == rest)(functools.partial(first, rest))

    def step(n, _):
        k_cat, v_cat = keys_of([inv[STEP * n + i] for i in range(STEP)])

        def use(r, score):
            old = top[r:r + tile, :]
            peak = jnp.maximum(old, jnp.max(score, axis=1, keepdims=True))
            top[r:r + tile, :] = peak
            wide = jnp.concatenate([peak] * (STEP * half // HD), axis=1)
            weight = jnp.exp2((score - wide) * factor)
            shrink = jnp.exp2((old - peak) * factor)
            acc[r:r + tile, :] = acc[r:r + tile, :] * jnp.concatenate(
                [shrink, shrink], axis=1) + jnp.dot(
                    weight.astype(jnp.bfloat16), v_cat, preferred_element_type=jnp.float32)

        over_tiles(k_cat, use)
        return 0

    lax.fori_loop(0, earlier // STEP, step, 0)
    for g in range(group):
        part = acc[g * tok:(g + 1) * tok, :]
        o_ref[:, g * HD:(g + 1) * HD] = (part[:, :HD] / part[:, HD:]).astype(o_ref.dtype)


def attend(queries, k_pieces, v_pieces, order, me, chunk, half, after=()):
    tok = half
    pieces = len(k_pieces)
    shard, kv_width = k_pieces[0].shape
    kv_local = kv_width // HD
    width = queries.shape[1] // kv_local
    keys = shard * pieces
    rows = width // HD * tok
    tile = min(rows, 256)
    piece_spec = pl.BlockSpec((shard, HD), lambda h, *_: (0, h))
    return pl.pallas_call(
        functools.partial(attend_kernel, half, tile, chunk, pieces, len(after)),
        out_shape=jax.ShapeDtypeStruct((tok, queries.shape[1]), jnp.bfloat16),
        grid_spec=pltpu.PrefetchScalarGridSpec(
            num_scalar_prefetch=2,
            grid=(kv_local,),
            in_specs=[pl.BlockSpec((tok, width), lambda h, *refs: (block_place(chunk, *refs), h))]
            + [piece_spec] * (2 * pieces)
            + [pl.BlockSpec(memory_space=pl.ANY)] * len(after),
            out_specs=pl.BlockSpec((tok, width), lambda h, *_: (0, h)),
            scratch_shapes=[
                pltpu.SMEM((order.shape[0],), jnp.int32),
                pltpu.VMEM((rows, HD), jnp.bfloat16),
                pltpu.VMEM((keys, HD), jnp.bfloat16),
                pltpu.VMEM((keys, 2 * HD), jnp.bfloat16),
                pltpu.VMEM((rows, 2 * HD), jnp.float32),
                pltpu.VMEM((rows, HD), jnp.float32),
            ],
        ),
        compiler_params=pltpu.CompilerParams(vmem_limit_bytes=40 * MIB),
        cost_estimate=pl.CostEstimate(flops=1, bytes_accessed=0, transcendentals=0),
        name="attend",
    )(order, me, in_hbm(queries), in_hbm(k_pieces[0]), *k_pieces[1:], in_hbm(v_pieces[0]), *v_pieces[1:], *after)


def exchange(arrays, axis, bits):
    count = lax.axis_size(axis)
    held = {0: arrays}
    for bit in bits:
        pairs = [(i, i ^ (1 << bit)) for i in range(count)]
        held.update({r ^ (1 << bit): lax.ppermute(a, axis, pairs) for r, a in held.items()})
    return [held[r] for r in range(count)]


def pick(z, options):
    value = jnp.int32(options[-1])
    for i in range(len(options) - 1):
        value = jnp.where(z == i, jnp.int32(options[i]), value)
    return value


def share_kernel(extra, blocks, z_ref, a_ref, w_ref, *refs):
    @pl.when(pick(z_ref[0], blocks) >= 0)
    def _():
        total = jnp.dot(a_ref[...], w_ref[...], preferred_element_type=jnp.float32)
        for ref in refs[:extra]:
            total = total + ref[...].astype(jnp.float32)
        refs[-1][...] = total.astype(refs[-1].dtype)


def share(attended, w_out, arrived, z, blocks, columns, after=(), kind=jnp.bfloat16):
    tok, depth = attended.shape
    wide = min(columns, 512)
    tiles = columns // wide
    extra = len(arrived)

    def at(j, z_ref):
        block = pick(z_ref[0], blocks)
        return (0, jnp.maximum(block, 0) * tiles + jnp.where(block >= 0, j, 0))

    def inside(j, z_ref):
        return (0, jnp.where(pick(z_ref[0], blocks) >= 0, j, 0))

    return pl.pallas_call(
        functools.partial(share_kernel, extra, blocks),
        out_shape=jax.ShapeDtypeStruct((tok, columns), kind),
        grid_spec=pltpu.PrefetchScalarGridSpec(
            num_scalar_prefetch=1,
            grid=(tiles,),
            in_specs=[
                pl.BlockSpec((tok, depth), lambda j, z_ref: (0, 0)),
                pl.BlockSpec((depth, wide), at),
            ] + [pl.BlockSpec((tok, wide), inside)] * extra
            + [pl.BlockSpec(memory_space=pl.ANY)] * len(after),
            out_specs=pl.BlockSpec((tok, wide), inside),
        ),
        compiler_params=pltpu.CompilerParams(vmem_limit_bytes=40 * MIB),
        cost_estimate=pl.CostEstimate(flops=1, bytes_accessed=0, transcendentals=0),
        name="share",
    )(z, attended, in_hbm(w_out), *arrived, *after)


def finish_kernel(extra, order_ref, me_ref, *refs):
    total = refs[0][...].astype(jnp.float32)
    for ref in refs[1:extra]:
        total = total + ref[...].astype(jnp.float32)
    refs[-1][...] = total.astype(jnp.bfloat16)


def finish(terms, order, me, chunk, whole_tok, out):
    tok, columns = terms[0].shape
    wide = min(columns, 1024)
    operands = list(terms)
    specs = [pl.BlockSpec((tok, wide), lambda j, *_: (0, j))] * len(terms)
    aliases = {}
    if out is not None:
        operands.append(out)
        specs.append(pl.BlockSpec(memory_space=pl.ANY))
        aliases = {1 + len(operands): 0}
    return pl.pallas_call(
        functools.partial(finish_kernel, len(terms)),
        out_shape=jax.ShapeDtypeStruct((whole_tok, columns), jnp.bfloat16),
        grid_spec=pltpu.PrefetchScalarGridSpec(
            num_scalar_prefetch=2,
            grid=(columns // wide,),
            in_specs=specs,
            out_specs=pl.BlockSpec((tok, wide), lambda j, *refs: (block_place(chunk, *refs), j)),
        ),
        input_output_aliases=aliases,
        compiler_params=pltpu.CompilerParams(vmem_limit_bytes=40 * MIB),
        cost_estimate=pl.CostEstimate(flops=1, bytes_accessed=0, transcendentals=0),
        name="finish",
    )(order, me, *operands)


def swap(array, pairs):
    return lax.ppermute(array, "head", pairs)


def line_of_four(attended, w_out, z, order, me, columns, tok):
    outer, inner, back = [(0, 1), (3, 2)], [(1, 2), (2, 1)], [(1, 0), (2, 3)]

    def part(a, arrived, blocks, after=(), kind=jnp.bfloat16):
        return share(a, w_out, arrived, z, blocks, columns, after, kind)

    far_end, near_end, last_end = (3, -1, -1, 0), (2, -1, -1, 1), (1, -1, -1, 2)
    far_on, near_on, home_on, all_own = (-1, 3, 0, -1), (-1, 2, 1, -1), (-1, 0, 3, -1), (0, 1, 2, 3)
    a0 = attended(0, [])
    far0 = part(a0, [], far_end)
    near0 = part(a0, [], near_end, [far0])
    a1 = attended(1, [near0])
    far0, near0 = swap(far0, outer), swap(near0, outer)
    far1 = part(a1, [], far_end)
    mid0 = part(a0, [far0], far_on, [far1])
    near1 = part(a1, [], near_end, [mid0])
    far1, far0 = swap(far1, outer), swap(mid0, inner)
    mid1 = part(a0, [near0], near_on, [near1])
    last0 = part(a0, [], last_end, [mid1])
    last1 = part(a1, [], last_end, [last0])
    near1, near0 = swap(near1, outer), swap(mid1, inner)
    home0 = part(a0, [far0], home_on, [last1])
    last0, last1 = swap(last0, outer), swap(last1, outer)
    mid0 = part(a1, [far1], far_on, [home0])
    home0, far1 = swap(home0, back), swap(mid0, inner)
    own0 = part(a0, [], all_own, [mid0], jnp.float32)
    mid1 = part(a1, [near1], near_on, [own0])
    near1 = swap(mid1, inner)
    own1 = part(a1, [], all_own, [mid1], jnp.float32)
    home1 = swap(part(a1, [far1], home_on, [own1]), back)
    out = finish([own0, near0, last0, home0], order, me, 0, tok, None)
    return finish([own1, near1, last1, home1], order, me, 1, tok, out)


def per_device(queries, keys, values, w_out, order):
    tok = queries.shape[0]
    half = tok // 2
    line = lax.axis_size("head")
    columns = w_out.shape[1] // line
    me = lax.axis_index("blk").astype(jnp.int32).reshape(1)
    z = lax.axis_index("head").astype(jnp.int32).reshape(1)
    bits = list(range(1, lax.axis_size("blk").bit_length() - 1))
    k_pieces = exchange(keys, "blk", bits + [0])
    v_pieces = exchange(values, "blk", bits[::-1] + [0])

    def attended(chunk, after):
        return attend(queries, k_pieces, v_pieces, order, me, chunk, half, after)

    if line == 4:
        return line_of_four(attended, w_out, z, order, me, columns, tok)
    outs = []
    for c in range(2):
        sums = jnp.dot(attended(c, []), w_out, preferred_element_type=jnp.float32)
        outs.append(lax.psum_scatter(
            sums.astype(jnp.bfloat16), "head", scatter_dimension=1, tiled=True))
    swapped = block_place(0, order, me) == 1
    outs = [jnp.where(swapped, outs[1 - c], outs[c]) for c in range(2)]
    return jnp.concatenate(outs, axis=0)


def solution(mesh):
    return jax.shard_map(
        per_device,
        mesh=mesh,
        in_specs=(P("blk", "head"), P("blk", "head"), P("blk", "head"), P("head", None), P()),
        out_specs=P("blk", "head"),
        check_vma=False,
    )
```

```python
import functools
import math

import jax
import jax.numpy as jnp
from jax import lax
from jax.experimental import pallas as pl
from jax.experimental.pallas import tpu as pltpu
from jax.sharding import PartitionSpec as P

HD = 128
NT = (((1,), (1,)), ((), ()))
MIB = 2 ** 20
STEP = 4


def in_hbm(array):
    return pltpu.with_memory_space_constraint(array, pltpu.HBM)


def block_place(chunk, order_ref, me_ref):
    own = 2 * me_ref[0]
    return jnp.where(order_ref[own] > order_ref[own + 1], 1 - chunk, chunk)


def attend_kernel(half, chunk, pieces, heads, waited, order_ref, me_ref, q_ref, *refs):
    k_refs, v_refs = refs[:pieces], refs[pieces:2 * pieces]
    o_ref, inv, q_heads, k_all, v_wide, acc, top, sems = refs[2 * pieces + waited:]
    blocks = order_ref.shape[0]
    per = blocks // pieces
    tile = half
    width = o_ref.shape[1]
    group = width // HD
    shard = per * half
    factor = HD ** (-0.5) * math.log2(math.e)
    own = block_place(chunk, order_ref, me_ref)
    me = me_ref[0]
    head = pl.program_id(0)

    def copies(h):
        rows = pl.ds(pl.multiple_of(own * half, half), half)
        pairs = [(q_ref.at[rows, pl.ds(h * width, width)], q_heads.at[h])]
        for r in range(pieces):
            here = pl.ds(r * shard, shard)
            lanes = pl.ds(h * HD, HD)
            pairs.append((k_refs[r].at[:, lanes], k_all.at[h, here, :]))
            pairs.append((v_refs[r].at[:, lanes], v_wide.at[h, here, pl.ds(0, HD)]))
        return [pltpu.make_async_copy(src, dst, sems.at[h, i])
                for i, (src, dst) in enumerate(pairs)]

    @pl.when(head == 0)
    def _():
        for h in range(heads):
            for copy in copies(h):
                copy.start()

    def invert(b, _):
        inv[order_ref[b]] = jnp.bitwise_xor(b // per, me) * per + lax.rem(b, per)
        return 0

    lax.fori_loop(0, blocks, invert, 0)
    v_wide[head, :, HD:] = jnp.ones((v_wide.shape[1], HD), v_wide.dtype)
    for h in range(heads):
        @pl.when(head == h)
        def _():
            for copy in copies(h):
                copy.wait()

    earlier = order_ref[me * per + own]

    def block_of(ref, b):
        return ref[head, pl.ds(pl.multiple_of(b * half, half), half), :]

    def first(blocks_in):
        k_cat = jnp.concatenate([block_of(k_all, b) for b in blocks_in], axis=0)
        v_cat = jnp.concatenate([block_of(v_wide, b) for b in blocks_in], axis=0)
        width = k_cat.shape[0]
        query = lax.rem(lax.broadcasted_iota(jnp.int32, (tile, width), 0), tok)
        key = lax.broadcasted_iota(jnp.int32, (tile, width), 1) - (width - half)
        seen = key <= query
        for r in range(0, rows, tile):
            score = lax.dot_general(q_rows[r:r + tile, :], k_cat, NT,
                                    preferred_element_type=jnp.float32)
            score = jnp.where(seen, score, -1e30)
            peak = jnp.max(score, axis=1, keepdims=True)
            weight = jnp.exp2((score - peak) * factor)
            top[r:r + tile, :] = jnp.broadcast_to(peak, (tile, HD))
            acc[r:r + tile, :] = jnp.dot(weight.astype(jnp.bfloat16), v_cat,
                                         preferred_element_type=jnp.float32)

    def keys_of(blocks_in):
        return (jnp.concatenate([block_of(k_all, b) for b in blocks_in], axis=0),
                jnp.concatenate([block_of(v_wide, b) for b in blocks_in], axis=0))

    def over_tiles(k_cat, use):
        def scores(g):
            return lax.dot_general(q_heads[head, :, g * HD:(g + 1) * HD], k_cat, NT,
                                   preferred_element_type=jnp.float32)

        score = scores(0)
        for g in range(group):
            ahead = scores(g + 1) if g + 1 < group else None
            use(g * tile, score)
            score = ahead

    def first(rest):
        k_cat, v_cat = keys_of([inv[earlier - rest + i] for i in range(rest)] + [own])
        query = lax.broadcasted_iota(jnp.int32, (tile, half), 0)
        seen = lax.broadcasted_iota(jnp.int32, (tile, half), 1) <= query

        def use(r, score):
            masked = jnp.where(seen, score[:, rest * half:], -1e30)
            score = jnp.concatenate([score[:, :rest * half], masked], axis=1) if rest else masked
            peak = jnp.max(score, axis=1, keepdims=True)
            weight = jnp.exp2((score - peak) * factor)
            top[r:r + tile, :] = jnp.broadcast_to(peak, (tile, HD))
            acc[r:r + tile, :] = jnp.dot(weight.astype(jnp.bfloat16), v_cat,
                                         preferred_element_type=jnp.float32)

        over_tiles(k_cat, use)

    for rest in range(STEP):
        pl.when(lax.rem(earlier, STEP) == rest)(functools.partial(first, rest))

    def step(n, _):
        k_cat, v_cat = keys_of([inv[STEP * n + i] for i in range(STEP)])

        def use(r, score):
            old = top[r:r + tile, :]
            peak = jnp.maximum(old, jnp.max(score, axis=1, keepdims=True))
            top[r:r + tile, :] = peak
            wide = jnp.concatenate([peak] * (STEP * half // HD), axis=1)
            weight = jnp.exp2((score - wide) * factor)
            shrink = jnp.exp2((old - peak) * factor)
            acc[r:r + tile, :] = acc[r:r + tile, :] * jnp.concatenate(
                [shrink, shrink], axis=1) + jnp.dot(
                    weight.astype(jnp.bfloat16), v_cat, preferred_element_type=jnp.float32)

        over_tiles(k_cat, use)
        return 0

    lax.fori_loop(0, earlier // STEP, step, 0)
    for g in range(group):
        part = acc[g * tile:(g + 1) * tile, :]
        o_ref[:, g * HD:(g + 1) * HD] = (part[:, :HD] / part[:, HD:]).astype(o_ref.dtype)


def attend(queries, k_pieces, v_pieces, order, me, chunk, half, after=()):
    pieces = len(k_pieces)
    shard, kv_width = k_pieces[0].shape
    heads = kv_width // HD
    width = queries.shape[1] // heads
    keys = shard * pieces
    rows = width // HD * half
    anywhere = pl.BlockSpec(memory_space=pl.ANY)
    return pl.pallas_call(
        functools.partial(attend_kernel, half, chunk, pieces, heads, len(after)),
        out_shape=jax.ShapeDtypeStruct((half, queries.shape[1]), jnp.bfloat16),
        grid_spec=pltpu.PrefetchScalarGridSpec(
            num_scalar_prefetch=2,
            grid=(heads,),
            in_specs=[anywhere] * (1 + 2 * pieces + len(after)),
            out_specs=pl.BlockSpec((half, width), lambda h, *_: (0, h)),
            scratch_shapes=[
                pltpu.SMEM((order.shape[0],), jnp.int32),
                pltpu.VMEM((heads, half, width), jnp.bfloat16),
                pltpu.VMEM((heads, keys, HD), jnp.bfloat16),
                pltpu.VMEM((heads, keys, 2 * HD), jnp.bfloat16),
                pltpu.VMEM((rows, 2 * HD), jnp.float32),
                pltpu.VMEM((rows, HD), jnp.float32),
                pltpu.SemaphoreType.DMA((heads, 2 * pieces + 1)),
            ],
        ),
        compiler_params=pltpu.CompilerParams(vmem_limit_bytes=40 * MIB),
        cost_estimate=pl.CostEstimate(flops=1, bytes_accessed=0, transcendentals=0),
        name="attend",
    )(order, me, in_hbm(queries), in_hbm(k_pieces[0]), *k_pieces[1:],
      in_hbm(v_pieces[0]), *v_pieces[1:], *after)


def exchange(arrays, axis, bits):
    count = lax.axis_size(axis)
    held = {0: arrays}
    for bit in bits:
        pairs = [(i, i ^ (1 << bit)) for i in range(count)]
        held.update({r ^ (1 << bit): lax.ppermute(a, axis, pairs) for r, a in held.items()})
    return [held[r] for r in range(count)]


def pick(z, options):
    value = jnp.int32(options[-1])
    for i in range(len(options) - 1):
        value = jnp.where(z == i, jnp.int32(options[i]), value)
    return value


def share_kernel(extra, waited, blocks, z_ref, a_ref, w_ref, *refs):
    arrived = refs[:extra]
    out, tiles, sems = refs[extra + waited:]
    count, _, wide = tiles.shape
    block = pick(z_ref[0], blocks)

    @pl.when(block >= 0)
    def _():
        def copy(j):
            place = pl.multiple_of((block * count + j) * wide, wide)
            return pltpu.make_async_copy(w_ref.at[:, pl.ds(place, wide)], tiles.at[j], sems.at[j])

        def column(j, _):
            copy(j).wait()
            lanes = pl.ds(pl.multiple_of(j * wide, wide), wide)
            total = jnp.dot(a_ref[...], tiles[j], preferred_element_type=jnp.float32)
            for ref in arrived:
                total = total + ref[:, lanes].astype(jnp.float32)
            out[:, lanes] = total.astype(out.dtype)
            return 0

        for j in range(count):
            copy(j).start()
        lax.fori_loop(0, count, column, 0)


def share(attended, w_out, arrived, z, blocks, columns, after=(), kind=jnp.bfloat16):
    tok, depth = attended.shape
    wide = min(columns, 256)
    count = columns // wide
    extra = len(arrived)
    whole = pl.BlockSpec(memory_space=pltpu.VMEM)
    anywhere = pl.BlockSpec(memory_space=pl.ANY)
    return pl.pallas_call(
        functools.partial(share_kernel, extra, len(after), blocks),
        out_shape=jax.ShapeDtypeStruct((tok, columns), kind),
        grid_spec=pltpu.PrefetchScalarGridSpec(
            num_scalar_prefetch=1,
            grid=(),
            in_specs=[whole, anywhere] + [whole] * extra + [anywhere] * len(after),
            out_specs=whole,
            scratch_shapes=[
                pltpu.VMEM((count, depth, wide), w_out.dtype),
                pltpu.SemaphoreType.DMA((count,)),
            ],
        ),
        compiler_params=pltpu.CompilerParams(vmem_limit_bytes=40 * MIB),
        cost_estimate=pl.CostEstimate(flops=1, bytes_accessed=0, transcendentals=0),
        name="share",
    )(z, attended, in_hbm(w_out), *arrived, *after)


def finish_kernel(extra, order_ref, me_ref, *refs):
    total = refs[0][...].astype(jnp.float32)
    for ref in refs[1:extra]:
        total = total + ref[...].astype(jnp.float32)
    refs[-1][...] = total.astype(jnp.bfloat16)


def finish(terms, order, me, chunk, whole_tok, out):
    tok, columns = terms[0].shape
    wide = min(columns, 1024)
    operands = list(terms)
    specs = [pl.BlockSpec((tok, wide), lambda j, *_: (0, j))] * len(terms)
    aliases = {}
    if out is not None:
        operands.append(out)
        specs.append(pl.BlockSpec(memory_space=pl.ANY))
        aliases = {1 + len(operands): 0}
    return pl.pallas_call(
        functools.partial(finish_kernel, len(terms)),
        out_shape=jax.ShapeDtypeStruct((whole_tok, columns), jnp.bfloat16),
        grid_spec=pltpu.PrefetchScalarGridSpec(
            num_scalar_prefetch=2,
            grid=(columns // wide,),
            in_specs=specs,
            out_specs=pl.BlockSpec((tok, wide), lambda j, *refs: (block_place(chunk, *refs), j)),
        ),
        input_output_aliases=aliases,
        compiler_params=pltpu.CompilerParams(vmem_limit_bytes=40 * MIB),
        cost_estimate=pl.CostEstimate(flops=1, bytes_accessed=0, transcendentals=0),
        name="finish",
    )(order, me, *operands)


def swap(array, pairs):
    return lax.ppermute(array, "head", pairs)


def line_of_four(attended, w_out, z, order, me, columns, tok):
    outer, inner, back = [(0, 1), (3, 2)], [(1, 2), (2, 1)], [(1, 0), (2, 3)]

    def part(a, arrived, blocks, after=(), kind=jnp.bfloat16):
        return share(a, w_out, arrived, z, blocks, columns, after, kind)

    far_end, near_end, last_end = (3, -1, -1, 0), (2, -1, -1, 1), (1, -1, -1, 2)
    far_on, near_on, home_on, all_own = (-1, 3, 0, -1), (-1, 2, 1, -1), (-1, 0, 3, -1), (0, 1, 2, 3)
    a0 = attended(0, [])
    far0 = part(a0, [], far_end)
    near0 = part(a0, [], near_end, [far0])
    a1 = attended(1, [near0])
    far0, near0 = swap(far0, outer), swap(near0, outer)
    far1 = part(a1, [], far_end)
    mid0 = part(a0, [far0], far_on, [far1])
    near1 = part(a1, [], near_end, [mid0])
    far1, far0 = swap(far1, outer), swap(mid0, inner)
    mid1 = part(a0, [near0], near_on, [near1])
    last0 = part(a0, [], last_end, [mid1])
    last1 = part(a1, [], last_end, [last0])
    near1, near0 = swap(near1, outer), swap(mid1, inner)
    home0 = part(a0, [far0], home_on, [last1])
    last0, last1 = swap(last0, outer), swap(last1, outer)
    mid0 = part(a1, [far1], far_on, [home0])
    home0, far1 = swap(home0, back), swap(mid0, inner)
    own0 = part(a0, [], all_own, [mid0], jnp.float32)
    mid1 = part(a1, [near1], near_on, [own0])
    near1 = swap(mid1, inner)
    own1 = part(a1, [], all_own, [mid1, near0, home0], jnp.float32)
    home1 = swap(part(a1, [far1], home_on, [own1]), back)
    out = finish([own0, near0, last0, home0], order, me, 0, tok, None)
    return finish([own1, near1, last1, home1], order, me, 1, tok, out)


def per_device(queries, keys, values, w_out, order):
    tok = queries.shape[0]
    half = tok // 2
    line = lax.axis_size("head")
    columns = w_out.shape[1] // line
    me = lax.axis_index("blk").astype(jnp.int32).reshape(1)
    z = lax.axis_index("head").astype(jnp.int32).reshape(1)
    bits = list(range(1, lax.axis_size("blk").bit_length() - 1))
    k_pieces = exchange(keys, "blk", bits + [0])
    v_pieces = exchange(values, "blk", bits[::-1] + [0])

    def attended(chunk, after):
        return attend(queries, k_pieces, v_pieces, order, me, chunk, half, after)

    if line == 4:
        return line_of_four(attended, w_out, z, order, me, columns, tok)
    outs = []
    for c in range(2):
        sums = jnp.dot(attended(c, []), w_out, preferred_element_type=jnp.float32)
        outs.append(lax.psum_scatter(
            sums.astype(jnp.bfloat16), "head", scatter_dimension=1, tiled=True))
    swapped = block_place(0, order, me) == 1
    outs = [jnp.where(swapped, outs[1 - c], outs[c]) for c in range(2)]
    return jnp.concatenate(outs, axis=0)


def solution(mesh):
    return jax.shard_map(
        per_device,
        mesh=mesh,
        in_specs=(P("blk", "head"), P("blk", "head"), P("blk", "head"), P("head", None), P()),
        out_specs=P("blk", "head"),
        check_vma=False,
    )
```

```python
import functools
import math

import jax
import jax.numpy as jnp
from jax import lax
from jax.experimental import pallas as pl
from jax.experimental.pallas import tpu as pltpu
from jax.sharding import PartitionSpec as P

HD = 128
NT = (((1,), (1,)), ((), ()))
MIB = 2 ** 20
STEP = 4
LIMIT = 64.0


def in_hbm(array):
    return pltpu.with_memory_space_constraint(array, pltpu.HBM)


def block_place(chunk, order_ref, me_ref):
    own = 2 * me_ref[0]
    return jnp.where(order_ref[own] > order_ref[own + 1], 1 - chunk, chunk)


def attend_kernel(half, chunk, pieces, heads, waited, order_ref, me_ref, q_ref, *refs):
    k_refs, v_refs = refs[:pieces], refs[pieces:2 * pieces]
    o_ref, inv, redo, q_all, k_all, v_all, v_wide, acc, top, above, sems = refs[2 * pieces + waited:]
    blocks = order_ref.shape[0]
    per = blocks // pieces
    tile = half
    width = o_ref.shape[1]
    group = width // HD
    shard = per * half
    factor = HD ** (-0.5) * math.log2(math.e)
    own = block_place(chunk, order_ref, me_ref)
    me = me_ref[0]
    head = pl.program_id(0)
    lanes = pl.ds(pl.multiple_of(head * HD, HD), HD)

    @pl.when(head == 0)
    def _():
        mine = pl.ds(pl.multiple_of(own * half, half), half)
        pairs = [(q_ref.at[mine, :], q_all)]
        for r in range(pieces):
            here = pl.ds(r * shard, shard)
            pairs += [(k_refs[r], k_all.at[here, :]), (v_refs[r], v_all.at[here, :])]
        copies = [pltpu.make_async_copy(src, dst, sems.at[i]) for i, (src, dst) in enumerate(pairs)]
        for copy in copies:
            copy.start()

        def invert(b, _):
            inv[order_ref[b]] = jnp.bitwise_xor(b // per, me) * per + lax.rem(b, per)
            return 0

        lax.fori_loop(0, blocks, invert, 0)
        v_wide[:, HD:] = jnp.ones((v_wide.shape[0], HD), v_wide.dtype)
        for copy in copies:
            copy.wait()

    v_wide[:, :HD] = v_all[:, lanes]
    earlier = order_ref[me * per + own]

    def keys_of(blocks_in):
        rows = [pl.ds(pl.multiple_of(b * half, half), half) for b in blocks_in]
        return (jnp.concatenate([k_all[r, lanes] for r in rows], axis=0),
                jnp.concatenate([v_wide[r, :] for r in rows], axis=0))

    def over_tiles(k_cat, use):
        def scores(g):
            at = pl.ds(pl.multiple_of(head * width + g * HD, HD), HD)
            return lax.dot_general(q_all[:, at], k_cat, NT, preferred_element_type=jnp.float32)

        score = scores(0)
        for g in range(group):
            ahead = scores(g + 1) if g + 1 < group else None
            use(pl.ds(g * tile, tile), score)
            score = ahead

    def first(rest):
        k_cat, v_cat = keys_of([inv[earlier - rest + i] for i in range(rest)] + [own])
        query = lax.broadcasted_iota(jnp.int32, (tile, half), 0)
        seen = lax.broadcasted_iota(jnp.int32, (tile, half), 1) <= query

        def use(rows, score):
            masked = jnp.where(seen, score[:, rest * half:], -1e30)
            score = jnp.concatenate([score[:, :rest * half], masked], axis=1) if rest else masked
            peak = jnp.max(score, axis=1, keepdims=True)
            weight = jnp.exp2((score - peak) * factor)
            top[rows, :] = jnp.broadcast_to(peak, (tile, HD))
            acc[rows, :] = jnp.dot(weight.astype(jnp.bfloat16), v_cat,
                                   preferred_element_type=jnp.float32)

        over_tiles(k_cat, use)

    def wide(array):
        return jnp.concatenate([array] * (STEP * half // HD), axis=1)

    def step(n, _):
        k_cat, v_cat = keys_of([inv[STEP * n + i] for i in range(STEP)])

        def use(rows, score):
            power = (score - wide(top[rows, :])) * factor
            above[...] = jnp.maximum(
                above[...], jnp.max(power.reshape(-1, 8, power.shape[1]), axis=0))
            acc[rows, :] = acc[rows, :] + jnp.dot(
                jnp.exp2(power).astype(jnp.bfloat16), v_cat, preferred_element_type=jnp.float32)

        over_tiles(k_cat, use)
        return 0

    def careful_step(n, _):
        k_cat, v_cat = keys_of([inv[STEP * n + i] for i in range(STEP)])

        def one(g, _):
            at = pl.ds(pl.multiple_of(head * width + g * HD, HD), HD)
            rows = pl.ds(pl.multiple_of(g * tile, tile), tile)
            score = lax.dot_general(q_all[:, at], k_cat, NT, preferred_element_type=jnp.float32)
            old = top[rows, :]
            peak = jnp.maximum(old, jnp.max(score, axis=1, keepdims=True))
            top[rows, :] = peak
            weight = jnp.exp2((score - wide(peak)) * factor)
            shrink = jnp.exp2((old - peak) * factor)
            acc[rows, :] = acc[rows, :] * jnp.concatenate([shrink, shrink], axis=1) + jnp.dot(
                weight.astype(jnp.bfloat16), v_cat, preferred_element_type=jnp.float32)
            return 0

        lax.fori_loop(0, group, one, 0)
        return 0

    redo[0] = 1
    above[...] = jnp.zeros_like(above)

    def attempt(i, _):
        @pl.when(redo[0] == 1)
        def _():
            for rest in range(STEP):
                pl.when(lax.rem(earlier, STEP) == rest)(functools.partial(first, rest))

            @pl.when(i == 0)
            def _():
                lax.fori_loop(0, earlier // STEP, step, 0)
                redo[0] = (jnp.max(above[...]) > LIMIT).astype(jnp.int32)

            @pl.when(i == 1)
            def _():
                lax.fori_loop(0, earlier // STEP, careful_step, 0)

        return 0

    lax.fori_loop(0, 2, attempt, 0)
    for g in range(group):
        part = acc[g * tile:(g + 1) * tile, :]
        o_ref[:, g * HD:(g + 1) * HD] = (part[:, :HD] / part[:, HD:]).astype(o_ref.dtype)


def attend(queries, k_pieces, v_pieces, order, me, chunk, half, after=()):
    pieces = len(k_pieces)
    shard, kv_width = k_pieces[0].shape
    heads = kv_width // HD
    width = queries.shape[1] // heads
    keys = shard * pieces
    rows = width // HD * half
    anywhere = pl.BlockSpec(memory_space=pl.ANY)
    return pl.pallas_call(
        functools.partial(attend_kernel, half, chunk, pieces, heads, len(after)),
        out_shape=jax.ShapeDtypeStruct((half, queries.shape[1]), jnp.bfloat16),
        grid_spec=pltpu.PrefetchScalarGridSpec(
            num_scalar_prefetch=2,
            grid=(heads,),
            in_specs=[anywhere] * (1 + 2 * pieces + len(after)),
            out_specs=pl.BlockSpec((half, width), lambda h, *_: (0, h)),
            scratch_shapes=[
                pltpu.SMEM((order.shape[0],), jnp.int32),
                pltpu.SMEM((1,), jnp.int32),
                pltpu.VMEM((half, heads * width), jnp.bfloat16),
                pltpu.VMEM((keys, kv_width), jnp.bfloat16),
                pltpu.VMEM((keys, kv_width), jnp.bfloat16),
                pltpu.VMEM((keys, 2 * HD), jnp.bfloat16),
                pltpu.VMEM((rows, 2 * HD), jnp.float32),
                pltpu.VMEM((rows, HD), jnp.float32),
                pltpu.VMEM((8, STEP * half), jnp.float32),
                pltpu.SemaphoreType.DMA((2 * pieces + 1,)),
            ],
        ),
        compiler_params=pltpu.CompilerParams(vmem_limit_bytes=40 * MIB),
        cost_estimate=pl.CostEstimate(flops=1, bytes_accessed=0, transcendentals=0),
        name="attend",
    )(order, me, in_hbm(queries), in_hbm(k_pieces[0]), *k_pieces[1:],
      in_hbm(v_pieces[0]), *v_pieces[1:], *after)


def exchange(arrays, axis, bits):
    count = lax.axis_size(axis)
    held = {0: arrays}
    for bit in bits:
        pairs = [(i, i ^ (1 << bit)) for i in range(count)]
        held.update({r ^ (1 << bit): lax.ppermute(a, axis, pairs) for r, a in held.items()})
    return [held[r] for r in range(count)]


def pick(z, options):
    value = jnp.int32(options[-1])
    for i in range(len(options) - 1):
        value = jnp.where(z == i, jnp.int32(options[i]), value)
    return value


def share_kernel(extra, waited, blocks, z_ref, a_ref, w_ref, *refs):
    arrived = refs[:extra]
    out, tiles, sems = refs[extra + waited:]
    count, _, wide = tiles.shape
    block = pick(z_ref[0], blocks)

    @pl.when(block >= 0)
    def _():
        def copy(j):
            place = pl.multiple_of((block * count + j) * wide, wide)
            return pltpu.make_async_copy(w_ref.at[:, pl.ds(place, wide)], tiles.at[j], sems.at[j])

        def column(j, _):
            copy(j).wait()
            lanes = pl.ds(pl.multiple_of(j * wide, wide), wide)
            total = jnp.dot(a_ref[...], tiles[j], preferred_element_type=jnp.float32)
            for ref in arrived:
                total = total + ref[:, lanes].astype(jnp.float32)
            out[:, lanes] = total.astype(out.dtype)
            return 0

        for j in range(count):
            copy(j).start()
        lax.fori_loop(0, count, column, 0)


def share(attended, w_out, arrived, z, blocks, columns, after=(), kind=jnp.bfloat16):
    tok, depth = attended.shape
    wide = min(columns, 256)
    count = columns // wide
    extra = len(arrived)
    whole = pl.BlockSpec(memory_space=pltpu.VMEM)
    anywhere = pl.BlockSpec(memory_space=pl.ANY)
    return pl.pallas_call(
        functools.partial(share_kernel, extra, len(after), blocks),
        out_shape=jax.ShapeDtypeStruct((tok, columns), kind),
        grid_spec=pltpu.PrefetchScalarGridSpec(
            num_scalar_prefetch=1,
            grid=(),
            in_specs=[whole, anywhere] + [whole] * extra + [anywhere] * len(after),
            out_specs=whole,
            scratch_shapes=[
                pltpu.VMEM((count, depth, wide), w_out.dtype),
                pltpu.SemaphoreType.DMA((count,)),
            ],
        ),
        compiler_params=pltpu.CompilerParams(vmem_limit_bytes=40 * MIB),
        cost_estimate=pl.CostEstimate(flops=1, bytes_accessed=0, transcendentals=0),
        name="share",
    )(z, attended, in_hbm(w_out), *arrived, *after)


def finish_kernel(extra, order_ref, me_ref, *refs):
    total = refs[0][...].astype(jnp.float32)
    for ref in refs[1:extra]:
        total = total + ref[...].astype(jnp.float32)
    refs[-1][...] = total.astype(jnp.bfloat16)


def finish(terms, order, me, chunk, whole_tok, out):
    tok, columns = terms[0].shape
    wide = min(columns, 1024)
    operands = list(terms)
    specs = [pl.BlockSpec((tok, wide), lambda j, *_: (0, j))] * len(terms)
    aliases = {}
    if out is not None:
        operands.append(out)
        specs.append(pl.BlockSpec(memory_space=pl.ANY))
        aliases = {1 + len(operands): 0}
    return pl.pallas_call(
        functools.partial(finish_kernel, len(terms)),
        out_shape=jax.ShapeDtypeStruct((whole_tok, columns), jnp.bfloat16),
        grid_spec=pltpu.PrefetchScalarGridSpec(
            num_scalar_prefetch=2,
            grid=(columns // wide,),
            in_specs=specs,
            out_specs=pl.BlockSpec((tok, wide), lambda j, *refs: (block_place(chunk, *refs), j)),
        ),
        input_output_aliases=aliases,
        compiler_params=pltpu.CompilerParams(vmem_limit_bytes=40 * MIB),
        cost_estimate=pl.CostEstimate(flops=1, bytes_accessed=0, transcendentals=0),
        name="finish",
    )(order, me, *operands)


def swap(array, pairs):
    return lax.ppermute(array, "head", pairs)


def line_of_four(attended, w_out, z, order, me, columns, tok):
    outer, inner, back = [(0, 1), (3, 2)], [(1, 2), (2, 1)], [(1, 0), (2, 3)]

    def part(a, arrived, blocks, after=(), kind=jnp.bfloat16):
        return share(a, w_out, arrived, z, blocks, columns, after, kind)

    far_end, near_end, last_end = (3, -1, -1, 0), (2, -1, -1, 1), (1, -1, -1, 2)
    far_on, near_on, home_on, all_own = (-1, 3, 0, -1), (-1, 2, 1, -1), (-1, 0, 3, -1), (0, 1, 2, 3)
    a0 = attended(0, [])
    far0 = part(a0, [], far_end)
    near0 = part(a0, [], near_end, [far0])
    a1 = attended(1, [near0])
    far0, near0 = swap(far0, outer), swap(near0, outer)
    far1 = part(a1, [], far_end)
    mid0 = part(a0, [far0], far_on, [far1])
    near1 = part(a1, [], near_end, [mid0])
    far1, far0 = swap(far1, outer), swap(mid0, inner)
    mid1 = part(a0, [near0], near_on, [near1])
    last0 = part(a0, [], last_end, [mid1])
    last1 = part(a1, [], last_end, [last0])
    near1, near0 = swap(near1, outer), swap(mid1, inner)
    home0 = part(a0, [far0], home_on, [last1])
    last0, last1 = swap(last0, outer), swap(last1, outer)
    mid0 = part(a1, [far1], far_on, [home0])
    home0, far1 = swap(home0, back), swap(mid0, inner)
    own0 = part(a0, [], all_own, [mid0], jnp.float32)
    mid1 = part(a1, [near1], near_on, [own0])
    near1 = swap(mid1, inner)
    own1 = part(a1, [], all_own, [mid1, near0, home0], jnp.float32)
    home1 = swap(part(a1, [far1], home_on, [own1]), back)
    out = finish([own0, near0, last0, home0], order, me, 0, tok, None)
    return finish([own1, near1, last1, home1], order, me, 1, tok, out)


def per_device(queries, keys, values, w_out, order):
    tok = queries.shape[0]
    half = tok // 2
    line = lax.axis_size("head")
    columns = w_out.shape[1] // line
    me = lax.axis_index("blk").astype(jnp.int32).reshape(1)
    z = lax.axis_index("head").astype(jnp.int32).reshape(1)
    bits = list(range(1, lax.axis_size("blk").bit_length() - 1))
    k_pieces = exchange(keys, "blk", bits + [0])
    v_pieces = exchange(values, "blk", bits[::-1] + [0])

    def attended(chunk, after):
        return attend(queries, k_pieces, v_pieces, order, me, chunk, half, after)

    if line == 4:
        return line_of_four(attended, w_out, z, order, me, columns, tok)
    outs = []
    for c in range(2):
        sums = jnp.dot(attended(c, []), w_out, preferred_element_type=jnp.float32)
        outs.append(lax.psum_scatter(
            sums.astype(jnp.bfloat16), "head", scatter_dimension=1, tiled=True))
    swapped = block_place(0, order, me) == 1
    outs = [jnp.where(swapped, outs[1 - c], outs[c]) for c in range(2)]
    return jnp.concatenate(outs, axis=0)


def solution(mesh):
    return jax.shard_map(
        per_device,
        mesh=mesh,
        in_specs=(P("blk", "head"), P("blk", "head"), P("blk", "head"), P("head", None), P()),
        out_specs=P("blk", "head"),
        check_vma=False,
    )
```

```python
import functools
import math

import jax
import jax.numpy as jnp
from jax import lax
from jax.experimental import pallas as pl
from jax.experimental.pallas import tpu as pltpu
from jax.sharding import PartitionSpec as P

HD = 128
NT = (((1,), (1,)), ((), ()))
MIB = 2 ** 20
STEP = 4
LIMIT = 64.0
JOINT = 4


def in_hbm(array):
    return pltpu.with_memory_space_constraint(array, pltpu.HBM)


def block_place(chunk, order_ref, me_ref):
    own = 2 * me_ref[0]
    return jnp.where(order_ref[own] > order_ref[own + 1], 1 - chunk, chunk)


def attend_kernel(half, chunk, pieces, heads, waited, order_ref, me_ref, q_ref, *refs):
    k_refs, v_refs = refs[:pieces], refs[pieces:2 * pieces]
    o_ref, inv, redo, q_all, k_all, v_all, v_wide, acc, top, above, sems = refs[2 * pieces + waited:]
    blocks = order_ref.shape[0]
    per = blocks // pieces
    tile = half
    width = o_ref.shape[1]
    group = width // HD
    joint = math.gcd(group, JOINT)
    shard = per * half
    factor = HD ** (-0.5) * math.log2(math.e)
    own = block_place(chunk, order_ref, me_ref)
    me = me_ref[0]
    head = pl.program_id(0)
    lanes = pl.ds(pl.multiple_of(head * HD, HD), HD)

    @pl.when(head == 0)
    def _():
        mine = pl.ds(pl.multiple_of(own * half, half), half)
        pairs = [(q_ref.at[mine, :], q_all)]
        for r in range(pieces):
            here = pl.ds(r * shard, shard)
            pairs += [(k_refs[r], k_all.at[here, :]), (v_refs[r], v_all.at[here, :])]
        copies = [pltpu.make_async_copy(src, dst, sems.at[i]) for i, (src, dst) in enumerate(pairs)]
        for copy in copies:
            copy.start()

        def invert(b, _):
            inv[order_ref[b]] = jnp.bitwise_xor(b // per, me) * per + lax.rem(b, per)
            return 0

        lax.fori_loop(0, blocks, invert, 0)
        v_wide[:, HD:] = jnp.ones((v_wide.shape[0], HD), v_wide.dtype)
        for copy in copies:
            copy.wait()

    v_wide[:, :HD] = v_all[:, lanes]
    earlier = order_ref[me * per + own]

    def keys_of(blocks_in):
        rows = [pl.ds(pl.multiple_of(b * half, half), half) for b in blocks_in]
        return (jnp.concatenate([k_all[r, lanes] for r in rows], axis=0),
                jnp.concatenate([v_wide[r, :] for r in rows], axis=0))

    def over_tiles(k_cat, use):
        def scores(g):
            q_cat = jnp.concatenate([
                q_all[:, pl.ds(pl.multiple_of(head * width + i * HD, HD), HD)]
                for i in range(g, g + joint)], axis=0)
            return lax.dot_general(q_cat, k_cat, NT, preferred_element_type=jnp.float32)

        score = scores(0)
        for g in range(0, group, joint):
            ahead = scores(g + joint) if g + joint < group else None
            use(pl.ds(g * tile, joint * tile), score)
            score = ahead

    def first(rest):
        k_cat, v_cat = keys_of([inv[earlier - rest + i] for i in range(rest)] + [own])
        query = lax.rem(lax.broadcasted_iota(jnp.int32, (joint * tile, half), 0), tile)
        seen = lax.broadcasted_iota(jnp.int32, (joint * tile, half), 1) <= query

        def use(rows, score):
            masked = jnp.where(seen, score[:, rest * half:], -1e30)
            score = jnp.concatenate([score[:, :rest * half], masked], axis=1) if rest else masked
            peak = jnp.max(score, axis=1, keepdims=True)
            weight = jnp.exp2((score - peak) * factor)
            top[rows, :] = jnp.broadcast_to(peak, (joint * tile, HD))
            acc[rows, :] = jnp.dot(weight.astype(jnp.bfloat16), v_cat,
                                   preferred_element_type=jnp.float32)

        over_tiles(k_cat, use)

    def wide(array):
        return jnp.concatenate([array] * (STEP * half // HD), axis=1)

    def step(n, _):
        k_cat, v_cat = keys_of([inv[STEP * n + i] for i in range(STEP)])

        def use(rows, score):
            power = (score - wide(top[rows, :])) * factor
            above[...] = jnp.maximum(
                above[...], jnp.max(power.reshape(-1, 8, power.shape[1]), axis=0))
            acc[rows, :] = acc[rows, :] + jnp.dot(
                jnp.exp2(power).astype(jnp.bfloat16), v_cat, preferred_element_type=jnp.float32)

        over_tiles(k_cat, use)
        return 0

    def careful_step(n, _):
        k_cat, v_cat = keys_of([inv[STEP * n + i] for i in range(STEP)])

        def one(g, _):
            at = pl.ds(pl.multiple_of(head * width + g * HD, HD), HD)
            rows = pl.ds(pl.multiple_of(g * tile, tile), tile)
            score = lax.dot_general(q_all[:, at], k_cat, NT, preferred_element_type=jnp.float32)
            old = top[rows, :]
            peak = jnp.maximum(old, jnp.max(score, axis=1, keepdims=True))
            top[rows, :] = peak
            weight = jnp.exp2((score - wide(peak)) * factor)
            shrink = jnp.exp2((old - peak) * factor)
            acc[rows, :] = acc[rows, :] * jnp.concatenate([shrink, shrink], axis=1) + jnp.dot(
                weight.astype(jnp.bfloat16), v_cat, preferred_element_type=jnp.float32)
            return 0

        lax.fori_loop(0, group, one, 0)
        return 0

    redo[0] = 1
    above[...] = jnp.zeros_like(above)

    def attempt(i, _):
        @pl.when(redo[0] == 1)
        def _():
            for rest in range(STEP):
                pl.when(lax.rem(earlier, STEP) == rest)(functools.partial(first, rest))

            @pl.when(i == 0)
            def _():
                lax.fori_loop(0, earlier // STEP, step, 0)
                redo[0] = (jnp.max(above[...]) > LIMIT).astype(jnp.int32)

            @pl.when(i == 1)
            def _():
                lax.fori_loop(0, earlier // STEP, careful_step, 0)

        return 0

    lax.fori_loop(0, 2, attempt, 0)
    for g in range(group):
        part = acc[g * tile:(g + 1) * tile, :]
        o_ref[:, g * HD:(g + 1) * HD] = (part[:, :HD] / part[:, HD:]).astype(o_ref.dtype)


def attend(queries, k_pieces, v_pieces, order, me, chunk, half, after=()):
    pieces = len(k_pieces)
    shard, kv_width = k_pieces[0].shape
    heads = kv_width // HD
    width = queries.shape[1] // heads
    keys = shard * pieces
    rows = width // HD * half
    anywhere = pl.BlockSpec(memory_space=pl.ANY)
    return pl.pallas_call(
        functools.partial(attend_kernel, half, chunk, pieces, heads, len(after)),
        out_shape=jax.ShapeDtypeStruct((half, queries.shape[1]), jnp.bfloat16),
        grid_spec=pltpu.PrefetchScalarGridSpec(
            num_scalar_prefetch=2,
            grid=(heads,),
            in_specs=[anywhere] * (1 + 2 * pieces + len(after)),
            out_specs=pl.BlockSpec((half, width), lambda h, *_: (0, h)),
            scratch_shapes=[
                pltpu.SMEM((order.shape[0],), jnp.int32),
                pltpu.SMEM((1,), jnp.int32),
                pltpu.VMEM((half, heads * width), jnp.bfloat16),
                pltpu.VMEM((keys, kv_width), jnp.bfloat16),
                pltpu.VMEM((keys, kv_width), jnp.bfloat16),
                pltpu.VMEM((keys, 2 * HD), jnp.bfloat16),
                pltpu.VMEM((rows, 2 * HD), jnp.float32),
                pltpu.VMEM((rows, HD), jnp.float32),
                pltpu.VMEM((8, STEP * half), jnp.float32),
                pltpu.SemaphoreType.DMA((2 * pieces + 1,)),
            ],
        ),
        compiler_params=pltpu.CompilerParams(vmem_limit_bytes=40 * MIB),
        cost_estimate=pl.CostEstimate(flops=1, bytes_accessed=0, transcendentals=0),
        name="attend",
    )(order, me, in_hbm(queries), in_hbm(k_pieces[0]), *k_pieces[1:],
      in_hbm(v_pieces[0]), *v_pieces[1:], *after)


def exchange(arrays, axis, bits):
    count = lax.axis_size(axis)
    held = {0: arrays}
    for bit in bits:
        pairs = [(i, i ^ (1 << bit)) for i in range(count)]
        held.update({r ^ (1 << bit): lax.ppermute(a, axis, pairs) for r, a in held.items()})
    return [held[r] for r in range(count)]


def pick(z, options):
    value = jnp.int32(options[-1])
    for i in range(len(options) - 1):
        value = jnp.where(z == i, jnp.int32(options[i]), value)
    return value


def share_kernel(extra, waited, blocks, z_ref, a_ref, w_ref, *refs):
    arrived = refs[:extra]
    out, tiles, sems = refs[extra + waited:]
    count, _, wide = tiles.shape
    block = pick(z_ref[0], blocks)

    @pl.when(block >= 0)
    def _():
        def copy(j):
            place = pl.multiple_of((block * count + j) * wide, wide)
            return pltpu.make_async_copy(w_ref.at[:, pl.ds(place, wide)], tiles.at[j], sems.at[j])

        def column(j, _):
            copy(j).wait()
            lanes = pl.ds(pl.multiple_of(j * wide, wide), wide)
            total = jnp.dot(a_ref[...], tiles[j], preferred_element_type=jnp.float32)
            for ref in arrived:
                total = total + ref[:, lanes].astype(jnp.float32)
            out[:, lanes] = total.astype(out.dtype)
            return 0

        for j in range(count):
            copy(j).start()
        lax.fori_loop(0, count, column, 0)


def share(attended, w_out, arrived, z, blocks, columns, after=(), kind=jnp.bfloat16):
    tok, depth = attended.shape
    wide = min(columns, 256)
    count = columns // wide
    extra = len(arrived)
    whole = pl.BlockSpec(memory_space=pltpu.VMEM)
    anywhere = pl.BlockSpec(memory_space=pl.ANY)
    return pl.pallas_call(
        functools.partial(share_kernel, extra, len(after), blocks),
        out_shape=jax.ShapeDtypeStruct((tok, columns), kind),
        grid_spec=pltpu.PrefetchScalarGridSpec(
            num_scalar_prefetch=1,
            grid=(),
            in_specs=[whole, anywhere] + [whole] * extra + [anywhere] * len(after),
            out_specs=whole,
            scratch_shapes=[
                pltpu.VMEM((count, depth, wide), w_out.dtype),
                pltpu.SemaphoreType.DMA((count,)),
            ],
        ),
        compiler_params=pltpu.CompilerParams(vmem_limit_bytes=40 * MIB),
        cost_estimate=pl.CostEstimate(flops=1, bytes_accessed=0, transcendentals=0),
        name="share",
    )(z, attended, in_hbm(w_out), *arrived, *after)


def finish_kernel(extra, order_ref, me_ref, *refs):
    total = refs[0][...].astype(jnp.float32)
    for ref in refs[1:extra]:
        total = total + ref[...].astype(jnp.float32)
    refs[-1][...] = total.astype(jnp.bfloat16)


def finish(terms, order, me, chunk, whole_tok, out):
    tok, columns = terms[0].shape
    wide = min(columns, 1024)
    operands = list(terms)
    specs = [pl.BlockSpec((tok, wide), lambda j, *_: (0, j))] * len(terms)
    aliases = {}
    if out is not None:
        operands.append(out)
        specs.append(pl.BlockSpec(memory_space=pl.ANY))
        aliases = {1 + len(operands): 0}
    return pl.pallas_call(
        functools.partial(finish_kernel, len(terms)),
        out_shape=jax.ShapeDtypeStruct((whole_tok, columns), jnp.bfloat16),
        grid_spec=pltpu.PrefetchScalarGridSpec(
            num_scalar_prefetch=2,
            grid=(columns // wide,),
            in_specs=specs,
            out_specs=pl.BlockSpec((tok, wide), lambda j, *refs: (block_place(chunk, *refs), j)),
        ),
        input_output_aliases=aliases,
        compiler_params=pltpu.CompilerParams(vmem_limit_bytes=40 * MIB),
        cost_estimate=pl.CostEstimate(flops=1, bytes_accessed=0, transcendentals=0),
        name="finish",
    )(order, me, *operands)


def swap(array, pairs):
    return lax.ppermute(array, "head", pairs)


def line_of_four(attended, w_out, z, order, me, columns, tok):
    outer, inner, back = [(0, 1), (3, 2)], [(1, 2), (2, 1)], [(1, 0), (2, 3)]

    def part(a, arrived, blocks, after=(), kind=jnp.bfloat16):
        return share(a, w_out, arrived, z, blocks, columns, after, kind)

    far_end, near_end, last_end = (3, -1, -1, 0), (2, -1, -1, 1), (1, -1, -1, 2)
    far_on, near_on, home_on, all_own = (-1, 3, 0, -1), (-1, 2, 1, -1), (-1, 0, 3, -1), (0, 1, 2, 3)
    a0 = attended(0, [])
    far0 = part(a0, [], far_end)
    near0 = part(a0, [], near_end, [far0])
    a1 = attended(1, [near0])
    far0, near0 = swap(far0, outer), swap(near0, outer)
    far1 = part(a1, [], far_end)
    mid0 = part(a0, [far0], far_on, [far1])
    near1 = part(a1, [], near_end, [mid0])
    far1, far0 = swap(far1, outer), swap(mid0, inner)
    mid1 = part(a0, [near0], near_on, [near1])
    last0 = part(a0, [], last_end, [mid1])
    last1 = part(a1, [], last_end, [last0])
    near1, near0 = swap(near1, outer), swap(mid1, inner)
    home0 = part(a0, [far0], home_on, [last1])
    last0, last1 = swap(last0, outer), swap(last1, outer)
    mid0 = part(a1, [far1], far_on, [home0])
    home0, far1 = swap(home0, back), swap(mid0, inner)
    own0 = part(a0, [], all_own, [mid0], jnp.float32)
    mid1 = part(a1, [near1], near_on, [own0])
    near1 = swap(mid1, inner)
    own1 = part(a1, [], all_own, [mid1, near0, home0], jnp.float32)
    home1 = swap(part(a1, [far1], home_on, [own1]), back)
    out = finish([own0, near0, last0, home0], order, me, 0, tok, None)
    return finish([own1, near1, last1, home1], order, me, 1, tok, out)


def per_device(queries, keys, values, w_out, order):
    tok = queries.shape[0]
    half = tok // 2
    line = lax.axis_size("head")
    columns = w_out.shape[1] // line
    me = lax.axis_index("blk").astype(jnp.int32).reshape(1)
    z = lax.axis_index("head").astype(jnp.int32).reshape(1)
    bits = list(range(1, lax.axis_size("blk").bit_length() - 1))
    k_pieces = exchange(keys, "blk", bits + [0])
    v_pieces = exchange(values, "blk", bits[::-1] + [0])

    def attended(chunk, after):
        return attend(queries, k_pieces, v_pieces, order, me, chunk, half, after)

    if line == 4:
        return line_of_four(attended, w_out, z, order, me, columns, tok)
    outs = []
    for c in range(2):
        sums = jnp.dot(attended(c, []), w_out, preferred_element_type=jnp.float32)
        outs.append(lax.psum_scatter(
            sums.astype(jnp.bfloat16), "head", scatter_dimension=1, tiled=True))
    swapped = block_place(0, order, me) == 1
    outs = [jnp.where(swapped, outs[1 - c], outs[c]) for c in range(2)]
    return jnp.concatenate(outs, axis=0)


def solution(mesh):
    return jax.shard_map(
        per_device,
        mesh=mesh,
        in_specs=(P("blk", "head"), P("blk", "head"), P("blk", "head"), P("head", None), P()),
        out_specs=P("blk", "head"),
        check_vma=False,
    )
```

```python
import functools
import math

import jax
import jax.numpy as jnp
from jax import lax
from jax.experimental import pallas as pl
from jax.experimental.pallas import tpu as pltpu
from jax.sharding import PartitionSpec as P

HD = 128
NT = (((1,), (1,)), ((), ()))
MIB = 2 ** 20
STEP = 4
LIMIT = 64.0
JOINT = 4


def in_hbm(array):
    return pltpu.with_memory_space_constraint(array, pltpu.HBM)


def block_place(chunk, order_ref, me_ref):
    own = 2 * me_ref[0]
    return jnp.where(order_ref[own] > order_ref[own + 1], 1 - chunk, chunk)


def attend_kernel(half, chunk, pieces, heads, waited, order_ref, me_ref, q_ref, *refs):
    k_refs, v_refs = refs[:pieces], refs[pieces:2 * pieces]
    o_ref, inv, q_all, k_all, v_all, v_wide, acc, top, above, sems = refs[2 * pieces + waited:]
    blocks = order_ref.shape[0]
    per = blocks // pieces
    tile = half
    width = o_ref.shape[1]
    group = width // HD
    joint = math.gcd(group, JOINT)
    shard = per * half
    factor = HD ** (-0.5) * math.log2(math.e)
    own = block_place(chunk, order_ref, me_ref)
    me = me_ref[0]
    head = pl.program_id(0)
    lanes = pl.ds(pl.multiple_of(head * HD, HD), HD)

    def copies():
        mine = pl.ds(pl.multiple_of(own * half, half), half)
        pairs = [(q_ref.at[mine, :], q_all)]
        for r in range(pieces):
            here = pl.ds(r * shard, shard)
            pairs += [(k_refs[r], k_all.at[here, :]), (v_refs[r], v_all.at[here, :])]
        return [pltpu.make_async_copy(src, dst, sems.at[i]) for i, (src, dst) in enumerate(pairs)]

    @pl.when(head == 0)
    def _():
        for copy in copies():
            copy.start()

        def invert(b, _):
            inv[order_ref[b]] = jnp.bitwise_xor(b // per, me) * per + lax.rem(b, per)
            return 0

        lax.fori_loop(0, blocks, invert, 0)
        v_wide[:, HD:] = jnp.ones((v_wide.shape[0], HD), v_wide.dtype)
        for copy in copies()[:3]:
            copy.wait()

    v_wide[:shard, :HD] = v_all[:shard, lanes]
    earlier = order_ref[me * per + own]

    def keys_of(blocks_in):
        rows = [pl.ds(pl.multiple_of(b * half, half), half) for b in blocks_in]
        return (jnp.concatenate([k_all[r, lanes] for r in rows], axis=0),
                jnp.concatenate([v_wide[r, :] for r in rows], axis=0))

    def over_tiles(k_cat, use):
        def scores(g):
            q_cat = jnp.concatenate([
                q_all[:, pl.ds(pl.multiple_of(head * width + i * HD, HD), HD)]
                for i in range(g, g + joint)], axis=0)
            return lax.dot_general(q_cat, k_cat, NT, preferred_element_type=jnp.float32)

        score = scores(0)
        for g in range(0, group, joint):
            ahead = scores(g + joint) if g + joint < group else None
            use(pl.ds(g * tile, joint * tile), score)
            score = ahead

    def diagonal():
        k_cat, v_cat = keys_of([own])
        query = lax.rem(lax.broadcasted_iota(jnp.int32, (joint * tile, half), 0), tile)
        seen = lax.broadcasted_iota(jnp.int32, (joint * tile, half), 1) <= query

        def use(rows, score):
            score = jnp.where(seen, score, -1e30)
            peak = jnp.max(score, axis=1, keepdims=True)
            weight = jnp.exp2((score - peak) * factor)
            top[rows, :] = jnp.broadcast_to(peak, (joint * tile, HD))
            acc[rows, :] = jnp.dot(weight.astype(jnp.bfloat16), v_cat,
                                   preferred_element_type=jnp.float32)

        over_tiles(k_cat, use)

    def wide(array, count):
        return jnp.concatenate([array] * (count * half // HD), axis=1)

    def step(places):
        k_cat, v_cat = keys_of(places)
        count = len(places)

        def use(rows, score):
            power = (score - wide(top[rows, :], count)) * factor
            across = pl.ds(0, count * half)
            above[:, across] = jnp.maximum(
                above[:, across], jnp.max(power.reshape(-1, 8, power.shape[1]), axis=0))
            acc[rows, :] = acc[rows, :] + jnp.dot(
                jnp.exp2(power).astype(jnp.bfloat16), v_cat, preferred_element_type=jnp.float32)

        over_tiles(k_cat, use)

    def full_step(n, _):
        step([inv[STEP * n + i] for i in range(STEP)])
        return 0

    def careful_step(n, _):
        k_cat, v_cat = keys_of([inv[n]])

        def one(g, _):
            at = pl.ds(pl.multiple_of(head * width + g * HD, HD), HD)
            rows = pl.ds(pl.multiple_of(g * tile, tile), tile)
            score = lax.dot_general(q_all[:, at], k_cat, NT, preferred_element_type=jnp.float32)
            old = top[rows, :]
            peak = jnp.maximum(old, jnp.max(score, axis=1, keepdims=True))
            top[rows, :] = peak
            weight = jnp.exp2((score - wide(peak, 1)) * factor)
            shrink = jnp.exp2((old - peak) * factor)
            acc[rows, :] = acc[rows, :] * jnp.concatenate([shrink, shrink], axis=1) + jnp.dot(
                weight.astype(jnp.bfloat16), v_cat, preferred_element_type=jnp.float32)
            return 0

        lax.fori_loop(0, group, one, 0)
        return 0

    diagonal()

    @pl.when(head == 0)
    def _():
        for copy in copies()[3:]:
            copy.wait()

    v_wide[shard:, :HD] = v_all[shard:, lanes]
    above[...] = jnp.zeros_like(above)
    lax.fori_loop(0, earlier // STEP, full_step, 0)
    for rest in range(1, STEP):
        @pl.when(lax.rem(earlier, STEP) == rest)
        def _():
            step([inv[earlier - rest + i] for i in range(rest)])

    @pl.when(jnp.max(above[...]) > LIMIT)
    def _():
        diagonal()
        lax.fori_loop(0, earlier, careful_step, 0)

    for g in range(group):
        part = acc[g * tile:(g + 1) * tile, :]
        o_ref[:, g * HD:(g + 1) * HD] = (part[:, :HD] / part[:, HD:]).astype(o_ref.dtype)


def attend(queries, k_pieces, v_pieces, order, me, chunk, half, after=()):
    pieces = len(k_pieces)
    shard, kv_width = k_pieces[0].shape
    heads = kv_width // HD
    width = queries.shape[1] // heads
    keys = shard * pieces
    rows = width // HD * half
    anywhere = pl.BlockSpec(memory_space=pl.ANY)
    return pl.pallas_call(
        functools.partial(attend_kernel, half, chunk, pieces, heads, len(after)),
        out_shape=jax.ShapeDtypeStruct((half, queries.shape[1]), jnp.bfloat16),
        grid_spec=pltpu.PrefetchScalarGridSpec(
            num_scalar_prefetch=2,
            grid=(heads,),
            in_specs=[anywhere] * (1 + 2 * pieces + len(after)),
            out_specs=pl.BlockSpec((half, width), lambda h, *_: (0, h)),
            scratch_shapes=[
                pltpu.SMEM((order.shape[0],), jnp.int32),
                pltpu.VMEM((half, heads * width), jnp.bfloat16),
                pltpu.VMEM((keys, kv_width), jnp.bfloat16),
                pltpu.VMEM((keys, kv_width), jnp.bfloat16),
                pltpu.VMEM((keys, 2 * HD), jnp.bfloat16),
                pltpu.VMEM((rows, 2 * HD), jnp.float32),
                pltpu.VMEM((rows, HD), jnp.float32),
                pltpu.VMEM((8, STEP * half), jnp.float32),
                pltpu.SemaphoreType.DMA((2 * pieces + 1,)),
            ],
        ),
        compiler_params=pltpu.CompilerParams(vmem_limit_bytes=40 * MIB),
        cost_estimate=pl.CostEstimate(flops=1, bytes_accessed=0, transcendentals=0),
        name="attend",
    )(order, me, in_hbm(queries), in_hbm(k_pieces[0]), *k_pieces[1:],
      in_hbm(v_pieces[0]), *v_pieces[1:], *after)


def hold_kernel(count, *refs):
    outs, sems = refs[-count - 1:-1], refs[-1]
    copies = [pltpu.make_async_copy(refs[i], outs[i], sems.at[i]) for i in range(count)]
    for copy in copies:
        copy.start()
    for copy in copies:
        copy.wait()


def hold(arrays, until):
    count = len(arrays)
    anywhere = pl.BlockSpec(memory_space=pl.ANY)
    return pl.pallas_call(
        functools.partial(hold_kernel, count),
        out_shape=[jax.ShapeDtypeStruct(a.shape, a.dtype) for a in arrays],
        in_specs=[anywhere] * (count + len(until)),
        out_specs=[pl.BlockSpec(memory_space=pltpu.VMEM)] * count,
        scratch_shapes=[pltpu.SemaphoreType.DMA((count,))],
        compiler_params=pltpu.CompilerParams(vmem_limit_bytes=40 * MIB),
        cost_estimate=pl.CostEstimate(flops=1, bytes_accessed=0, transcendentals=0),
        name="hold",
    )(*[in_hbm(a) for a in arrays], *until)


def gather(keys, values, axis):
    count = lax.axis_size(axis)

    def spread(held, bit):
        pairs = [(i, i ^ (1 << bit)) for i in range(count)]
        return {r ^ (1 << bit): lax.ppermute(a, axis, pairs) for r, a in held.items()}

    bits = list(range(1, count.bit_length() - 1))
    k_held, v_held = {0: keys}, {0: values}
    for k_bit, v_bit in zip(bits, bits[::-1]):
        k_held.update(spread(k_held, k_bit))
        v_held.update(spread(v_held, v_bit))
    until = [k_held[1 << bits[0]], v_held[1 << bits[-1]]]
    k_own, v_own = hold([keys, values], until)
    k_held.update(spread({**k_held, 0: k_own}, 0))
    v_held.update(spread({**v_held, 0: v_own}, 0))
    return [k_held[r] for r in range(count)], [v_held[r] for r in range(count)]


def pick(z, options):
    value = jnp.int32(options[-1])
    for i in range(len(options) - 1):
        value = jnp.where(z == i, jnp.int32(options[i]), value)
    return value


def share_kernel(extra, waited, blocks, z_ref, a_ref, w_ref, *refs):
    arrived = refs[:extra]
    out, tiles, sems = refs[extra + waited:]
    count, _, wide = tiles.shape
    block = pick(z_ref[0], blocks)

    @pl.when(block >= 0)
    def _():
        def copy(j):
            place = pl.multiple_of((block * count + j) * wide, wide)
            return pltpu.make_async_copy(w_ref.at[:, pl.ds(place, wide)], tiles.at[j], sems.at[j])

        def column(j, _):
            copy(j).wait()
            lanes = pl.ds(pl.multiple_of(j * wide, wide), wide)
            total = jnp.dot(a_ref[...], tiles[j], preferred_element_type=jnp.float32)
            for ref in arrived:
                total = total + ref[:, lanes].astype(jnp.float32)
            out[:, lanes] = total.astype(out.dtype)
            return 0

        for j in range(count):
            copy(j).start()
        lax.fori_loop(0, count, column, 0)


def share(attended, w_out, arrived, z, blocks, columns, after=(), kind=jnp.bfloat16):
    tok, depth = attended.shape
    wide = min(columns, 256)
    count = columns // wide
    extra = len(arrived)
    whole = pl.BlockSpec(memory_space=pltpu.VMEM)
    anywhere = pl.BlockSpec(memory_space=pl.ANY)
    return pl.pallas_call(
        functools.partial(share_kernel, extra, len(after), blocks),
        out_shape=jax.ShapeDtypeStruct((tok, columns), kind),
        grid_spec=pltpu.PrefetchScalarGridSpec(
            num_scalar_prefetch=1,
            grid=(),
            in_specs=[whole, anywhere] + [whole] * extra + [anywhere] * len(after),
            out_specs=whole,
            scratch_shapes=[
                pltpu.VMEM((count, depth, wide), w_out.dtype),
                pltpu.SemaphoreType.DMA((count,)),
            ],
        ),
        compiler_params=pltpu.CompilerParams(vmem_limit_bytes=40 * MIB),
        cost_estimate=pl.CostEstimate(flops=1, bytes_accessed=0, transcendentals=0),
        name="share",
    )(z, attended, in_hbm(w_out), *arrived, *after)


def finish_kernel(extra, chunk, order_ref, me_ref, *refs):
    out, summed, sem = refs[-3:]
    total = refs[0][...].astype(jnp.float32)
    for ref in refs[1:extra]:
        total = total + ref[...].astype(jnp.float32)
    summed[...] = total.astype(summed.dtype)
    tok = summed.shape[0]
    first = pl.multiple_of(block_place(chunk, order_ref, me_ref) * tok, tok)
    copy = pltpu.make_async_copy(summed, out.at[pl.ds(first, tok), :], sem)
    copy.start()
    copy.wait()


def finish(terms, order, me, chunk, whole_tok, out):
    tok, columns = terms[0].shape
    anywhere = pl.BlockSpec(memory_space=pl.ANY)
    before = [] if out is None else [out]
    return pl.pallas_call(
        functools.partial(finish_kernel, len(terms), chunk),
        out_shape=jax.ShapeDtypeStruct((whole_tok, columns), jnp.bfloat16),
        grid_spec=pltpu.PrefetchScalarGridSpec(
            num_scalar_prefetch=2,
            grid=(),
            in_specs=[pl.BlockSpec(memory_space=pltpu.VMEM)] * len(terms)
            + [anywhere] * len(before),
            out_specs=anywhere,
            scratch_shapes=[pltpu.VMEM((tok, columns), jnp.bfloat16), pltpu.SemaphoreType.DMA],
        ),
        input_output_aliases={2 + len(terms): 0} if before else {},
        compiler_params=pltpu.CompilerParams(vmem_limit_bytes=40 * MIB),
        cost_estimate=pl.CostEstimate(flops=1, bytes_accessed=0, transcendentals=0),
        name="finish",
    )(order, me, *terms, *before)


def swap(array, pairs):
    return lax.ppermute(array, "head", pairs)


def line_of_four(attended, w_out, z, order, me, columns, tok):
    outer, inner, back = [(0, 1), (3, 2)], [(1, 2), (2, 1)], [(1, 0), (2, 3)]

    def part(a, arrived, blocks, after=(), kind=jnp.bfloat16):
        return share(a, w_out, arrived, z, blocks, columns, after, kind)

    far_end, near_end, last_end = (3, -1, -1, 0), (2, -1, -1, 1), (1, -1, -1, 2)
    far_on, near_on, home_on, all_own = (-1, 3, 0, -1), (-1, 2, 1, -1), (-1, 0, 3, -1), (0, 1, 2, 3)
    a0 = attended(0, [])
    far0 = part(a0, [], far_end)
    near0 = part(a0, [], near_end, [far0])
    a1 = attended(1, [near0])
    far0, near0 = swap(far0, outer), swap(near0, outer)
    far1 = part(a1, [], far_end)
    mid0 = part(a0, [far0], far_on, [far1])
    near1 = part(a1, [], near_end, [mid0])
    far1, far0 = swap(far1, outer), swap(mid0, inner)
    mid1 = part(a0, [near0], near_on, [near1])
    last0 = part(a0, [], last_end, [mid1])
    last1 = part(a1, [], last_end, [last0])
    near1, near0 = swap(near1, outer), swap(mid1, inner)
    home0 = part(a0, [far0], home_on, [last1])
    last0, last1 = swap(last0, outer), swap(last1, outer)
    mid0 = part(a1, [far1], far_on, [home0])
    home0, far1 = swap(home0, back), swap(mid0, inner)
    own0 = part(a0, [], all_own, [mid0], jnp.float32)
    mid1 = part(a1, [near1], near_on, [own0])
    near1 = swap(mid1, inner)
    own1 = part(a1, [], all_own, [mid1, near0, home0], jnp.float32)
    home1 = swap(part(a1, [far1], home_on, [own1]), back)
    out = finish([own0, near0, last0, home0], order, me, 0, tok, None)
    return finish([own1, near1, last1, home1], order, me, 1, tok, out)


def per_device(queries, keys, values, w_out, order):
    tok = queries.shape[0]
    half = tok // 2
    line = lax.axis_size("head")
    columns = w_out.shape[1] // line
    me = lax.axis_index("blk").astype(jnp.int32).reshape(1)
    z = lax.axis_index("head").astype(jnp.int32).reshape(1)
    k_pieces, v_pieces = gather(keys, values, "blk")

    def attended(chunk, after):
        return attend(queries, k_pieces, v_pieces, order, me, chunk, half, after)

    if line == 4:
        return line_of_four(attended, w_out, z, order, me, columns, tok)
    outs = []
    for c in range(2):
        sums = jnp.dot(attended(c, []), w_out, preferred_element_type=jnp.float32)
        outs.append(lax.psum_scatter(
            sums.astype(jnp.bfloat16), "head", scatter_dimension=1, tiled=True))
    swapped = block_place(0, order, me) == 1
    outs = [jnp.where(swapped, outs[1 - c], outs[c]) for c in range(2)]
    return jnp.concatenate(outs, axis=0)


def solution(mesh):
    return jax.shard_map(
        per_device,
        mesh=mesh,
        in_specs=(P("blk", "head"), P("blk", "head"), P("blk", "head"), P("head", None), P()),
        out_specs=P("blk", "head"),
        check_vma=False,
    )
```

```python
import functools
import math

import jax
import jax.numpy as jnp
from jax import lax
from jax.experimental import pallas as pl
from jax.experimental.pallas import tpu as pltpu
from jax.sharding import PartitionSpec as P

HD = 128
NT = (((1,), (1,)), ((), ()))
MIB = 2 ** 20
STEP = 4
LIMIT = 64.0
JOINT = 4


def in_hbm(array):
    return pltpu.with_memory_space_constraint(array, pltpu.HBM)


def block_place(chunk, order_ref, me_ref):
    own = 2 * me_ref[0]
    return jnp.where(order_ref[own] > order_ref[own + 1], 1 - chunk, chunk)


def attend_kernel(half, chunk, pieces, heads, waited, order_ref, me_ref, q_ref, *refs):
    k_refs, v_refs = refs[:pieces], refs[pieces:2 * pieces]
    o_ref, inv, q_all, k_all, v_all, v_wide, acc, top, above, sems = refs[2 * pieces + waited:]
    blocks = order_ref.shape[0]
    per = blocks // pieces
    tile = half
    width = o_ref.shape[1]
    group = width // HD
    joint = math.gcd(group, JOINT)
    shard = per * half
    factor = HD ** (-0.5) * math.log2(math.e)
    own = block_place(chunk, order_ref, me_ref)
    me = me_ref[0]
    head = pl.program_id(0)
    lanes = pl.ds(pl.multiple_of(head * HD, HD), HD)

    def copies():
        mine = pl.ds(pl.multiple_of(own * half, half), half)
        pairs = [(q_ref.at[mine, :], q_all)]
        for r in range(pieces):
            here = pl.ds(r * shard, shard)
            pairs += [(k_refs[r], k_all.at[here, :]), (v_refs[r], v_all.at[here, :])]
        return [pltpu.make_async_copy(src, dst, sems.at[i]) for i, (src, dst) in enumerate(pairs)]

    @pl.when(head == 0)
    def _():
        for copy in copies():
            copy.start()

        def invert(b, _):
            inv[order_ref[b]] = jnp.bitwise_xor(b // per, me) * per + lax.rem(b, per)
            return 0

        lax.fori_loop(0, blocks, invert, 0)
        v_wide[:, HD:] = jnp.ones((v_wide.shape[0], HD), v_wide.dtype)
        for copy in copies()[:3]:
            copy.wait()

    v_wide[:shard, :HD] = v_all[:shard, lanes]
    earlier = order_ref[me * per + own]

    def keys_of(blocks_in):
        rows = [pl.ds(pl.multiple_of(b * half, half), half) for b in blocks_in]
        return (jnp.concatenate([k_all[r, lanes] for r in rows], axis=0),
                jnp.concatenate([v_wide[r, :] for r in rows], axis=0))

    def over_tiles(k_cat, use):
        def scores(g):
            q_cat = jnp.concatenate([
                q_all[:, pl.ds(pl.multiple_of(head * width + i * HD, HD), HD)]
                for i in range(g, g + joint)], axis=0)
            return lax.dot_general(q_cat, k_cat, NT, preferred_element_type=jnp.float32)

        score = scores(0)
        for g in range(0, group, joint):
            ahead = scores(g + joint) if g + joint < group else None
            use(pl.ds(g * tile, joint * tile), score)
            score = ahead

    def diagonal():
        k_cat, v_cat = keys_of([own])
        query = lax.rem(lax.broadcasted_iota(jnp.int32, (joint * tile, half), 0), tile)
        seen = lax.broadcasted_iota(jnp.int32, (joint * tile, half), 1) <= query

        def use(rows, score):
            score = jnp.where(seen, score, -1e30)
            peak = jnp.max(score, axis=1, keepdims=True)
            weight = jnp.exp2((score - peak) * factor)
            top[rows, :] = jnp.broadcast_to(peak, (joint * tile, HD))
            acc[rows, :] = jnp.dot(weight.astype(jnp.bfloat16), v_cat,
                                   preferred_element_type=jnp.float32)

        over_tiles(k_cat, use)

    def wide(array, count):
        return jnp.concatenate([array] * (count * half // HD), axis=1)

    def step(places):
        k_cat, v_cat = keys_of(places)
        count = len(places)

        def use(rows, score):
            power = (score - wide(top[rows, :], count)) * factor
            across = pl.ds(0, count * half)
            above[:, across] = jnp.maximum(
                above[:, across], jnp.max(power.reshape(-1, 8, power.shape[1]), axis=0))
            acc[rows, :] = acc[rows, :] + jnp.dot(
                jnp.exp2(power).astype(jnp.bfloat16), v_cat, preferred_element_type=jnp.float32)

        over_tiles(k_cat, use)

    def full_step(n, _):
        step([inv[STEP * n + i] for i in range(STEP)])
        return 0

    def careful_step(n, _):
        k_cat, v_cat = keys_of([inv[n]])

        def one(g, _):
            at = pl.ds(pl.multiple_of(head * width + g * HD, HD), HD)
            rows = pl.ds(pl.multiple_of(g * tile, tile), tile)
            score = lax.dot_general(q_all[:, at], k_cat, NT, preferred_element_type=jnp.float32)
            old = top[rows, :]
            peak = jnp.maximum(old, jnp.max(score, axis=1, keepdims=True))
            top[rows, :] = peak
            weight = jnp.exp2((score - wide(peak, 1)) * factor)
            shrink = jnp.exp2((old - peak) * factor)
            acc[rows, :] = acc[rows, :] * jnp.concatenate([shrink, shrink], axis=1) + jnp.dot(
                weight.astype(jnp.bfloat16), v_cat, preferred_element_type=jnp.float32)
            return 0

        lax.fori_loop(0, group, one, 0)
        return 0

    diagonal()

    @pl.when(head == 0)
    def _():
        for copy in copies()[3:]:
            copy.wait()

    v_wide[shard:, :HD] = v_all[shard:, lanes]
    above[...] = jnp.zeros_like(above)
    lax.fori_loop(0, earlier // STEP, full_step, 0)
    for rest in range(1, STEP):
        @pl.when(lax.rem(earlier, STEP) == rest)
        def _():
            step([inv[earlier - rest + i] for i in range(rest)])

    @pl.when(jnp.max(above[...]) > LIMIT)
    def _():
        diagonal()
        lax.fori_loop(0, earlier, careful_step, 0)

    for g in range(group):
        part = acc[g * tile:(g + 1) * tile, :]
        o_ref[:, g * HD:(g + 1) * HD] = (part[:, :HD] / part[:, HD:]).astype(o_ref.dtype)


def attend(queries, k_pieces, v_pieces, order, me, chunk, half, after=()):
    pieces = len(k_pieces)
    shard, kv_width = k_pieces[0].shape
    heads = kv_width // HD
    width = queries.shape[1] // heads
    keys = shard * pieces
    rows = width // HD * half
    anywhere = pl.BlockSpec(memory_space=pl.ANY)
    return pl.pallas_call(
        functools.partial(attend_kernel, half, chunk, pieces, heads, len(after)),
        out_shape=jax.ShapeDtypeStruct((half, queries.shape[1]), jnp.bfloat16),
        grid_spec=pltpu.PrefetchScalarGridSpec(
            num_scalar_prefetch=2,
            grid=(heads,),
            in_specs=[anywhere] * (1 + 2 * pieces + len(after)),
            out_specs=pl.BlockSpec((half, width), lambda h, *_: (0, h)),
            scratch_shapes=[
                pltpu.SMEM((order.shape[0],), jnp.int32),
                pltpu.VMEM((half, heads * width), jnp.bfloat16),
                pltpu.VMEM((keys, kv_width), jnp.bfloat16),
                pltpu.VMEM((keys, kv_width), jnp.bfloat16),
                pltpu.VMEM((keys, 2 * HD), jnp.bfloat16),
                pltpu.VMEM((rows, 2 * HD), jnp.float32),
                pltpu.VMEM((rows, HD), jnp.float32),
                pltpu.VMEM((8, STEP * half), jnp.float32),
                pltpu.SemaphoreType.DMA((2 * pieces + 1,)),
            ],
        ),
        compiler_params=pltpu.CompilerParams(vmem_limit_bytes=40 * MIB),
        cost_estimate=pl.CostEstimate(flops=1, bytes_accessed=0, transcendentals=0),
        name="attend",
    )(order, me, in_hbm(queries), in_hbm(k_pieces[0]), *k_pieces[1:],
      in_hbm(v_pieces[0]), *v_pieces[1:], *after)


def hold_kernel(count, *refs):
    outs, sems = refs[-count - 1:-1], refs[-1]
    copies = [pltpu.make_async_copy(refs[i], outs[i], sems.at[i]) for i in range(count)]
    for copy in copies:
        copy.start()
    for copy in copies:
        copy.wait()


def hold(arrays, until):
    count = len(arrays)
    anywhere = pl.BlockSpec(memory_space=pl.ANY)
    return pl.pallas_call(
        functools.partial(hold_kernel, count),
        out_shape=[jax.ShapeDtypeStruct(a.shape, a.dtype) for a in arrays],
        in_specs=[anywhere] * (count + len(until)),
        out_specs=[pl.BlockSpec(memory_space=pltpu.VMEM)] * count,
        scratch_shapes=[pltpu.SemaphoreType.DMA((count,))],
        compiler_params=pltpu.CompilerParams(vmem_limit_bytes=40 * MIB),
        cost_estimate=pl.CostEstimate(flops=1, bytes_accessed=0, transcendentals=0),
        name="hold",
    )(*[in_hbm(a) for a in arrays], *until)


def gather(keys, values, axis):
    count = lax.axis_size(axis)

    def spread(held, bit):
        pairs = [(i, i ^ (1 << bit)) for i in range(count)]
        return {r ^ (1 << bit): lax.ppermute(a, axis, pairs) for r, a in held.items()}

    bits = list(range(1, count.bit_length() - 1))
    k_held, v_held = {0: keys}, {0: values}
    for k_bit, v_bit in zip(bits, bits[::-1]):
        k_held.update(spread(k_held, k_bit))
        v_held.update(spread(v_held, v_bit))
    until = [k_held[1 << bits[0]], v_held[1 << bits[-1]]]
    k_own, v_own = hold([keys, values], until)
    k_held.update(spread({**k_held, 0: k_own}, 0))
    v_held.update(spread({**v_held, 0: v_own}, 0))
    return [k_held[r] for r in range(count)], [v_held[r] for r in range(count)]


def pick(z, options):
    value = jnp.int32(options[-1])
    for i in range(len(options) - 1):
        value = jnp.where(z == i, jnp.int32(options[i]), value)
    return value


def share_kernel(roles, waited, z_ref, w_ref, *refs):
    operands = sum(1 + extra for _, extra in roles)
    out, tiles, sems = refs[operands + waited:]
    count, _, wide = tiles.shape
    for blocks, extra in roles:
        a_ref, arrived, refs = refs[0], refs[1:1 + extra], refs[1 + extra:]
        block = pick(z_ref[0], blocks)

        @pl.when(block >= 0)
        def _(block=block, a_ref=a_ref, arrived=arrived):
            def copy(j):
                place = pl.multiple_of((block * count + j) * wide, wide)
                return pltpu.make_async_copy(
                    w_ref.at[:, pl.ds(place, wide)], tiles.at[j], sems.at[j])

            def column(j, _):
                copy(j).wait()
                lanes = pl.ds(pl.multiple_of(j * wide, wide), wide)
                total = jnp.dot(a_ref[...], tiles[j], preferred_element_type=jnp.float32)
                for ref in arrived:
                    total = total + ref[:, lanes].astype(jnp.float32)
                out[:, lanes] = total.astype(out.dtype)
                return 0

            for j in range(count):
                copy(j).start()
            lax.fori_loop(0, count, column, 0)


def share(roles, w_out, z, columns, after=()):
    tok, depth = roles[0][1].shape
    wide = min(columns, 256)
    count = columns // wide
    whole = pl.BlockSpec(memory_space=pltpu.VMEM)
    anywhere = pl.BlockSpec(memory_space=pl.ANY)
    operands = [a for _, attended, arrived in roles for a in (attended, *arrived)]
    return pl.pallas_call(
        functools.partial(share_kernel, [(b, len(arrived)) for b, _, arrived in roles], len(after)),
        out_shape=jax.ShapeDtypeStruct((tok, columns), jnp.bfloat16),
        grid_spec=pltpu.PrefetchScalarGridSpec(
            num_scalar_prefetch=1,
            grid=(),
            in_specs=[anywhere] + [whole] * len(operands) + [anywhere] * len(after),
            out_specs=whole,
            scratch_shapes=[
                pltpu.VMEM((count, depth, wide), w_out.dtype),
                pltpu.SemaphoreType.DMA((count,)),
            ],
        ),
        compiler_params=pltpu.CompilerParams(vmem_limit_bytes=40 * MIB),
        cost_estimate=pl.CostEstimate(flops=1, bytes_accessed=0, transcendentals=0),
        name="share",
    )(z, in_hbm(w_out), *operands, *after)


def own_kernel(chunks, waited, z_ref, w_ref, *refs):
    a_refs, outs, (tiles, sems) = refs[:chunks], refs[chunks + waited:-2], refs[-2:]
    count, _, wide = tiles.shape

    def copy(j):
        place = pl.multiple_of((z_ref[0] * count + j) * wide, wide)
        return pltpu.make_async_copy(w_ref.at[:, pl.ds(place, wide)], tiles.at[j], sems.at[j])

    def column(j, _):
        copy(j).wait()
        lanes = pl.ds(pl.multiple_of(j * wide, wide), wide)
        rows = jnp.concatenate([ref[...] for ref in a_refs], axis=0)
        total = jnp.dot(rows, tiles[j], preferred_element_type=jnp.float32)
        tok = outs[0].shape[0]
        for i, out in enumerate(outs):
            out[:, lanes] = total[i * tok:(i + 1) * tok]
        return 0

    for j in range(count):
        copy(j).start()
    lax.fori_loop(0, count, column, 0)


def own_columns(chunks, w_out, z, columns, after):
    tok, depth = chunks[0].shape
    wide = min(columns, 256)
    count = columns // wide
    whole = pl.BlockSpec(memory_space=pltpu.VMEM)
    anywhere = pl.BlockSpec(memory_space=pl.ANY)
    return pl.pallas_call(
        functools.partial(own_kernel, len(chunks), len(after)),
        out_shape=[jax.ShapeDtypeStruct((tok, columns), jnp.float32)] * len(chunks),
        grid_spec=pltpu.PrefetchScalarGridSpec(
            num_scalar_prefetch=1,
            grid=(),
            in_specs=[anywhere] + [whole] * len(chunks) + [anywhere] * len(after),
            out_specs=[whole] * len(chunks),
            scratch_shapes=[
                pltpu.VMEM((count, depth, wide), w_out.dtype),
                pltpu.SemaphoreType.DMA((count,)),
            ],
        ),
        compiler_params=pltpu.CompilerParams(vmem_limit_bytes=40 * MIB),
        cost_estimate=pl.CostEstimate(flops=1, bytes_accessed=0, transcendentals=0),
        name="own",
    )(z, in_hbm(w_out), *chunks, *after)


def finish_kernel(extra, chunk, order_ref, me_ref, *refs):
    out, summed, sem = refs[-3:]
    total = refs[0][...].astype(jnp.float32)
    for ref in refs[1:extra]:
        total = total + ref[...].astype(jnp.float32)
    summed[...] = total.astype(summed.dtype)
    tok = summed.shape[0]
    first = pl.multiple_of(block_place(chunk, order_ref, me_ref) * tok, tok)
    copy = pltpu.make_async_copy(summed, out.at[pl.ds(first, tok), :], sem)
    copy.start()
    copy.wait()


def finish(terms, order, me, chunk, whole_tok, out, after=()):
    tok, columns = terms[0].shape
    anywhere = pl.BlockSpec(memory_space=pl.ANY)
    before = [] if out is None else [out]
    return pl.pallas_call(
        functools.partial(finish_kernel, len(terms), chunk),
        out_shape=jax.ShapeDtypeStruct((whole_tok, columns), jnp.bfloat16),
        grid_spec=pltpu.PrefetchScalarGridSpec(
            num_scalar_prefetch=2,
            grid=(),
            in_specs=[pl.BlockSpec(memory_space=pltpu.VMEM)] * len(terms)
            + [anywhere] * len(before + list(after)),
            out_specs=anywhere,
            scratch_shapes=[pltpu.VMEM((tok, columns), jnp.bfloat16), pltpu.SemaphoreType.DMA],
        ),
        input_output_aliases={2 + len(terms): 0} if before else {},
        compiler_params=pltpu.CompilerParams(vmem_limit_bytes=40 * MIB),
        cost_estimate=pl.CostEstimate(flops=1, bytes_accessed=0, transcendentals=0),
        name="finish",
    )(order, me, *terms, *before, *after)


def swap(array, pairs):
    return lax.ppermute(array, "head", pairs)


def line_of_four(attended, w_out, z, order, me, columns, tok):
    outer, inner, back = [(0, 1), (3, 2)], [(1, 2), (2, 1)], [(1, 0), (2, 3)]
    far_end, near_end, last_end = (3, -1, -1, 0), (2, -1, -1, 1), (1, -1, -1, 2)
    far_on, near_on, home_on = (-1, 3, 0, -1), (-1, 2, 1, -1), (-1, 0, 3, -1)

    def part(roles, after=()):
        return share(roles, w_out, z, columns, after)

    a0 = attended(0, [])
    far_0 = part([(far_end, a0, [])])
    near_0 = part([(near_end, a0, [])], [far_0])
    a1 = attended(1, [near_0])
    far_0, near_0 = swap(far_0, outer), swap(near_0, outer)
    step = part([(far_end, a1, []), (far_on, a0, [far_0])])
    far_1, far_0 = swap(step, outer), swap(step, inner)
    step = part([(near_end, a1, []), (near_on, a0, [near_0])], [step])
    near_1, near_0 = swap(step, outer), swap(step, inner)
    own = own_columns([a0, a1], w_out, z, columns, [step])
    step = part([(last_end, a0, []), (home_on, a0, [far_0])], own[:1])
    edge_0 = swap(step, outer + back)
    step = part([(last_end, a1, []), (far_on, a1, [far_1])], [step])
    last_1, far_1 = swap(step, outer), swap(step, inner)
    step = part([(near_on, a1, [near_1])], [step, near_0])
    near_1 = swap(step, inner)
    step = part([(home_on, a1, [far_1])], [step])
    home_1 = swap(step, back)
    out = finish([own[0], near_0, edge_0], order, me, 0, tok, None, [step])
    return finish([own[1], near_1, last_1, home_1], order, me, 1, tok, out)


def per_device(queries, keys, values, w_out, order):
    tok = queries.shape[0]
    half = tok // 2
    line = lax.axis_size("head")
    columns = w_out.shape[1] // line
    me = lax.axis_index("blk").astype(jnp.int32).reshape(1)
    z = lax.axis_index("head").astype(jnp.int32).reshape(1)
    k_pieces, v_pieces = gather(keys, values, "blk")

    def attended(chunk, after):
        return attend(queries, k_pieces, v_pieces, order, me, chunk, half, after)

    if line == 4:
        return line_of_four(attended, w_out, z, order, me, columns, tok)
    outs = []
    for c in range(2):
        sums = jnp.dot(attended(c, []), w_out, preferred_element_type=jnp.float32)
        outs.append(lax.psum_scatter(
            sums.astype(jnp.bfloat16), "head", scatter_dimension=1, tiled=True))
    swapped = block_place(0, order, me) == 1
    outs = [jnp.where(swapped, outs[1 - c], outs[c]) for c in range(2)]
    return jnp.concatenate(outs, axis=0)


def solution(mesh):
    return jax.shard_map(
        per_device,
        mesh=mesh,
        in_specs=(P("blk", "head"), P("blk", "head"), P("blk", "head"), P("head", None), P()),
        out_specs=P("blk", "head"),
        check_vma=False,
    )
```

```python
import functools
import math

import jax
import jax.numpy as jnp
from jax import lax
from jax.experimental import pallas as pl
from jax.experimental.pallas import tpu as pltpu
from jax.sharding import PartitionSpec as P

HD = 128
NT = (((1,), (1,)), ((), ()))
MIB = 2 ** 20
STEP = 4
LIMIT = 64.0
JOINT = 4


def in_hbm(array):
    return pltpu.with_memory_space_constraint(array, pltpu.HBM)


def block_place(chunk, order_ref, me_ref):
    own = 2 * me_ref[0]
    return jnp.where(order_ref[own] > order_ref[own + 1], 1 - chunk, chunk)


def pick(z, options):
    value = jnp.int32(options[-1])
    for i in range(len(options) - 1):
        value = jnp.where(z == i, jnp.int32(options[i]), value)
    return value


def attend_kernel(half, chunk, pieces, heads, waited, blocks_by_z, order_ref, me_ref, z_ref,
                  q_ref, w_ref, *refs):
    k_refs, v_refs = refs[:pieces], refs[pieces:2 * pieces]
    refs = refs[2 * pieces + waited:]
    if blocks_by_z:
        o_ref, far_ref, *refs, tiles, tile_sems = refs
        count, _, wide_tile = tiles.shape
        block = pick(z_ref[0], blocks_by_z)

        def tile_copy(j):
            place = pl.multiple_of((block * count + j) * wide_tile, wide_tile)
            return pltpu.make_async_copy(
                w_ref.at[:, pl.ds(place, wide_tile)], tiles.at[j], tile_sems.at[j])
    else:
        o_ref, *refs = refs
    inv, q_all, k_all, v_all, v_wide, acc, top, above, sems = refs
    blocks = order_ref.shape[0]
    per = blocks // pieces
    tile = half
    width = o_ref.shape[1] // heads
    group = width // HD
    joint = math.gcd(group, JOINT)
    shard = per * half
    factor = HD ** (-0.5) * math.log2(math.e)
    own = block_place(chunk, order_ref, me_ref)
    me = me_ref[0]
    head = pl.program_id(0)
    lanes = pl.ds(pl.multiple_of(head * HD, HD), HD)

    def copies():
        mine = pl.ds(pl.multiple_of(own * half, half), half)
        pairs = [(q_ref.at[mine, :], q_all)]
        for r in range(pieces):
            here = pl.ds(r * shard, shard)
            pairs += [(k_refs[r], k_all.at[here, :]), (v_refs[r], v_all.at[here, :])]
        return [pltpu.make_async_copy(src, dst, sems.at[i]) for i, (src, dst) in enumerate(pairs)]

    @pl.when(head == 0)
    def _():
        for copy in copies():
            copy.start()
        if blocks_by_z:
            @pl.when(block >= 0)
            def _():
                for j in range(count):
                    tile_copy(j).start()

        def invert(b, _):
            inv[order_ref[b]] = jnp.bitwise_xor(b // per, me) * per + lax.rem(b, per)
            return 0

        lax.fori_loop(0, blocks, invert, 0)
        v_wide[:, HD:] = jnp.ones((v_wide.shape[0], HD), v_wide.dtype)
        for copy in copies()[:3]:
            copy.wait()

    v_wide[:shard, :HD] = v_all[:shard, lanes]
    earlier = order_ref[me * per + own]

    def keys_of(blocks_in):
        rows = [pl.ds(pl.multiple_of(b * half, half), half) for b in blocks_in]
        return (jnp.concatenate([k_all[r, lanes] for r in rows], axis=0),
                jnp.concatenate([v_wide[r, :] for r in rows], axis=0))

    def over_tiles(k_cat, use):
        def scores(g):
            q_cat = jnp.concatenate([
                q_all[:, pl.ds(pl.multiple_of(head * width + i * HD, HD), HD)]
                for i in range(g, g + joint)], axis=0)
            return lax.dot_general(q_cat, k_cat, NT, preferred_element_type=jnp.float32)

        score = scores(0)
        for g in range(0, group, joint):
            ahead = scores(g + joint) if g + joint < group else None
            use(pl.ds(g * tile, joint * tile), score)
            score = ahead

    def diagonal():
        k_cat, v_cat = keys_of([own])
        query = lax.rem(lax.broadcasted_iota(jnp.int32, (joint * tile, half), 0), tile)
        seen = lax.broadcasted_iota(jnp.int32, (joint * tile, half), 1) <= query

        def use(rows, score):
            score = jnp.where(seen, score, -1e30)
            peak = jnp.max(score, axis=1, keepdims=True)
            weight = jnp.exp2((score - peak) * factor)
            top[rows, :] = jnp.broadcast_to(peak, (joint * tile, HD))
            acc[rows, :] = jnp.dot(weight.astype(jnp.bfloat16), v_cat,
                                   preferred_element_type=jnp.float32)

        over_tiles(k_cat, use)

    def wide(array, count):
        return jnp.concatenate([array] * (count * half // HD), axis=1)

    def step(places):
        k_cat, v_cat = keys_of(places)
        count = len(places)

        def use(rows, score):
            power = (score - wide(top[rows, :], count)) * factor
            across = pl.ds(0, count * half)
            above[:, across] = jnp.maximum(
                above[:, across], jnp.max(power.reshape(-1, 8, power.shape[1]), axis=0))
            acc[rows, :] = acc[rows, :] + jnp.dot(
                jnp.exp2(power).astype(jnp.bfloat16), v_cat, preferred_element_type=jnp.float32)

        over_tiles(k_cat, use)

    def full_step(n, _):
        step([inv[STEP * n + i] for i in range(STEP)])
        return 0

    def careful_step(n, _):
        k_cat, v_cat = keys_of([inv[n]])

        def one(g, _):
            at = pl.ds(pl.multiple_of(head * width + g * HD, HD), HD)
            rows = pl.ds(pl.multiple_of(g * tile, tile), tile)
            score = lax.dot_general(q_all[:, at], k_cat, NT, preferred_element_type=jnp.float32)
            old = top[rows, :]
            peak = jnp.maximum(old, jnp.max(score, axis=1, keepdims=True))
            top[rows, :] = peak
            weight = jnp.exp2((score - wide(peak, 1)) * factor)
            shrink = jnp.exp2((old - peak) * factor)
            acc[rows, :] = acc[rows, :] * jnp.concatenate([shrink, shrink], axis=1) + jnp.dot(
                weight.astype(jnp.bfloat16), v_cat, preferred_element_type=jnp.float32)
            return 0

        lax.fori_loop(0, group, one, 0)
        return 0

    diagonal()

    @pl.when(head == 0)
    def _():
        for copy in copies()[3:]:
            copy.wait()

    v_wide[shard:, :HD] = v_all[shard:, lanes]
    above[...] = jnp.zeros_like(above)
    lax.fori_loop(0, earlier // STEP, full_step, 0)
    for rest in range(1, STEP):
        @pl.when(lax.rem(earlier, STEP) == rest)
        def _():
            step([inv[earlier - rest + i] for i in range(rest)])

    @pl.when(jnp.max(above[...]) > LIMIT)
    def _():
        diagonal()
        lax.fori_loop(0, earlier, careful_step, 0)

    for g in range(group):
        part = acc[g * tile:(g + 1) * tile, :]
        at = pl.ds(pl.multiple_of(head * width + g * HD, HD), HD)
        o_ref[:, at] = (part[:, :HD] / part[:, HD:]).astype(o_ref.dtype)
    if not blocks_by_z:
        return

    @pl.when(jnp.logical_and(head == heads - 1, block >= 0))
    def _():
        def column(j, _):
            tile_copy(j).wait()
            across = pl.ds(pl.multiple_of(j * wide_tile, wide_tile), wide_tile)
            far_ref[:, across] = jnp.dot(
                o_ref[...], tiles[j], preferred_element_type=jnp.float32).astype(far_ref.dtype)
            return 0

        lax.fori_loop(0, count, column, 0)


def attend(queries, k_pieces, v_pieces, w_out, order, me, z, chunk, half, after=(), blocks=None,
           columns=0):
    pieces = len(k_pieces)
    shard, kv_width = k_pieces[0].shape
    heads = kv_width // HD
    depth = queries.shape[1]
    keys = shard * pieces
    rows = depth // heads // HD * half
    anywhere = pl.BlockSpec(memory_space=pl.ANY)
    whole = pl.BlockSpec(memory_space=pltpu.VMEM)
    out_shape = [jax.ShapeDtypeStruct((half, depth), jnp.bfloat16)]
    scratch = [
        pltpu.SMEM((order.shape[0],), jnp.int32),
        pltpu.VMEM((half, depth), jnp.bfloat16),
        pltpu.VMEM((keys, kv_width), jnp.bfloat16),
        pltpu.VMEM((keys, kv_width), jnp.bfloat16),
        pltpu.VMEM((keys, 2 * HD), jnp.bfloat16),
        pltpu.VMEM((rows, 2 * HD), jnp.float32),
        pltpu.VMEM((rows, HD), jnp.float32),
        pltpu.VMEM((8, STEP * half), jnp.float32),
        pltpu.SemaphoreType.DMA((2 * pieces + 1,)),
    ]
    if blocks:
        wide = min(columns, 256)
        out_shape.append(jax.ShapeDtypeStruct((half, columns), jnp.bfloat16))
        scratch += [
            pltpu.VMEM((columns // wide, depth, wide), w_out.dtype),
            pltpu.SemaphoreType.DMA((columns // wide,)),
        ]
    return pl.pallas_call(
        functools.partial(attend_kernel, half, chunk, pieces, heads, len(after), blocks),
        out_shape=out_shape,
        grid_spec=pltpu.PrefetchScalarGridSpec(
            num_scalar_prefetch=3,
            grid=(heads,),
            in_specs=[anywhere] * (2 + 2 * pieces + len(after)),
            out_specs=[whole] * len(out_shape),
            scratch_shapes=scratch,
        ),
        compiler_params=pltpu.CompilerParams(vmem_limit_bytes=44 * MIB),
        cost_estimate=pl.CostEstimate(flops=1, bytes_accessed=0, transcendentals=0),
        name="attend",
    )(in_hbm(order), me, z, in_hbm(queries), in_hbm(w_out), in_hbm(k_pieces[0]), *k_pieces[1:],
      in_hbm(v_pieces[0]), *v_pieces[1:], *after)


def hold_kernel(count, *refs):
    outs, sems = refs[-count - 1:-1], refs[-1]
    copies = [pltpu.make_async_copy(refs[i], outs[i], sems.at[i]) for i in range(count)]
    for copy in copies:
        copy.start()
    for copy in copies:
        copy.wait()


def hold(arrays, until):
    count = len(arrays)
    anywhere = pl.BlockSpec(memory_space=pl.ANY)
    return pl.pallas_call(
        functools.partial(hold_kernel, count),
        out_shape=[jax.ShapeDtypeStruct(a.shape, a.dtype) for a in arrays],
        in_specs=[anywhere] * (count + len(until)),
        out_specs=[pl.BlockSpec(memory_space=pltpu.VMEM)] * count,
        scratch_shapes=[pltpu.SemaphoreType.DMA((count,))],
        compiler_params=pltpu.CompilerParams(vmem_limit_bytes=40 * MIB),
        cost_estimate=pl.CostEstimate(flops=1, bytes_accessed=0, transcendentals=0),
        name="hold",
    )(*[in_hbm(a) for a in arrays], *until)


def gather(keys, values, axis):
    count = lax.axis_size(axis)

    def spread(held, bit):
        pairs = [(i, i ^ (1 << bit)) for i in range(count)]
        return {r ^ (1 << bit): lax.ppermute(a, axis, pairs) for r, a in held.items()}

    bits = list(range(1, count.bit_length() - 1))
    k_held, v_held = {0: keys}, {0: values}
    for k_bit, v_bit in zip(bits, bits[::-1]):
        k_held.update(spread(k_held, k_bit))
        v_held.update(spread(v_held, v_bit))
    until = [k_held[1 << bits[0]], v_held[1 << bits[-1]]]
    k_own, v_own = hold([keys, values], until)
    k_held.update(spread({**k_held, 0: k_own}, 0))
    v_held.update(spread({**v_held, 0: v_own}, 0))
    return [k_held[r] for r in range(count)], [v_held[r] for r in range(count)]


def share_kernel(roles, waited, z_ref, w_ref, *refs):
    operands = sum(1 + extra for _, extra in roles)
    out, tiles, sems = refs[operands + waited:]
    count, _, wide = tiles.shape
    for blocks, extra in roles:
        a_ref, arrived, refs = refs[0], refs[1:1 + extra], refs[1 + extra:]
        block = pick(z_ref[0], blocks)

        @pl.when(block >= 0)
        def _(block=block, a_ref=a_ref, arrived=arrived):
            def copy(j):
                place = pl.multiple_of((block * count + j) * wide, wide)
                return pltpu.make_async_copy(
                    w_ref.at[:, pl.ds(place, wide)], tiles.at[j], sems.at[j])

            def column(j, _):
                copy(j).wait()
                lanes = pl.ds(pl.multiple_of(j * wide, wide), wide)
                total = jnp.dot(a_ref[...], tiles[j], preferred_element_type=jnp.float32)
                for ref in arrived:
                    total = total + ref[:, lanes].astype(jnp.float32)
                out[:, lanes] = total.astype(out.dtype)
                return 0

            for j in range(count):
                copy(j).start()
            lax.fori_loop(0, count, column, 0)


def share(roles, w_out, z, columns, after=()):
    tok, depth = roles[0][1].shape
    wide = min(columns, 256)
    count = columns // wide
    whole = pl.BlockSpec(memory_space=pltpu.VMEM)
    anywhere = pl.BlockSpec(memory_space=pl.ANY)
    operands = [a for _, attended, arrived in roles for a in (attended, *arrived)]
    return pl.pallas_call(
        functools.partial(share_kernel, [(b, len(arrived)) for b, _, arrived in roles], len(after)),
        out_shape=jax.ShapeDtypeStruct((tok, columns), jnp.bfloat16),
        grid_spec=pltpu.PrefetchScalarGridSpec(
            num_scalar_prefetch=1,
            grid=(),
            in_specs=[anywhere] + [whole] * len(operands) + [anywhere] * len(after),
            out_specs=whole,
            scratch_shapes=[
                pltpu.VMEM((count, depth, wide), w_out.dtype),
                pltpu.SemaphoreType.DMA((count,)),
            ],
        ),
        compiler_params=pltpu.CompilerParams(vmem_limit_bytes=40 * MIB),
        cost_estimate=pl.CostEstimate(flops=1, bytes_accessed=0, transcendentals=0),
        name="share",
    )(z, in_hbm(w_out), *operands, *after)


def own_kernel(chunks, waited, z_ref, w_ref, *refs):
    a_refs, outs, (tiles, sems) = refs[:chunks], refs[chunks + waited:-2], refs[-2:]
    count, _, wide = tiles.shape

    def copy(j):
        place = pl.multiple_of((z_ref[0] * count + j) * wide, wide)
        return pltpu.make_async_copy(w_ref.at[:, pl.ds(place, wide)], tiles.at[j], sems.at[j])

    def column(j, _):
        copy(j).wait()
        lanes = pl.ds(pl.multiple_of(j * wide, wide), wide)
        rows = jnp.concatenate([ref[...] for ref in a_refs], axis=0)
        total = jnp.dot(rows, tiles[j], preferred_element_type=jnp.float32)
        tok = outs[0].shape[0]
        for i, out in enumerate(outs):
            out[:, lanes] = total[i * tok:(i + 1) * tok]
        return 0

    for j in range(count):
        copy(j).start()
    lax.fori_loop(0, count, column, 0)


def own_columns(chunks, w_out, z, columns, after):
    tok, depth = chunks[0].shape
    wide = min(columns, 256)
    count = columns // wide
    whole = pl.BlockSpec(memory_space=pltpu.VMEM)
    anywhere = pl.BlockSpec(memory_space=pl.ANY)
    return pl.pallas_call(
        functools.partial(own_kernel, len(chunks), len(after)),
        out_shape=[jax.ShapeDtypeStruct((tok, columns), jnp.float32)] * len(chunks),
        grid_spec=pltpu.PrefetchScalarGridSpec(
            num_scalar_prefetch=1,
            grid=(),
            in_specs=[anywhere] + [whole] * len(chunks) + [anywhere] * len(after),
            out_specs=[whole] * len(chunks),
            scratch_shapes=[
                pltpu.VMEM((count, depth, wide), w_out.dtype),
                pltpu.SemaphoreType.DMA((count,)),
            ],
        ),
        compiler_params=pltpu.CompilerParams(vmem_limit_bytes=40 * MIB),
        cost_estimate=pl.CostEstimate(flops=1, bytes_accessed=0, transcendentals=0),
        name="own",
    )(z, in_hbm(w_out), *chunks, *after)


def finish_kernel(extra, chunk, order_ref, me_ref, *refs):
    out, summed, sem = refs[-3:]
    total = refs[0][...].astype(jnp.float32)
    for ref in refs[1:extra]:
        total = total + ref[...].astype(jnp.float32)
    summed[...] = total.astype(summed.dtype)
    tok = summed.shape[0]
    first = pl.multiple_of(block_place(chunk, order_ref, me_ref) * tok, tok)
    copy = pltpu.make_async_copy(summed, out.at[pl.ds(first, tok), :], sem)
    copy.start()
    copy.wait()


def finish(terms, order, me, chunk, whole_tok, out, after=()):
    tok, columns = terms[0].shape
    anywhere = pl.BlockSpec(memory_space=pl.ANY)
    before = [] if out is None else [out]
    return pl.pallas_call(
        functools.partial(finish_kernel, len(terms), chunk),
        out_shape=jax.ShapeDtypeStruct((whole_tok, columns), jnp.bfloat16),
        grid_spec=pltpu.PrefetchScalarGridSpec(
            num_scalar_prefetch=2,
            grid=(),
            in_specs=[pl.BlockSpec(memory_space=pltpu.VMEM)] * len(terms)
            + [anywhere] * len(before + list(after)),
            out_specs=anywhere,
            scratch_shapes=[pltpu.VMEM((tok, columns), jnp.bfloat16), pltpu.SemaphoreType.DMA],
        ),
        input_output_aliases={2 + len(terms): 0} if before else {},
        compiler_params=pltpu.CompilerParams(vmem_limit_bytes=40 * MIB),
        cost_estimate=pl.CostEstimate(flops=1, bytes_accessed=0, transcendentals=0),
        name="finish",
    )(order, me, *terms, *before, *after)


def swap(array, pairs):
    return lax.ppermute(array, "head", pairs)


def line_of_four(attended, w_out, z, order, me, columns, tok):
    outer, inner, back = [(0, 1), (3, 2)], [(1, 2), (2, 1)], [(1, 0), (2, 3)]
    far_end, near_end, last_end = (3, -1, -1, 0), (2, -1, -1, 1), (1, -1, -1, 2)
    far_on, near_on, home_on = (-1, 3, 0, -1), (-1, 2, 1, -1), (-1, 0, 3, -1)

    def part(roles, after=()):
        return share(roles, w_out, z, columns, after)

    a0, far_0 = attended(0, [], far_end)
    near_0 = part([(near_end, a0, [])])
    a1, = attended(1, [near_0])
    far_0, near_0 = swap(far_0, outer), swap(near_0, outer)
    step = part([(far_end, a1, []), (far_on, a0, [far_0])])
    far_1, far_0 = swap(step, outer), swap(step, inner)
    step = part([(near_end, a1, []), (near_on, a0, [near_0])], [step])
    near_1, near_0 = swap(step, outer), swap(step, inner)
    own = own_columns([a0, a1], w_out, z, columns, [step])
    step = part([(last_end, a0, []), (home_on, a0, [far_0])], own[:1])
    edge_0 = swap(step, outer + back)
    step = part([(last_end, a1, []), (far_on, a1, [far_1])], [step])
    last_1, far_1 = swap(step, outer), swap(step, inner)
    step = part([(near_on, a1, [near_1])], [step, near_0])
    near_1 = swap(step, inner)
    step = part([(home_on, a1, [far_1])], [step])
    home_1 = swap(step, back)
    out = finish([own[0], near_0, edge_0], order, me, 0, tok, None, [step])
    return finish([own[1], near_1, last_1, home_1], order, me, 1, tok, out)


def per_device(queries, keys, values, w_out, order):
    tok = queries.shape[0]
    half = tok // 2
    line = lax.axis_size("head")
    columns = w_out.shape[1] // line
    me = lax.axis_index("blk").astype(jnp.int32).reshape(1)
    z = lax.axis_index("head").astype(jnp.int32).reshape(1)
    k_pieces, v_pieces = gather(keys, values, "blk")

    def attended(chunk, after, blocks=None):
        return attend(queries, k_pieces, v_pieces, w_out, order, me, z, chunk, half, after, blocks,
                      columns)

    if line == 4:
        return line_of_four(attended, w_out, z, order, me, columns, tok)
    outs = []
    for c in range(2):
        sums = jnp.dot(attended(c, [])[0], w_out, preferred_element_type=jnp.float32)
        outs.append(lax.psum_scatter(
            sums.astype(jnp.bfloat16), "head", scatter_dimension=1, tiled=True))
    swapped = block_place(0, order, me) == 1
    outs = [jnp.where(swapped, outs[1 - c], outs[c]) for c in range(2)]
    return jnp.concatenate(outs, axis=0)


def solution(mesh):
    return jax.shard_map(
        per_device,
        mesh=mesh,
        in_specs=(P("blk", "head"), P("blk", "head"), P("blk", "head"), P("head", None), P()),
        out_specs=P("blk", "head"),
        check_vma=False,
    )
```

```python
import functools
import math

import jax
import jax.numpy as jnp
from jax import lax
from jax.experimental import pallas as pl
from jax.experimental.pallas import tpu as pltpu
from jax.sharding import PartitionSpec as P

HD = 128
NT = (((1,), (1,)), ((), ()))
MIB = 2 ** 20
STEP = 4
LIMIT = 64.0
JOINT = 4


def in_hbm(array):
    return pltpu.with_memory_space_constraint(array, pltpu.HBM)


def block_place(chunk, order_ref, me_ref):
    own = 2 * me_ref[0]
    return jnp.where(order_ref[own] > order_ref[own + 1], 1 - chunk, chunk)


def pick(z, options):
    value = jnp.int32(options[-1])
    for i in range(len(options) - 1):
        value = jnp.where(z == i, jnp.int32(options[i]), value)
    return value


def attend_kernel(half, chunk, pieces, heads, waited, blocks_by_z, order_ref, me_ref, z_ref,
                  q_ref, w_ref, *refs):
    k_refs, v_refs = refs[:pieces], refs[pieces:2 * pieces]
    refs = refs[2 * pieces + waited:]
    if blocks_by_z:
        o_ref, far_ref, *refs, tiles, tile_sems = refs
        count, _, wide_tile = tiles.shape
        block = pick(z_ref[0], blocks_by_z)

        def tile_copy(j):
            place = pl.multiple_of((block * count + j) * wide_tile, wide_tile)
            return pltpu.make_async_copy(
                w_ref.at[:, pl.ds(place, wide_tile)], tiles.at[j], tile_sems.at[j])
    else:
        o_ref, *refs = refs
    inv, q_all, k_all, v_all, v_wide, acc, top, above, sems = refs
    blocks = order_ref.shape[0]
    per = blocks // pieces
    tile = half
    width = o_ref.shape[1] // heads
    group = width // HD
    joint = math.gcd(group, JOINT)
    shard = per * half
    factor = HD ** (-0.5) * math.log2(math.e)
    own = block_place(chunk, order_ref, me_ref)
    me = me_ref[0]
    head = pl.program_id(0)
    lanes = pl.ds(pl.multiple_of(head * HD, HD), HD)

    def copies():
        mine = pl.ds(pl.multiple_of(own * half, half), half)
        pairs = [(q_ref.at[mine, :], q_all)]
        for r in range(pieces):
            here = pl.ds(r * shard, shard)
            pairs += [(k_refs[r], k_all.at[here, :]), (v_refs[r], v_all.at[here, :])]
        return [pltpu.make_async_copy(src, dst, sems.at[i]) for i, (src, dst) in enumerate(pairs)]

    @pl.when(head == 0)
    def _():
        for copy in copies():
            copy.start()
        if blocks_by_z:
            @pl.when(block >= 0)
            def _():
                for j in range(count):
                    tile_copy(j).start()

        def invert(b, _):
            inv[order_ref[b]] = jnp.bitwise_xor(b // per, me) * per + lax.rem(b, per)
            return 0

        lax.fori_loop(0, blocks, invert, 0)
        v_wide[:, HD:] = jnp.ones((v_wide.shape[0], HD), v_wide.dtype)
        for copy in copies()[:3]:
            copy.wait()

    v_wide[:shard, :HD] = v_all[:shard, lanes]
    earlier = order_ref[me * per + own]

    def keys_of(blocks_in):
        rows = [pl.ds(pl.multiple_of(b * half, half), half) for b in blocks_in]
        return (jnp.concatenate([k_all[r, lanes] for r in rows], axis=0),
                jnp.concatenate([v_wide[r, :] for r in rows], axis=0))

    def over_tiles(k_cat, use):
        def scores(g):
            q_cat = jnp.concatenate([
                q_all[:, pl.ds(pl.multiple_of(head * width + i * HD, HD), HD)]
                for i in range(g, g + joint)], axis=0)
            return lax.dot_general(q_cat, k_cat, NT, preferred_element_type=jnp.float32)

        score = scores(0)
        for g in range(0, group, joint):
            ahead = scores(g + joint) if g + joint < group else None
            use(pl.ds(g * tile, joint * tile), score)
            score = ahead

    def diagonal():
        k_cat, v_cat = keys_of([own])
        query = lax.rem(lax.broadcasted_iota(jnp.int32, (joint * tile, half), 0), tile)
        seen = lax.broadcasted_iota(jnp.int32, (joint * tile, half), 1) <= query

        def use(rows, score):
            score = jnp.where(seen, score, -1e30)
            peak = jnp.max(score, axis=1, keepdims=True)
            weight = jnp.exp2((score - peak) * factor)
            top[rows, :] = jnp.broadcast_to(peak, (joint * tile, HD))
            acc[rows, :] = jnp.dot(weight.astype(jnp.bfloat16), v_cat,
                                   preferred_element_type=jnp.float32)

        over_tiles(k_cat, use)

    def wide(array, count):
        return jnp.concatenate([array] * (count * half // HD), axis=1)

    def step(places):
        k_cat, v_cat = keys_of(places)
        count = len(places)

        def use(rows, score):
            power = (score - wide(top[rows, :], count)) * factor
            across = pl.ds(0, count * half)
            above[:, across] = jnp.maximum(
                above[:, across], jnp.max(power.reshape(-1, 8, power.shape[1]), axis=0))
            acc[rows, :] = acc[rows, :] + jnp.dot(
                jnp.exp2(power).astype(jnp.bfloat16), v_cat, preferred_element_type=jnp.float32)

        over_tiles(k_cat, use)

    def full_step(n, _):
        step([inv[STEP * n + i] for i in range(STEP)])
        return 0

    def careful_step(n, _):
        k_cat, v_cat = keys_of([inv[n]])

        def one(g, _):
            at = pl.ds(pl.multiple_of(head * width + g * HD, HD), HD)
            rows = pl.ds(pl.multiple_of(g * tile, tile), tile)
            score = lax.dot_general(q_all[:, at], k_cat, NT, preferred_element_type=jnp.float32)
            old = top[rows, :]
            peak = jnp.maximum(old, jnp.max(score, axis=1, keepdims=True))
            top[rows, :] = peak
            weight = jnp.exp2((score - wide(peak, 1)) * factor)
            shrink = jnp.exp2((old - peak) * factor)
            acc[rows, :] = acc[rows, :] * jnp.concatenate([shrink, shrink], axis=1) + jnp.dot(
                weight.astype(jnp.bfloat16), v_cat, preferred_element_type=jnp.float32)
            return 0

        lax.fori_loop(0, group, one, 0)
        return 0

    diagonal()

    @pl.when(head == 0)
    def _():
        for copy in copies()[3:]:
            copy.wait()

    v_wide[shard:, :HD] = v_all[shard:, lanes]
    above[...] = jnp.zeros_like(above)
    lax.fori_loop(0, earlier // STEP, full_step, 0)
    for rest in range(1, STEP):
        @pl.when(lax.rem(earlier, STEP) == rest)
        def _():
            step([inv[earlier - rest + i] for i in range(rest)])

    @pl.when(jnp.max(above[...]) > LIMIT)
    def _():
        diagonal()
        lax.fori_loop(0, earlier, careful_step, 0)

    for g in range(group):
        part = acc[g * tile:(g + 1) * tile, :]
        at = pl.ds(pl.multiple_of(head * width + g * HD, HD), HD)
        o_ref[:, at] = (part[:, :HD] / part[:, HD:]).astype(o_ref.dtype)
    if not blocks_by_z:
        return

    @pl.when(jnp.logical_and(head == heads - 1, block >= 0))
    def _():
        def column(j, _):
            tile_copy(j).wait()
            across = pl.ds(pl.multiple_of(j * wide_tile, wide_tile), wide_tile)
            far_ref[:, across] = jnp.dot(
                o_ref[...], tiles[j], preferred_element_type=jnp.float32).astype(far_ref.dtype)
            return 0

        lax.fori_loop(0, count, column, 0)


def attend(queries, k_pieces, v_pieces, w_out, order, me, z, chunk, half, after=(), blocks=None,
           columns=0):
    pieces = len(k_pieces)
    shard, kv_width = k_pieces[0].shape
    heads = kv_width // HD
    depth = queries.shape[1]
    keys = shard * pieces
    rows = depth // heads // HD * half
    anywhere = pl.BlockSpec(memory_space=pl.ANY)
    whole = pl.BlockSpec(memory_space=pltpu.VMEM)
    out_shape = [jax.ShapeDtypeStruct((half, depth), jnp.bfloat16)]
    scratch = [
        pltpu.SMEM((order.shape[0],), jnp.int32),
        pltpu.VMEM((half, depth), jnp.bfloat16),
        pltpu.VMEM((keys, kv_width), jnp.bfloat16),
        pltpu.VMEM((keys, kv_width), jnp.bfloat16),
        pltpu.VMEM((keys, 2 * HD), jnp.bfloat16),
        pltpu.VMEM((rows, 2 * HD), jnp.float32),
        pltpu.VMEM((rows, HD), jnp.float32),
        pltpu.VMEM((8, STEP * half), jnp.float32),
        pltpu.SemaphoreType.DMA((2 * pieces + 1,)),
    ]
    if blocks:
        wide = min(columns, 256)
        out_shape.append(jax.ShapeDtypeStruct((half, columns), jnp.bfloat16))
        scratch += [
            pltpu.VMEM((columns // wide, depth, wide), w_out.dtype),
            pltpu.SemaphoreType.DMA((columns // wide,)),
        ]
    return pl.pallas_call(
        functools.partial(attend_kernel, half, chunk, pieces, heads, len(after), blocks),
        out_shape=out_shape,
        grid_spec=pltpu.PrefetchScalarGridSpec(
            num_scalar_prefetch=3,
            grid=(heads,),
            in_specs=[anywhere] * (2 + 2 * pieces + len(after)),
            out_specs=[whole] * len(out_shape),
            scratch_shapes=scratch,
        ),
        compiler_params=pltpu.CompilerParams(vmem_limit_bytes=44 * MIB),
        cost_estimate=pl.CostEstimate(flops=1, bytes_accessed=0, transcendentals=0),
        name="attend",
    )(in_hbm(order), me, z, in_hbm(queries), in_hbm(w_out), in_hbm(k_pieces[0]), *k_pieces[1:],
      in_hbm(v_pieces[0]), *v_pieces[1:], *after)


def hold_kernel(count, *refs):
    outs, sems = refs[-count - 1:-1], refs[-1]
    copies = [pltpu.make_async_copy(refs[i], outs[i], sems.at[i]) for i in range(count)]
    for copy in copies:
        copy.start()
    for copy in copies:
        copy.wait()


def hold(arrays, until):
    count = len(arrays)
    anywhere = pl.BlockSpec(memory_space=pl.ANY)
    return pl.pallas_call(
        functools.partial(hold_kernel, count),
        out_shape=[jax.ShapeDtypeStruct(a.shape, a.dtype) for a in arrays],
        in_specs=[anywhere] * (count + len(until)),
        out_specs=[pl.BlockSpec(memory_space=pltpu.VMEM)] * count,
        scratch_shapes=[pltpu.SemaphoreType.DMA((count,))],
        compiler_params=pltpu.CompilerParams(vmem_limit_bytes=40 * MIB),
        cost_estimate=pl.CostEstimate(flops=1, bytes_accessed=0, transcendentals=0),
        name="hold",
    )(*[in_hbm(a) for a in arrays], *until)


def gather(keys, values, axis):
    count = lax.axis_size(axis)

    def spread(held, bit):
        pairs = [(i, i ^ (1 << bit)) for i in range(count)]
        return {r ^ (1 << bit): lax.ppermute(a, axis, pairs) for r, a in held.items()}

    bits = list(range(1, count.bit_length() - 1))
    k_held, v_held = {0: keys}, {0: values}
    for k_bit, v_bit in zip(bits, bits[::-1]):
        k_held.update(spread(k_held, k_bit))
        v_held.update(spread(v_held, v_bit))
    until = [k_held[1 << bits[0]], v_held[1 << bits[-1]]]
    k_own, v_own = hold([keys, values], until)
    k_held.update(spread({**k_held, 0: k_own}, 0))
    v_held.update(spread({**v_held, 0: v_own}, 0))
    return [k_held[r] for r in range(count)], [v_held[r] for r in range(count)]


def share_kernel(roles, waited, z_ref, w_ref, *refs):
    operands = sum(1 + extra for _, extra in roles)
    out, tiles, sems = refs[operands + waited:]
    count, _, wide = tiles.shape
    for blocks, extra in roles:
        a_ref, arrived, refs = refs[0], refs[1:1 + extra], refs[1 + extra:]
        block = pick(z_ref[0], blocks)

        @pl.when(block >= 0)
        def _(block=block, a_ref=a_ref, arrived=arrived):
            def copy(j):
                place = pl.multiple_of((block * count + j) * wide, wide)
                return pltpu.make_async_copy(
                    w_ref.at[:, pl.ds(place, wide)], tiles.at[j], sems.at[j])

            def column(j, _):
                copy(j).wait()
                lanes = pl.ds(pl.multiple_of(j * wide, wide), wide)
                total = jnp.dot(a_ref[...], tiles[j], preferred_element_type=jnp.float32)
                for ref in arrived:
                    total = total + ref[:, lanes].astype(jnp.float32)
                out[:, lanes] = total.astype(out.dtype)
                return 0

            for j in range(count):
                copy(j).start()
            lax.fori_loop(0, count, column, 0)


def share(roles, w_out, z, columns, after=()):
    tok, depth = roles[0][1].shape
    wide = min(columns, 256)
    count = columns // wide
    whole = pl.BlockSpec(memory_space=pltpu.VMEM)
    anywhere = pl.BlockSpec(memory_space=pl.ANY)
    operands = [a for _, attended, arrived in roles for a in (attended, *arrived)]
    return pl.pallas_call(
        functools.partial(share_kernel, [(b, len(arrived)) for b, _, arrived in roles], len(after)),
        out_shape=jax.ShapeDtypeStruct((tok, columns), jnp.bfloat16),
        grid_spec=pltpu.PrefetchScalarGridSpec(
            num_scalar_prefetch=1,
            grid=(),
            in_specs=[anywhere] + [whole] * len(operands) + [anywhere] * len(after),
            out_specs=whole,
            scratch_shapes=[
                pltpu.VMEM((count, depth, wide), w_out.dtype),
                pltpu.SemaphoreType.DMA((count,)),
            ],
        ),
        compiler_params=pltpu.CompilerParams(vmem_limit_bytes=40 * MIB),
        cost_estimate=pl.CostEstimate(flops=1, bytes_accessed=0, transcendentals=0),
        name="share",
    )(z, in_hbm(w_out), *operands, *after)


def own_kernel(chunks, waited, z_ref, w_ref, *refs):
    a_refs, outs, (tiles, sems) = refs[:chunks], refs[chunks + waited:-2], refs[-2:]
    count, _, wide = tiles.shape

    def copy(j):
        place = pl.multiple_of((z_ref[0] * count + j) * wide, wide)
        return pltpu.make_async_copy(w_ref.at[:, pl.ds(place, wide)], tiles.at[j], sems.at[j])

    def column(j, _):
        copy(j).wait()
        lanes = pl.ds(pl.multiple_of(j * wide, wide), wide)
        rows = jnp.concatenate([ref[...] for ref in a_refs], axis=0)
        total = jnp.dot(rows, tiles[j], preferred_element_type=jnp.float32)
        tok = outs[0].shape[0]
        for i, out in enumerate(outs):
            out[:, lanes] = total[i * tok:(i + 1) * tok]
        return 0

    for j in range(count):
        copy(j).start()
    lax.fori_loop(0, count, column, 0)


def own_columns(chunks, w_out, z, columns, after):
    tok, depth = chunks[0].shape
    wide = min(columns, 256)
    count = columns // wide
    whole = pl.BlockSpec(memory_space=pltpu.VMEM)
    anywhere = pl.BlockSpec(memory_space=pl.ANY)
    return pl.pallas_call(
        functools.partial(own_kernel, len(chunks), len(after)),
        out_shape=[jax.ShapeDtypeStruct((tok, columns), jnp.float32)] * len(chunks),
        grid_spec=pltpu.PrefetchScalarGridSpec(
            num_scalar_prefetch=1,
            grid=(),
            in_specs=[anywhere] + [whole] * len(chunks) + [anywhere] * len(after),
            out_specs=[whole] * len(chunks),
            scratch_shapes=[
                pltpu.VMEM((count, depth, wide), w_out.dtype),
                pltpu.SemaphoreType.DMA((count,)),
            ],
        ),
        compiler_params=pltpu.CompilerParams(vmem_limit_bytes=40 * MIB),
        cost_estimate=pl.CostEstimate(flops=1, bytes_accessed=0, transcendentals=0),
        name="own",
    )(z, in_hbm(w_out), *chunks, *after)


def finish_kernel(extra, chunk, order_ref, me_ref, *refs):
    out, summed, sem = refs[-3:]
    total = refs[0][...].astype(jnp.float32)
    for ref in refs[1:extra]:
        total = total + ref[...].astype(jnp.float32)
    summed[...] = total.astype(summed.dtype)
    tok = summed.shape[0]
    first = pl.multiple_of(block_place(chunk, order_ref, me_ref) * tok, tok)
    copy = pltpu.make_async_copy(summed, out.at[pl.ds(first, tok), :], sem)
    copy.start()
    copy.wait()


def finish(terms, order, me, chunk, whole_tok, out, after=()):
    tok, columns = terms[0].shape
    anywhere = pl.BlockSpec(memory_space=pl.ANY)
    before = [] if out is None else [out]
    return pl.pallas_call(
        functools.partial(finish_kernel, len(terms), chunk),
        out_shape=jax.ShapeDtypeStruct((whole_tok, columns), jnp.bfloat16),
        grid_spec=pltpu.PrefetchScalarGridSpec(
            num_scalar_prefetch=2,
            grid=(),
            in_specs=[pl.BlockSpec(memory_space=pltpu.VMEM)] * len(terms)
            + [anywhere] * len(before + list(after)),
            out_specs=anywhere,
            scratch_shapes=[pltpu.VMEM((tok, columns), jnp.bfloat16), pltpu.SemaphoreType.DMA],
        ),
        input_output_aliases={2 + len(terms): 0} if before else {},
        compiler_params=pltpu.CompilerParams(vmem_limit_bytes=40 * MIB),
        cost_estimate=pl.CostEstimate(flops=1, bytes_accessed=0, transcendentals=0),
        name="finish",
    )(order, me, *terms, *before, *after)


def swap(array, pairs):
    return lax.ppermute(array, "head", pairs)


def line_of_four(attended, w_out, z, order, me, columns, tok):
    outer, inner, back = [(0, 1), (3, 2)], [(1, 2), (2, 1)], [(1, 0), (2, 3)]
    far_end, near_end, last_end = (3, -1, -1, 0), (2, -1, -1, 1), (1, -1, -1, 2)
    far_on, near_on, home_on = (-1, 3, 0, -1), (-1, 2, 1, -1), (-1, 0, 3, -1)

    def part(roles, after=()):
        return share(roles, w_out, z, columns, after)

    a0, far_0 = attended(0, [], far_end)
    near_0 = part([(near_end, a0, [])])
    a1, = attended(1, [near_0])
    far_0, near_0 = swap(far_0, outer), swap(near_0, outer)
    step = part([(far_end, a1, []), (far_on, a0, [far_0])])
    far_1, far_0 = swap(step, outer), swap(step, inner)
    step = part([(near_end, a1, []), (near_on, a0, [near_0])], [step])
    near_1, near_0 = swap(step, outer), swap(step, inner)
    step = part([(last_end, a0, []), (home_on, a0, [far_0])], [step])
    edge_0 = swap(step, outer + back)
    step = part([(last_end, a1, []), (far_on, a1, [far_1])], [step])
    last_1, far_1 = swap(step, outer), swap(step, inner)
    step = part([(near_on, a1, [near_1])], [step, near_0])
    near_1 = swap(step, inner)
    step = part([(home_on, a1, [far_1])], [step])
    home_1 = swap(step, back)
    own = own_columns([a0, a1], w_out, z, columns, [step])
    out = finish([own[0], near_0, edge_0], order, me, 0, tok, None)
    return finish([own[1], near_1, last_1, home_1], order, me, 1, tok, out)


def per_device(queries, keys, values, w_out, order):
    tok = queries.shape[0]
    half = tok // 2
    line = lax.axis_size("head")
    columns = w_out.shape[1] // line
    me = lax.axis_index("blk").astype(jnp.int32).reshape(1)
    z = lax.axis_index("head").astype(jnp.int32).reshape(1)
    k_pieces, v_pieces = gather(keys, values, "blk")

    def attended(chunk, after, blocks=None):
        return attend(queries, k_pieces, v_pieces, w_out, order, me, z, chunk, half, after, blocks,
                      columns)

    if line == 4:
        return line_of_four(attended, w_out, z, order, me, columns, tok)
    outs = []
    for c in range(2):
        sums = jnp.dot(attended(c, [])[0], w_out, preferred_element_type=jnp.float32)
        outs.append(lax.psum_scatter(
            sums.astype(jnp.bfloat16), "head", scatter_dimension=1, tiled=True))
    swapped = block_place(0, order, me) == 1
    outs = [jnp.where(swapped, outs[1 - c], outs[c]) for c in range(2)]
    return jnp.concatenate(outs, axis=0)


def solution(mesh):
    return jax.shard_map(
        per_device,
        mesh=mesh,
        in_specs=(P("blk", "head"), P("blk", "head"), P("blk", "head"), P("head", None), P()),
        out_specs=P("blk", "head"),
        check_vma=False,
    )
```

```python
import functools
import math

import jax
import jax.numpy as jnp
from jax import lax
from jax.experimental import pallas as pl
from jax.experimental.pallas import tpu as pltpu
from jax.sharding import PartitionSpec as P

HD = 128
NT = (((1,), (1,)), ((), ()))
MIB = 2 ** 20
STEP = 4
LIMIT = 64.0
JOINT = 4


def in_hbm(array):
    return pltpu.with_memory_space_constraint(array, pltpu.HBM)


def block_place(chunk, order_ref, me_ref):
    own = 2 * me_ref[0]
    return jnp.where(order_ref[own] > order_ref[own + 1], 1 - chunk, chunk)


def pick(z, options):
    value = jnp.int32(options[-1])
    for i in range(len(options) - 1):
        value = jnp.where(z == i, jnp.int32(options[i]), value)
    return value


def attend_kernel(half, chunk, pieces, heads, waited, blocks_by_z, order_ref, me_ref, z_ref,
                  q_ref, w_ref, *refs):
    k_refs, v_refs = refs[:pieces], refs[pieces:2 * pieces]
    refs = refs[2 * pieces + waited:]
    if blocks_by_z:
        o_ref, far_ref, *refs, tiles, tile_sems = refs
        count, _, wide_tile = tiles.shape
        block = pick(z_ref[0], blocks_by_z)

        def tile_copy(j):
            place = pl.multiple_of((block * count + j) * wide_tile, wide_tile)
            return pltpu.make_async_copy(
                w_ref.at[:, pl.ds(place, wide_tile)], tiles.at[j], tile_sems.at[j])
    else:
        o_ref, *refs = refs
    inv, q_all, k_all, v_all, v_wide, acc, top, above, sems = refs
    blocks = order_ref.shape[0]
    per = blocks // pieces
    tile = half
    width = o_ref.shape[1] // heads
    group = width // HD
    joint = math.gcd(group, JOINT)
    shard = per * half
    factor = HD ** (-0.5) * math.log2(math.e)
    own = block_place(chunk, order_ref, me_ref)
    me = me_ref[0]
    head = pl.program_id(0)
    lanes = pl.ds(pl.multiple_of(head * HD, HD), HD)

    def copies():
        mine = pl.ds(pl.multiple_of(own * half, half), half)
        pairs = [(q_ref.at[mine, :], q_all)]
        for r in range(pieces):
            here = pl.ds(r * shard, shard)
            pairs += [(k_refs[r], k_all.at[here, :]), (v_refs[r], v_all.at[here, :])]
        return [pltpu.make_async_copy(src, dst, sems.at[i]) for i, (src, dst) in enumerate(pairs)]

    @pl.when(head == 0)
    def _():
        for copy in copies():
            copy.start()
        if blocks_by_z:
            @pl.when(block >= 0)
            def _():
                for j in range(count):
                    tile_copy(j).start()

        def invert(b, _):
            inv[order_ref[b]] = jnp.bitwise_xor(b // per, me) * per + lax.rem(b, per)
            return 0

        lax.fori_loop(0, blocks, invert, 0)
        v_wide[:, HD:] = jnp.ones((v_wide.shape[0], HD), v_wide.dtype)
        for copy in copies()[:3]:
            copy.wait()

    v_wide[:shard, :HD] = v_all[:shard, lanes]
    earlier = order_ref[me * per + own]

    def keys_of(blocks_in):
        rows = [pl.ds(pl.multiple_of(b * half, half), half) for b in blocks_in]
        return (jnp.concatenate([k_all[r, lanes] for r in rows], axis=0),
                jnp.concatenate([v_wide[r, :] for r in rows], axis=0))

    def over_tiles(k_cat, use):
        def scores(g):
            q_cat = jnp.concatenate([
                q_all[:, pl.ds(pl.multiple_of(head * width + i * HD, HD), HD)]
                for i in range(g, g + joint)], axis=0)
            return lax.dot_general(q_cat, k_cat, NT, preferred_element_type=jnp.float32)

        score = scores(0)
        for g in range(0, group, joint):
            ahead = scores(g + joint) if g + joint < group else None
            use(pl.ds(g * tile, joint * tile), score)
            score = ahead

    def diagonal():
        k_cat, v_cat = keys_of([own])
        query = lax.rem(lax.broadcasted_iota(jnp.int32, (joint * tile, half), 0), tile)
        seen = lax.broadcasted_iota(jnp.int32, (joint * tile, half), 1) <= query

        def use(rows, score):
            score = jnp.where(seen, score, -1e30)
            peak = jnp.max(score, axis=1, keepdims=True)
            weight = jnp.exp2((score - peak) * factor)
            top[rows, :] = jnp.broadcast_to(peak, (joint * tile, HD))
            acc[rows, :] = jnp.dot(weight.astype(jnp.bfloat16), v_cat,
                                   preferred_element_type=jnp.float32)

        over_tiles(k_cat, use)

    def wide(array, count):
        return jnp.concatenate([array] * (count * half // HD), axis=1)

    def step(places):
        k_cat, v_cat = keys_of(places)
        count = len(places)

        def use(rows, score):
            power = (score - wide(top[rows, :], count)) * factor
            across = pl.ds(0, count * half)
            above[:, across] = jnp.maximum(
                above[:, across], jnp.max(power.reshape(-1, 8, power.shape[1]), axis=0))
            acc[rows, :] = acc[rows, :] + jnp.dot(
                jnp.exp2(power).astype(jnp.bfloat16), v_cat, preferred_element_type=jnp.float32)

        over_tiles(k_cat, use)

    def full_step(n, _):
        step([inv[STEP * n + i] for i in range(STEP)])
        return 0

    def careful_step(n, _):
        k_cat, v_cat = keys_of([inv[n]])

        def one(g, _):
            at = pl.ds(pl.multiple_of(head * width + g * HD, HD), HD)
            rows = pl.ds(pl.multiple_of(g * tile, tile), tile)
            score = lax.dot_general(q_all[:, at], k_cat, NT, preferred_element_type=jnp.float32)
            old = top[rows, :]
            peak = jnp.maximum(old, jnp.max(score, axis=1, keepdims=True))
            top[rows, :] = peak
            weight = jnp.exp2((score - wide(peak, 1)) * factor)
            shrink = jnp.exp2((old - peak) * factor)
            acc[rows, :] = acc[rows, :] * jnp.concatenate([shrink, shrink], axis=1) + jnp.dot(
                weight.astype(jnp.bfloat16), v_cat, preferred_element_type=jnp.float32)
            return 0

        lax.fori_loop(0, group, one, 0)
        return 0

    diagonal()

    @pl.when(head == 0)
    def _():
        for copy in copies()[3:]:
            copy.wait()

    v_wide[shard:, :HD] = v_all[shard:, lanes]
    above[...] = jnp.zeros_like(above)
    lax.fori_loop(0, earlier // STEP, full_step, 0)
    for rest in range(1, STEP):
        @pl.when(lax.rem(earlier, STEP) == rest)
        def _():
            step([inv[earlier - rest + i] for i in range(rest)])

    @pl.when(jnp.max(above[...]) > LIMIT)
    def _():
        diagonal()
        lax.fori_loop(0, earlier, careful_step, 0)

    for g in range(group):
        part = acc[g * tile:(g + 1) * tile, :]
        at = pl.ds(pl.multiple_of(head * width + g * HD, HD), HD)
        o_ref[:, at] = (part[:, :HD] / part[:, HD:]).astype(o_ref.dtype)
    if not blocks_by_z:
        return

    @pl.when(jnp.logical_and(head == heads - 1, block >= 0))
    def _():
        def column(j, _):
            tile_copy(j).wait()
            across = pl.ds(pl.multiple_of(j * wide_tile, wide_tile), wide_tile)
            far_ref[:, across] = jnp.dot(
                o_ref[...], tiles[j], preferred_element_type=jnp.float32).astype(far_ref.dtype)
            return 0

        lax.fori_loop(0, count, column, 0)


def attend(queries, k_pieces, v_pieces, w_out, order, me, z, chunk, half, after=(), blocks=None,
           columns=0):
    pieces = len(k_pieces)
    shard, kv_width = k_pieces[0].shape
    heads = kv_width // HD
    depth = queries.shape[1]
    keys = shard * pieces
    rows = depth // heads // HD * half
    anywhere = pl.BlockSpec(memory_space=pl.ANY)
    whole = pl.BlockSpec(memory_space=pltpu.VMEM)
    out_shape = [jax.ShapeDtypeStruct((half, depth), jnp.bfloat16)]
    scratch = [
        pltpu.SMEM((order.shape[0],), jnp.int32),
        pltpu.VMEM((half, depth), jnp.bfloat16),
        pltpu.VMEM((keys, kv_width), jnp.bfloat16),
        pltpu.VMEM((keys, kv_width), jnp.bfloat16),
        pltpu.VMEM((keys, 2 * HD), jnp.bfloat16),
        pltpu.VMEM((rows, 2 * HD), jnp.float32),
        pltpu.VMEM((rows, HD), jnp.float32),
        pltpu.VMEM((8, STEP * half), jnp.float32),
        pltpu.SemaphoreType.DMA((2 * pieces + 1,)),
    ]
    if blocks:
        wide = min(columns, 256)
        out_shape.append(jax.ShapeDtypeStruct((half, columns), jnp.bfloat16))
        scratch += [
            pltpu.VMEM((columns // wide, depth, wide), w_out.dtype),
            pltpu.SemaphoreType.DMA((columns // wide,)),
        ]
    return pl.pallas_call(
        functools.partial(attend_kernel, half, chunk, pieces, heads, len(after), blocks),
        out_shape=out_shape,
        grid_spec=pltpu.PrefetchScalarGridSpec(
            num_scalar_prefetch=3,
            grid=(heads,),
            in_specs=[anywhere] * (2 + 2 * pieces + len(after)),
            out_specs=[whole] * len(out_shape),
            scratch_shapes=scratch,
        ),
        compiler_params=pltpu.CompilerParams(vmem_limit_bytes=44 * MIB),
        cost_estimate=pl.CostEstimate(flops=1, bytes_accessed=0, transcendentals=0),
        name="attend",
    )(in_hbm(order), me, z, in_hbm(queries), in_hbm(w_out), in_hbm(k_pieces[0]), *k_pieces[1:],
      in_hbm(v_pieces[0]), *v_pieces[1:], *after)


def hold_kernel(count, *refs):
    outs, sems = refs[-count - 1:-1], refs[-1]
    copies = [pltpu.make_async_copy(refs[i], outs[i], sems.at[i]) for i in range(count)]
    for copy in copies:
        copy.start()
    for copy in copies:
        copy.wait()


def hold(arrays, until):
    count = len(arrays)
    anywhere = pl.BlockSpec(memory_space=pl.ANY)
    return pl.pallas_call(
        functools.partial(hold_kernel, count),
        out_shape=[jax.ShapeDtypeStruct(a.shape, a.dtype) for a in arrays],
        in_specs=[anywhere] * (count + len(until)),
        out_specs=[pl.BlockSpec(memory_space=pltpu.VMEM)] * count,
        scratch_shapes=[pltpu.SemaphoreType.DMA((count,))],
        compiler_params=pltpu.CompilerParams(vmem_limit_bytes=40 * MIB),
        cost_estimate=pl.CostEstimate(flops=1, bytes_accessed=0, transcendentals=0),
        name="hold",
    )(*[in_hbm(a) for a in arrays], *until)


def gather(keys, values, axis):
    count = lax.axis_size(axis)

    def spread(held, bit):
        pairs = [(i, i ^ (1 << bit)) for i in range(count)]
        return {r ^ (1 << bit): lax.ppermute(a, axis, pairs) for r, a in held.items()}

    bits = list(range(1, count.bit_length() - 1))
    k_held, v_held = {0: keys}, {0: values}
    for k_bit, v_bit in zip(bits, bits[::-1]):
        k_held.update(spread(k_held, k_bit))
        v_held.update(spread(v_held, v_bit))
    until = [k_held[count - 2], v_held[count - 2]]
    k_own, v_own = hold([keys, values], until)
    k_held.update(spread({**k_held, 0: k_own}, 0))
    v_held.update(spread({**v_held, 0: v_own}, 0))
    return [k_held[r] for r in range(count)], [v_held[r] for r in range(count)]


def share_kernel(roles, waited, z_ref, w_ref, *refs):
    operands = sum(1 + extra for _, extra in roles)
    out, tiles, sems = refs[operands + waited:]
    count, _, wide = tiles.shape
    for blocks, extra in roles:
        a_ref, arrived, refs = refs[0], refs[1:1 + extra], refs[1 + extra:]
        block = pick(z_ref[0], blocks)

        @pl.when(block >= 0)
        def _(block=block, a_ref=a_ref, arrived=arrived):
            def copy(j):
                place = pl.multiple_of((block * count + j) * wide, wide)
                return pltpu.make_async_copy(
                    w_ref.at[:, pl.ds(place, wide)], tiles.at[j], sems.at[j])

            def column(j, _):
                copy(j).wait()
                lanes = pl.ds(pl.multiple_of(j * wide, wide), wide)
                total = jnp.dot(a_ref[...], tiles[j], preferred_element_type=jnp.float32)
                for ref in arrived:
                    total = total + ref[:, lanes].astype(jnp.float32)
                out[:, lanes] = total.astype(out.dtype)
                return 0

            for j in range(count):
                copy(j).start()
            lax.fori_loop(0, count, column, 0)


def share(roles, w_out, z, columns, after=()):
    tok, depth = roles[0][1].shape
    wide = min(columns, 256)
    count = columns // wide
    whole = pl.BlockSpec(memory_space=pltpu.VMEM)
    anywhere = pl.BlockSpec(memory_space=pl.ANY)
    operands = [a for _, attended, arrived in roles for a in (attended, *arrived)]
    return pl.pallas_call(
        functools.partial(share_kernel, [(b, len(arrived)) for b, _, arrived in roles], len(after)),
        out_shape=jax.ShapeDtypeStruct((tok, columns), jnp.bfloat16),
        grid_spec=pltpu.PrefetchScalarGridSpec(
            num_scalar_prefetch=1,
            grid=(),
            in_specs=[anywhere] + [whole] * len(operands) + [anywhere] * len(after),
            out_specs=whole,
            scratch_shapes=[
                pltpu.VMEM((count, depth, wide), w_out.dtype),
                pltpu.SemaphoreType.DMA((count,)),
            ],
        ),
        compiler_params=pltpu.CompilerParams(vmem_limit_bytes=40 * MIB),
        cost_estimate=pl.CostEstimate(flops=1, bytes_accessed=0, transcendentals=0),
        name="share",
    )(z, in_hbm(w_out), *operands, *after)


def own_kernel(chunks, waited, z_ref, w_ref, *refs):
    a_refs, outs, (tiles, sems) = refs[:chunks], refs[chunks + waited:-2], refs[-2:]
    count, _, wide = tiles.shape

    def copy(j):
        place = pl.multiple_of((z_ref[0] * count + j) * wide, wide)
        return pltpu.make_async_copy(w_ref.at[:, pl.ds(place, wide)], tiles.at[j], sems.at[j])

    def column(j, _):
        copy(j).wait()
        lanes = pl.ds(pl.multiple_of(j * wide, wide), wide)
        rows = jnp.concatenate([ref[...] for ref in a_refs], axis=0)
        total = jnp.dot(rows, tiles[j], preferred_element_type=jnp.float32)
        tok = outs[0].shape[0]
        for i, out in enumerate(outs):
            out[:, lanes] = total[i * tok:(i + 1) * tok]
        return 0

    for j in range(count):
        copy(j).start()
    lax.fori_loop(0, count, column, 0)


def own_columns(chunks, w_out, z, columns, after):
    tok, depth = chunks[0].shape
    wide = min(columns, 256)
    count = columns // wide
    whole = pl.BlockSpec(memory_space=pltpu.VMEM)
    anywhere = pl.BlockSpec(memory_space=pl.ANY)
    return pl.pallas_call(
        functools.partial(own_kernel, len(chunks), len(after)),
        out_shape=[jax.ShapeDtypeStruct((tok, columns), jnp.float32)] * len(chunks),
        grid_spec=pltpu.PrefetchScalarGridSpec(
            num_scalar_prefetch=1,
            grid=(),
            in_specs=[anywhere] + [whole] * len(chunks) + [anywhere] * len(after),
            out_specs=[whole] * len(chunks),
            scratch_shapes=[
                pltpu.VMEM((count, depth, wide), w_out.dtype),
                pltpu.SemaphoreType.DMA((count,)),
            ],
        ),
        compiler_params=pltpu.CompilerParams(vmem_limit_bytes=40 * MIB),
        cost_estimate=pl.CostEstimate(flops=1, bytes_accessed=0, transcendentals=0),
        name="own",
    )(z, in_hbm(w_out), *chunks, *after)


def finish_kernel(extra, chunk, order_ref, me_ref, *refs):
    out, summed, sem = refs[-3:]
    total = refs[0][...].astype(jnp.float32)
    for ref in refs[1:extra]:
        total = total + ref[...].astype(jnp.float32)
    summed[...] = total.astype(summed.dtype)
    tok = summed.shape[0]
    first = pl.multiple_of(block_place(chunk, order_ref, me_ref) * tok, tok)
    copy = pltpu.make_async_copy(summed, out.at[pl.ds(first, tok), :], sem)
    copy.start()
    copy.wait()


def finish(terms, order, me, chunk, whole_tok, out, after=()):
    tok, columns = terms[0].shape
    anywhere = pl.BlockSpec(memory_space=pl.ANY)
    before = [] if out is None else [out]
    return pl.pallas_call(
        functools.partial(finish_kernel, len(terms), chunk),
        out_shape=jax.ShapeDtypeStruct((whole_tok, columns), jnp.bfloat16),
        grid_spec=pltpu.PrefetchScalarGridSpec(
            num_scalar_prefetch=2,
            grid=(),
            in_specs=[pl.BlockSpec(memory_space=pltpu.VMEM)] * len(terms)
            + [anywhere] * len(before + list(after)),
            out_specs=anywhere,
            scratch_shapes=[pltpu.VMEM((tok, columns), jnp.bfloat16), pltpu.SemaphoreType.DMA],
        ),
        input_output_aliases={2 + len(terms): 0} if before else {},
        compiler_params=pltpu.CompilerParams(vmem_limit_bytes=40 * MIB),
        cost_estimate=pl.CostEstimate(flops=1, bytes_accessed=0, transcendentals=0),
        name="finish",
    )(order, me, *terms, *before, *after)


def swap(array, pairs):
    return lax.ppermute(array, "head", pairs)


def line_of_four(attended, w_out, z, order, me, columns, tok):
    outer, inner, back = [(0, 1), (3, 2)], [(1, 2), (2, 1)], [(1, 0), (2, 3)]
    far_end, near_end, last_end = (3, -1, -1, 0), (2, -1, -1, 1), (1, -1, -1, 2)
    far_on, near_on, home_on = (-1, 3, 0, -1), (-1, 2, 1, -1), (-1, 0, 3, -1)

    def part(roles, after=()):
        return share(roles, w_out, z, columns, after)

    a0, far_0 = attended(0, [], far_end)
    near_0 = part([(near_end, a0, [])])
    a1, far_1 = attended(1, [near_0], far_end)
    far_0, near_0, far_1 = swap(far_0, outer), swap(near_0, outer), swap(far_1, outer)
    step = part([(far_on, a0, [far_0])], [a1])
    far_0 = swap(step, inner)
    step = part([(near_end, a1, []), (near_on, a0, [near_0])], [step])
    near_1, near_0 = swap(step, outer), swap(step, inner)
    step = part([(last_end, a0, []), (home_on, a0, [far_0])], [step])
    edge_0 = swap(step, outer + back)
    step = part([(last_end, a1, []), (far_on, a1, [far_1])], [step])
    last_1, far_1 = swap(step, outer), swap(step, inner)
    step = part([(near_on, a1, [near_1])], [step, near_0])
    near_1 = swap(step, inner)
    step = part([(home_on, a1, [far_1])], [step])
    home_1 = swap(step, back)
    own = own_columns([a0, a1], w_out, z, columns, [step])
    out = finish([own[0], near_0, edge_0], order, me, 0, tok, None)
    return finish([own[1], near_1, last_1, home_1], order, me, 1, tok, out)


def per_device(queries, keys, values, w_out, order):
    tok = queries.shape[0]
    half = tok // 2
    line = lax.axis_size("head")
    columns = w_out.shape[1] // line
    me = lax.axis_index("blk").astype(jnp.int32).reshape(1)
    z = lax.axis_index("head").astype(jnp.int32).reshape(1)
    k_pieces, v_pieces = gather(keys, values, "blk")

    def attended(chunk, after, blocks=None):
        return attend(queries, k_pieces, v_pieces, w_out, order, me, z, chunk, half, after, blocks,
                      columns)

    if line == 4:
        return line_of_four(attended, w_out, z, order, me, columns, tok)
    outs = []
    for c in range(2):
        sums = jnp.dot(attended(c, [])[0], w_out, preferred_element_type=jnp.float32)
        outs.append(lax.psum_scatter(
            sums.astype(jnp.bfloat16), "head", scatter_dimension=1, tiled=True))
    swapped = block_place(0, order, me) == 1
    outs = [jnp.where(swapped, outs[1 - c], outs[c]) for c in range(2)]
    return jnp.concatenate(outs, axis=0)


def solution(mesh):
    return jax.shard_map(
        per_device,
        mesh=mesh,
        in_specs=(P("blk", "head"), P("blk", "head"), P("blk", "head"), P("head", None), P()),
        out_specs=P("blk", "head"),
        check_vma=False,
    )
```

```python
import functools
import math

import jax
import jax.numpy as jnp
from jax import lax
from jax.experimental import pallas as pl
from jax.experimental.pallas import tpu as pltpu
from jax.sharding import PartitionSpec as P

HD = 128
NT = (((1,), (1,)), ((), ()))
MIB = 2 ** 20
STEP = 4
LIMIT = 64.0
JOINT = 4


def in_hbm(array):
    return pltpu.with_memory_space_constraint(array, pltpu.HBM)


def block_place(chunk, order_ref, me_ref):
    own = 2 * me_ref[0]
    return jnp.where(order_ref[own] > order_ref[own + 1], 1 - chunk, chunk)


def pick(z, options):
    value = jnp.int32(options[-1])
    for i in range(len(options) - 1):
        value = jnp.where(z == i, jnp.int32(options[i]), value)
    return value


def attend_kernel(half, chunk, pieces, heads, waited, blocks_by_z, order_ref, me_ref, z_ref,
                  q_ref, w_ref, *refs):
    k_refs, v_refs = refs[:pieces], refs[pieces:2 * pieces]
    refs = refs[2 * pieces + waited:]
    if blocks_by_z:
        o_ref, far_ref, *refs, tiles, tile_sems = refs
        count, _, wide_tile = tiles.shape
        block = pick(z_ref[0], blocks_by_z)

        def tile_copy(j):
            place = pl.multiple_of((block * count + j) * wide_tile, wide_tile)
            return pltpu.make_async_copy(
                w_ref.at[:, pl.ds(place, wide_tile)], tiles.at[j], tile_sems.at[j])
    else:
        o_ref, *refs = refs
    inv, q_all, k_all, v_all, v_wide, acc, top, above, sems = refs
    blocks = order_ref.shape[0]
    per = blocks // pieces
    tile = half
    width = o_ref.shape[1] // heads
    group = width // HD
    joint = math.gcd(group, JOINT)
    shard = per * half
    factor = HD ** (-0.5) * math.log2(math.e)
    own = block_place(chunk, order_ref, me_ref)
    me = me_ref[0]
    head = pl.program_id(0)
    lanes = pl.ds(pl.multiple_of(head * HD, HD), HD)

    def copies():
        mine = pl.ds(pl.multiple_of(own * half, half), half)
        pairs = [(q_ref.at[mine, :], q_all)]
        for r in range(pieces):
            here = pl.ds(r * shard, shard)
            pairs += [(k_refs[r], k_all.at[here, :]), (v_refs[r], v_all.at[here, :])]
        return [pltpu.make_async_copy(src, dst, sems.at[i]) for i, (src, dst) in enumerate(pairs)]

    @pl.when(head == 0)
    def _():
        for copy in copies():
            copy.start()
        if blocks_by_z:
            @pl.when(block >= 0)
            def _():
                for j in range(count):
                    tile_copy(j).start()

        def invert(b, _):
            inv[order_ref[b]] = jnp.bitwise_xor(b // per, me) * per + lax.rem(b, per)
            return 0

        lax.fori_loop(0, blocks, invert, 0)
        v_wide[:, HD:] = jnp.ones((v_wide.shape[0], HD), v_wide.dtype)
        for copy in copies()[:3]:
            copy.wait()

    v_wide[:shard, :HD] = v_all[:shard, lanes]
    earlier = order_ref[me * per + own]

    def keys_of(blocks_in):
        rows = [pl.ds(pl.multiple_of(b * half, half), half) for b in blocks_in]
        return (jnp.concatenate([k_all[r, lanes] for r in rows], axis=0),
                jnp.concatenate([v_wide[r, :] for r in rows], axis=0))

    def over_tiles(k_cat, use):
        def scores(g):
            q_cat = jnp.concatenate([
                q_all[:, pl.ds(pl.multiple_of(head * width + i * HD, HD), HD)]
                for i in range(g, g + joint)], axis=0)
            return lax.dot_general(q_cat, k_cat, NT, preferred_element_type=jnp.float32)

        score = scores(0)
        for g in range(0, group, joint):
            ahead = scores(g + joint) if g + joint < group else None
            use(pl.ds(g * tile, joint * tile), score)
            score = ahead

    def diagonal():
        k_cat, v_cat = keys_of([own])
        query = lax.rem(lax.broadcasted_iota(jnp.int32, (joint * tile, half), 0), tile)
        seen = lax.broadcasted_iota(jnp.int32, (joint * tile, half), 1) <= query

        def use(rows, score):
            score = jnp.where(seen, score, -1e30)
            peak = jnp.max(score, axis=1, keepdims=True)
            weight = jnp.exp2((score - peak) * factor)
            top[rows, :] = jnp.broadcast_to(peak, (joint * tile, HD))
            acc[rows, :] = jnp.dot(weight.astype(jnp.bfloat16), v_cat,
                                   preferred_element_type=jnp.float32)

        over_tiles(k_cat, use)

    def wide(array, count):
        return jnp.concatenate([array] * (count * half // HD), axis=1)

    def step(places):
        k_cat, v_cat = keys_of(places)
        count = len(places)

        def use(rows, score):
            power = (score - wide(top[rows, :], count)) * factor
            across = pl.ds(0, count * half)
            above[:, across] = jnp.maximum(
                above[:, across], jnp.max(power.reshape(-1, 8, power.shape[1]), axis=0))
            acc[rows, :] = acc[rows, :] + jnp.dot(
                jnp.exp2(power).astype(jnp.bfloat16), v_cat, preferred_element_type=jnp.float32)

        over_tiles(k_cat, use)

    def full_step(n, _):
        step([inv[STEP * n + i] for i in range(STEP)])
        return 0

    def careful_step(n, _):
        k_cat, v_cat = keys_of([inv[n]])

        def one(g, _):
            at = pl.ds(pl.multiple_of(head * width + g * HD, HD), HD)
            rows = pl.ds(pl.multiple_of(g * tile, tile), tile)
            score = lax.dot_general(q_all[:, at], k_cat, NT, preferred_element_type=jnp.float32)
            old = top[rows, :]
            peak = jnp.maximum(old, jnp.max(score, axis=1, keepdims=True))
            top[rows, :] = peak
            weight = jnp.exp2((score - wide(peak, 1)) * factor)
            shrink = jnp.exp2((old - peak) * factor)
            acc[rows, :] = acc[rows, :] * jnp.concatenate([shrink, shrink], axis=1) + jnp.dot(
                weight.astype(jnp.bfloat16), v_cat, preferred_element_type=jnp.float32)
            return 0

        lax.fori_loop(0, group, one, 0)
        return 0

    diagonal()

    @pl.when(head == 0)
    def _():
        for copy in copies()[3:]:
            copy.wait()

    v_wide[shard:, :HD] = v_all[shard:, lanes]
    above[...] = jnp.zeros_like(above)
    lax.fori_loop(0, earlier // STEP, full_step, 0)
    for rest in range(1, STEP):
        @pl.when(lax.rem(earlier, STEP) == rest)
        def _():
            step([inv[earlier - rest + i] for i in range(rest)])

    @pl.when(jnp.max(above[...]) > LIMIT)
    def _():
        diagonal()
        lax.fori_loop(0, earlier, careful_step, 0)

    for g in range(group):
        part = acc[g * tile:(g + 1) * tile, :]
        at = pl.ds(pl.multiple_of(head * width + g * HD, HD), HD)
        o_ref[:, at] = (part[:, :HD] / part[:, HD:]).astype(o_ref.dtype)
    if not blocks_by_z:
        return

    @pl.when(jnp.logical_and(head == heads - 1, block >= 0))
    def _():
        def column(j, _):
            tile_copy(j).wait()
            across = pl.ds(pl.multiple_of(j * wide_tile, wide_tile), wide_tile)
            far_ref[:, across] = jnp.dot(
                o_ref[...], tiles[j], preferred_element_type=jnp.float32).astype(far_ref.dtype)
            return 0

        lax.fori_loop(0, count, column, 0)


def attend(queries, k_pieces, v_pieces, w_out, order, me, z, chunk, half, after=(), blocks=None,
           columns=0):
    pieces = len(k_pieces)
    shard, kv_width = k_pieces[0].shape
    heads = kv_width // HD
    depth = queries.shape[1]
    keys = shard * pieces
    rows = depth // heads // HD * half
    anywhere = pl.BlockSpec(memory_space=pl.ANY)
    whole = pl.BlockSpec(memory_space=pltpu.VMEM)
    out_shape = [jax.ShapeDtypeStruct((half, depth), jnp.bfloat16)]
    scratch = [
        pltpu.SMEM((order.shape[0],), jnp.int32),
        pltpu.VMEM((half, depth), jnp.bfloat16),
        pltpu.VMEM((keys, kv_width), jnp.bfloat16),
        pltpu.VMEM((keys, kv_width), jnp.bfloat16),
        pltpu.VMEM((keys, 2 * HD), jnp.bfloat16),
        pltpu.VMEM((rows, 2 * HD), jnp.float32),
        pltpu.VMEM((rows, HD), jnp.float32),
        pltpu.VMEM((8, STEP * half), jnp.float32),
        pltpu.SemaphoreType.DMA((2 * pieces + 1,)),
    ]
    if blocks:
        wide = min(columns, 256)
        out_shape.append(jax.ShapeDtypeStruct((half, columns), jnp.bfloat16))
        scratch += [
            pltpu.VMEM((columns // wide, depth, wide), w_out.dtype),
            pltpu.SemaphoreType.DMA((columns // wide,)),
        ]
    return pl.pallas_call(
        functools.partial(attend_kernel, half, chunk, pieces, heads, len(after), blocks),
        out_shape=out_shape,
        grid_spec=pltpu.PrefetchScalarGridSpec(
            num_scalar_prefetch=3,
            grid=(heads,),
            in_specs=[anywhere] * (2 + 2 * pieces + len(after)),
            out_specs=[whole] * len(out_shape),
            scratch_shapes=scratch,
        ),
        compiler_params=pltpu.CompilerParams(vmem_limit_bytes=44 * MIB),
        cost_estimate=pl.CostEstimate(flops=1, bytes_accessed=0, transcendentals=0),
        name="attend",
    )(in_hbm(order), me, z, in_hbm(queries), in_hbm(w_out), in_hbm(k_pieces[0]), *k_pieces[1:],
      in_hbm(v_pieces[0]), *v_pieces[1:], *after)


def hold_kernel(count, *refs):
    outs, sems = refs[-count - 1:-1], refs[-1]
    copies = [pltpu.make_async_copy(refs[i], outs[i], sems.at[i]) for i in range(count)]
    for copy in copies:
        copy.start()
    for copy in copies:
        copy.wait()


def hold(arrays, until):
    count = len(arrays)
    anywhere = pl.BlockSpec(memory_space=pl.ANY)
    return pl.pallas_call(
        functools.partial(hold_kernel, count),
        out_shape=[jax.ShapeDtypeStruct(a.shape, a.dtype) for a in arrays],
        in_specs=[anywhere] * (count + len(until)),
        out_specs=[pl.BlockSpec(memory_space=pltpu.VMEM)] * count,
        scratch_shapes=[pltpu.SemaphoreType.DMA((count,))],
        compiler_params=pltpu.CompilerParams(vmem_limit_bytes=40 * MIB),
        cost_estimate=pl.CostEstimate(flops=1, bytes_accessed=0, transcendentals=0),
        name="hold",
    )(*[in_hbm(a) for a in arrays], *until)


def gather(keys, values, axis):
    count = lax.axis_size(axis)

    def spread(held, bit):
        pairs = [(i, i ^ (1 << bit)) for i in range(count)]
        return {r ^ (1 << bit): lax.ppermute(a, axis, pairs) for r, a in held.items()}

    bits = list(range(1, count.bit_length() - 1))
    k_held, v_held = {0: keys}, {0: values}
    for k_bit, v_bit in zip(bits, bits[::-1]):
        k_held.update(spread(k_held, k_bit))
        v_held.update(spread(v_held, v_bit))
    until = [k_held[1 << bits[0]], v_held[1 << bits[-1]]]
    k_own, v_own = hold([keys, values], until)
    k_held.update(spread({**k_held, 0: k_own}, 0))
    v_held.update(spread({**v_held, 0: v_own}, 0))
    return [k_held[r] for r in range(count)], [v_held[r] for r in range(count)]


def share_kernel(roles, waited, z_ref, w_ref, *refs):
    operands = sum(1 + extra for _, extra in roles)
    out, tiles, sems = refs[operands + waited:]
    count, _, wide = tiles.shape
    for blocks, extra in roles:
        a_ref, arrived, refs = refs[0], refs[1:1 + extra], refs[1 + extra:]
        block = pick(z_ref[0], blocks)

        @pl.when(block >= 0)
        def _(block=block, a_ref=a_ref, arrived=arrived):
            def copy(j):
                place = pl.multiple_of((block * count + j) * wide, wide)
                return pltpu.make_async_copy(
                    w_ref.at[:, pl.ds(place, wide)], tiles.at[j], sems.at[j])

            def column(j, _):
                copy(j).wait()
                lanes = pl.ds(pl.multiple_of(j * wide, wide), wide)
                total = jnp.dot(a_ref[...], tiles[j], preferred_element_type=jnp.float32)
                for ref in arrived:
                    total = total + ref[:, lanes].astype(jnp.float32)
                out[:, lanes] = total.astype(out.dtype)
                return 0

            for j in range(count):
                copy(j).start()
            lax.fori_loop(0, count, column, 0)


def share(roles, w_out, z, columns, after=()):
    tok, depth = roles[0][1].shape
    wide = min(columns, 256)
    count = columns // wide
    whole = pl.BlockSpec(memory_space=pltpu.VMEM)
    anywhere = pl.BlockSpec(memory_space=pl.ANY)
    operands = [a for _, attended, arrived in roles for a in (attended, *arrived)]
    return pl.pallas_call(
        functools.partial(share_kernel, [(b, len(arrived)) for b, _, arrived in roles], len(after)),
        out_shape=jax.ShapeDtypeStruct((tok, columns), jnp.bfloat16),
        grid_spec=pltpu.PrefetchScalarGridSpec(
            num_scalar_prefetch=1,
            grid=(),
            in_specs=[anywhere] + [whole] * len(operands) + [anywhere] * len(after),
            out_specs=whole,
            scratch_shapes=[
                pltpu.VMEM((count, depth, wide), w_out.dtype),
                pltpu.SemaphoreType.DMA((count,)),
            ],
        ),
        compiler_params=pltpu.CompilerParams(vmem_limit_bytes=40 * MIB),
        cost_estimate=pl.CostEstimate(flops=1, bytes_accessed=0, transcendentals=0),
        name="share",
    )(z, in_hbm(w_out), *operands, *after)


def own_kernel(chunks, waited, z_ref, w_ref, *refs):
    a_refs, outs, (tiles, sems) = refs[:chunks], refs[chunks + waited:-2], refs[-2:]
    count, _, wide = tiles.shape

    def copy(j):
        place = pl.multiple_of((z_ref[0] * count + j) * wide, wide)
        return pltpu.make_async_copy(w_ref.at[:, pl.ds(place, wide)], tiles.at[j], sems.at[j])

    def column(j, _):
        copy(j).wait()
        lanes = pl.ds(pl.multiple_of(j * wide, wide), wide)
        rows = jnp.concatenate([ref[...] for ref in a_refs], axis=0)
        total = jnp.dot(rows, tiles[j], preferred_element_type=jnp.float32)
        tok = outs[0].shape[0]
        for i, out in enumerate(outs):
            out[:, lanes] = total[i * tok:(i + 1) * tok]
        return 0

    for j in range(count):
        copy(j).start()
    lax.fori_loop(0, count, column, 0)


def own_columns(chunks, w_out, z, columns, after):
    tok, depth = chunks[0].shape
    wide = min(columns, 256)
    count = columns // wide
    whole = pl.BlockSpec(memory_space=pltpu.VMEM)
    anywhere = pl.BlockSpec(memory_space=pl.ANY)
    return pl.pallas_call(
        functools.partial(own_kernel, len(chunks), len(after)),
        out_shape=[jax.ShapeDtypeStruct((tok, columns), jnp.float32)] * len(chunks),
        grid_spec=pltpu.PrefetchScalarGridSpec(
            num_scalar_prefetch=1,
            grid=(),
            in_specs=[anywhere] + [whole] * len(chunks) + [anywhere] * len(after),
            out_specs=[whole] * len(chunks),
            scratch_shapes=[
                pltpu.VMEM((count, depth, wide), w_out.dtype),
                pltpu.SemaphoreType.DMA((count,)),
            ],
        ),
        compiler_params=pltpu.CompilerParams(vmem_limit_bytes=40 * MIB),
        cost_estimate=pl.CostEstimate(flops=1, bytes_accessed=0, transcendentals=0),
        name="own",
    )(z, in_hbm(w_out), *chunks, *after)


def finish_kernel(extra, chunk, order_ref, me_ref, *refs):
    out, summed, sem = refs[-3:]
    total = refs[0][...].astype(jnp.float32)
    for ref in refs[1:extra]:
        total = total + ref[...].astype(jnp.float32)
    summed[...] = total.astype(summed.dtype)
    tok = summed.shape[0]
    first = pl.multiple_of(block_place(chunk, order_ref, me_ref) * tok, tok)
    copy = pltpu.make_async_copy(summed, out.at[pl.ds(first, tok), :], sem)
    copy.start()
    copy.wait()


def finish(terms, order, me, chunk, whole_tok, out, after=()):
    tok, columns = terms[0].shape
    anywhere = pl.BlockSpec(memory_space=pl.ANY)
    before = [] if out is None else [out]
    return pl.pallas_call(
        functools.partial(finish_kernel, len(terms), chunk),
        out_shape=jax.ShapeDtypeStruct((whole_tok, columns), jnp.bfloat16),
        grid_spec=pltpu.PrefetchScalarGridSpec(
            num_scalar_prefetch=2,
            grid=(),
            in_specs=[pl.BlockSpec(memory_space=pltpu.VMEM)] * len(terms)
            + [anywhere] * len(before + list(after)),
            out_specs=anywhere,
            scratch_shapes=[pltpu.VMEM((tok, columns), jnp.bfloat16), pltpu.SemaphoreType.DMA],
        ),
        input_output_aliases={2 + len(terms): 0} if before else {},
        compiler_params=pltpu.CompilerParams(vmem_limit_bytes=40 * MIB),
        cost_estimate=pl.CostEstimate(flops=1, bytes_accessed=0, transcendentals=0),
        name="finish",
    )(order, me, *terms, *before, *after)


def swap(array, pairs):
    return lax.ppermute(array, "head", pairs)


def line_of_four(attended, w_out, z, order, me, columns, tok):
    outer, inner, back = [(0, 1), (3, 2)], [(1, 2), (2, 1)], [(1, 0), (2, 3)]
    far_end, near_end, last_end = (3, -1, -1, 0), (2, -1, -1, 1), (1, -1, -1, 2)
    far_on, near_on, home_on = (-1, 3, 0, -1), (-1, 2, 1, -1), (-1, 0, 3, -1)

    def part(roles, after=()):
        return share(roles, w_out, z, columns, after)

    a0, far_0 = attended(0, [], far_end)
    near_0 = part([(near_end, a0, [])])
    a1, far_1 = attended(1, [near_0], far_end)
    far_0, near_0, far_1 = swap(far_0, outer), swap(near_0, outer), swap(far_1, outer)
    step = part([(far_on, a0, [far_0])], [a1])
    far_0 = swap(step, inner)
    step = part([(near_end, a1, []), (near_on, a0, [near_0])], [step])
    near_1, near_0 = swap(step, outer), swap(step, inner)
    step = part([(last_end, a0, []), (home_on, a0, [far_0])], [step])
    edge_0 = swap(step, outer + back)
    step = part([(last_end, a1, []), (far_on, a1, [far_1])], [step])
    last_1, far_1 = swap(step, outer), swap(step, inner)
    step = part([(near_on, a1, [near_1])], [step, near_0])
    near_1 = swap(step, inner)
    step = part([(home_on, a1, [far_1])], [step])
    home_1 = swap(step, back)
    own = own_columns([a0, a1], w_out, z, columns, [step])
    out = finish([own[0], near_0, edge_0], order, me, 0, tok, None)
    return finish([own[1], near_1, last_1, home_1], order, me, 1, tok, out)


def per_device(queries, keys, values, w_out, order):
    tok = queries.shape[0]
    half = tok // 2
    line = lax.axis_size("head")
    columns = w_out.shape[1] // line
    me = lax.axis_index("blk").astype(jnp.int32).reshape(1)
    z = lax.axis_index("head").astype(jnp.int32).reshape(1)
    k_pieces, v_pieces = gather(keys, values, "blk")

    def attended(chunk, after, blocks=None):
        return attend(queries, k_pieces, v_pieces, w_out, order, me, z, chunk, half, after, blocks,
                      columns)

    if line == 4:
        return line_of_four(attended, w_out, z, order, me, columns, tok)
    outs = []
    for c in range(2):
        sums = jnp.dot(attended(c, [])[0], w_out, preferred_element_type=jnp.float32)
        outs.append(lax.psum_scatter(
            sums.astype(jnp.bfloat16), "head", scatter_dimension=1, tiled=True))
    swapped = block_place(0, order, me) == 1
    outs = [jnp.where(swapped, outs[1 - c], outs[c]) for c in range(2)]
    return jnp.concatenate(outs, axis=0)


def solution(mesh):
    return jax.shard_map(
        per_device,
        mesh=mesh,
        in_specs=(P("blk", "head"), P("blk", "head"), P("blk", "head"), P("head", None), P()),
        out_specs=P("blk", "head"),
        check_vma=False,
    )
```

```python
import functools
import math

import jax
import jax.numpy as jnp
from jax import lax
from jax.experimental import pallas as pl
from jax.experimental.pallas import tpu as pltpu
from jax.sharding import PartitionSpec as P

HD = 128
NT = (((1,), (1,)), ((), ()))
MIB = 2 ** 20
STEP = 4
LIMIT = 64.0
JOINT = 1024


def in_hbm(array):
    return pltpu.with_memory_space_constraint(array, pltpu.HBM)


def block_place(chunk, order_ref, me_ref):
    own = 2 * me_ref[0]
    return jnp.where(order_ref[own] > order_ref[own + 1], 1 - chunk, chunk)


def pick(z, options):
    value = jnp.int32(options[-1])
    for i in range(len(options) - 1):
        value = jnp.where(z == i, jnp.int32(options[i]), value)
    return value


def attend_kernel(half, chunk, start, pieces, heads, waited, before, blocks_by_z, order_ref, me_ref,
                  z_ref, q_ref, w_ref, *refs):
    k_refs, v_refs = refs[:pieces], refs[pieces:2 * pieces]
    refs = refs[2 * pieces:]
    done_refs, refs = refs[:before], refs[before + waited:]
    if blocks_by_z:
        o_ref, far_ref, *refs, tiles, tile_sems = refs
        count, _, wide_tile = tiles.shape
        block = pick(z_ref[0], blocks_by_z)

        def tile_copy(j):
            place = pl.multiple_of((block * count + j) * wide_tile, wide_tile)
            return pltpu.make_async_copy(
                w_ref.at[:, pl.ds(place, wide_tile)], tiles.at[j], tile_sems.at[j])
    else:
        o_ref, *refs = refs
    inv, q_all, k_all, v_all, v_wide, acc, top, above, sems = refs
    blocks = order_ref.shape[0]
    per = blocks // pieces
    tile = q_all.shape[0]
    width = o_ref.shape[1] // heads
    group = width // HD
    joint = math.gcd(group, JOINT // tile)
    mine = pl.ds(o_ref.shape[0] - tile, tile)
    shard = per * half
    factor = HD ** (-0.5) * math.log2(math.e)
    own = block_place(chunk, order_ref, me_ref)
    me = me_ref[0]
    head = pl.program_id(0)
    lanes = pl.ds(pl.multiple_of(head * HD, HD), HD)

    def copies():
        source = pl.ds(pl.multiple_of(own * half + start, math.gcd(half, start or half)), tile)
        pairs = [(q_ref.at[source, :], q_all)]
        for r in range(pieces):
            here = pl.ds(r * shard, shard)
            pairs += [(k_refs[r], k_all.at[here, :]), (v_refs[r], v_all.at[here, :])]
        return [pltpu.make_async_copy(src, dst, sems.at[i]) for i, (src, dst) in enumerate(pairs)]

    @pl.when(head == 0)
    def _():
        for copy in copies():
            copy.start()
        if blocks_by_z:
            @pl.when(block >= 0)
            def _():
                for j in range(count):
                    tile_copy(j).start()

        def invert(b, _):
            inv[order_ref[b]] = jnp.bitwise_xor(b // per, me) * per + lax.rem(b, per)
            return 0

        lax.fori_loop(0, blocks, invert, 0)
        v_wide[:, HD:] = jnp.ones((v_wide.shape[0], HD), v_wide.dtype)
        for ref in done_refs:
            o_ref[:ref.shape[0], :] = ref[...]
        for copy in copies()[:3]:
            copy.wait()

    v_wide[:shard, :HD] = v_all[:shard, lanes]
    earlier = order_ref[me * per + own]

    def keys_of(blocks_in):
        rows = [pl.ds(pl.multiple_of(b * half, half), half) for b in blocks_in]
        return (jnp.concatenate([k_all[r, lanes] for r in rows], axis=0),
                jnp.concatenate([v_wide[r, :] for r in rows], axis=0))

    def over_tiles(k_cat, use):
        def scores(g):
            q_cat = jnp.concatenate([
                q_all[:, pl.ds(pl.multiple_of(head * width + i * HD, HD), HD)]
                for i in range(g, g + joint)], axis=0)
            return lax.dot_general(q_cat, k_cat, NT, preferred_element_type=jnp.float32)

        score = scores(0)
        for g in range(0, group, joint):
            ahead = scores(g + joint) if g + joint < group else None
            use(pl.ds(g * tile, joint * tile), score)
            score = ahead

    def diagonal():
        k_cat, v_cat = keys_of([own])
        query = lax.rem(lax.broadcasted_iota(jnp.int32, (joint * tile, half), 0), tile) + start
        seen = lax.broadcasted_iota(jnp.int32, (joint * tile, half), 1) <= query

        def use(rows, score):
            score = jnp.where(seen, score, -1e30)
            peak = jnp.max(score, axis=1, keepdims=True)
            weight = jnp.exp2((score - peak) * factor)
            top[rows, :] = jnp.broadcast_to(peak, (joint * tile, HD))
            acc[rows, :] = jnp.dot(weight.astype(jnp.bfloat16), v_cat,
                                   preferred_element_type=jnp.float32)

        over_tiles(k_cat, use)

    def wide(array, count):
        return jnp.concatenate([array] * (count * half // HD), axis=1)

    def step(places):
        k_cat, v_cat = keys_of(places)
        count = len(places)

        def use(rows, score):
            power = (score - wide(top[rows, :], count)) * factor
            across = pl.ds(0, count * half)
            above[:, across] = jnp.maximum(
                above[:, across], jnp.max(power.reshape(-1, 8, power.shape[1]), axis=0))
            acc[rows, :] = acc[rows, :] + jnp.dot(
                jnp.exp2(power).astype(jnp.bfloat16), v_cat, preferred_element_type=jnp.float32)

        over_tiles(k_cat, use)

    def full_step(n, _):
        step([inv[STEP * n + i] for i in range(STEP)])
        return 0

    def careful_step(n, _):
        k_cat, v_cat = keys_of([inv[n]])

        def one(g, _):
            at = pl.ds(pl.multiple_of(head * width + g * HD, HD), HD)
            rows = pl.ds(pl.multiple_of(g * tile, tile), tile)
            score = lax.dot_general(q_all[:, at], k_cat, NT, preferred_element_type=jnp.float32)
            old = top[rows, :]
            peak = jnp.maximum(old, jnp.max(score, axis=1, keepdims=True))
            top[rows, :] = peak
            weight = jnp.exp2((score - wide(peak, 1)) * factor)
            shrink = jnp.exp2((old - peak) * factor)
            acc[rows, :] = acc[rows, :] * jnp.concatenate([shrink, shrink], axis=1) + jnp.dot(
                weight.astype(jnp.bfloat16), v_cat, preferred_element_type=jnp.float32)
            return 0

        lax.fori_loop(0, group, one, 0)
        return 0

    diagonal()

    @pl.when(head == 0)
    def _():
        for copy in copies()[3:]:
            copy.wait()

    v_wide[shard:, :HD] = v_all[shard:, lanes]
    above[...] = jnp.zeros_like(above)
    lax.fori_loop(0, earlier // STEP, full_step, 0)
    for rest in range(1, STEP):
        @pl.when(lax.rem(earlier, STEP) == rest)
        def _():
            step([inv[earlier - rest + i] for i in range(rest)])

    @pl.when(jnp.max(above[...]) > LIMIT)
    def _():
        diagonal()
        lax.fori_loop(0, earlier, careful_step, 0)

    for g in range(group):
        part = acc[g * tile:(g + 1) * tile, :]
        at = pl.ds(pl.multiple_of(head * width + g * HD, HD), HD)
        o_ref[mine, at] = (part[:, :HD] / part[:, HD:]).astype(o_ref.dtype)
    if not blocks_by_z:
        return

    @pl.when(jnp.logical_and(head == heads - 1, block >= 0))
    def _():
        def column(j, _):
            tile_copy(j).wait()
            across = pl.ds(pl.multiple_of(j * wide_tile, wide_tile), wide_tile)
            far_ref[:, across] = jnp.dot(
                o_ref[mine, :], tiles[j], preferred_element_type=jnp.float32).astype(far_ref.dtype)
            return 0

        lax.fori_loop(0, count, column, 0)


def attend(queries, k_pieces, v_pieces, w_out, order, me, z, chunk, half, after=(), blocks=None,
           columns=0, before=(), tok=None):
    tok = tok or half
    start = sum(a.shape[0] for a in before)
    pieces = len(k_pieces)
    shard, kv_width = k_pieces[0].shape
    heads = kv_width // HD
    depth = queries.shape[1]
    keys = shard * pieces
    rows = depth // heads // HD * tok
    anywhere = pl.BlockSpec(memory_space=pl.ANY)
    whole = pl.BlockSpec(memory_space=pltpu.VMEM)
    out_shape = [jax.ShapeDtypeStruct((start + tok, depth), jnp.bfloat16)]
    scratch = [
        pltpu.SMEM((order.shape[0],), jnp.int32),
        pltpu.VMEM((tok, depth), jnp.bfloat16),
        pltpu.VMEM((keys, kv_width), jnp.bfloat16),
        pltpu.VMEM((keys, kv_width), jnp.bfloat16),
        pltpu.VMEM((keys, 2 * HD), jnp.bfloat16),
        pltpu.VMEM((rows, 2 * HD), jnp.float32),
        pltpu.VMEM((rows, HD), jnp.float32),
        pltpu.VMEM((8, STEP * half), jnp.float32),
        pltpu.SemaphoreType.DMA((2 * pieces + 1,)),
    ]
    if blocks:
        wide = min(columns, 256)
        out_shape.append(jax.ShapeDtypeStruct((tok, columns), jnp.bfloat16))
        scratch += [
            pltpu.VMEM((columns // wide, depth, wide), w_out.dtype),
            pltpu.SemaphoreType.DMA((columns // wide,)),
        ]
    return pl.pallas_call(
        functools.partial(attend_kernel, half, chunk, start, pieces, heads, len(after), len(before),
                          blocks),
        out_shape=out_shape,
        grid_spec=pltpu.PrefetchScalarGridSpec(
            num_scalar_prefetch=3,
            grid=(heads,),
            in_specs=[anywhere] * (2 + 2 * pieces) + [whole] * len(before) + [anywhere] * len(after),
            out_specs=[whole] * len(out_shape),
            scratch_shapes=scratch,
        ),
        compiler_params=pltpu.CompilerParams(vmem_limit_bytes=44 * MIB),
        cost_estimate=pl.CostEstimate(flops=1, bytes_accessed=0, transcendentals=0),
        name="attend",
    )(in_hbm(order), me, z, in_hbm(queries), in_hbm(w_out), in_hbm(k_pieces[0]), *k_pieces[1:],
      in_hbm(v_pieces[0]), *v_pieces[1:], *before, *after)


def hold_kernel(count, *refs):
    outs, sems = refs[-count - 1:-1], refs[-1]
    copies = [pltpu.make_async_copy(refs[i], outs[i], sems.at[i]) for i in range(count)]
    for copy in copies:
        copy.start()
    for copy in copies:
        copy.wait()


def hold(arrays, until):
    count = len(arrays)
    anywhere = pl.BlockSpec(memory_space=pl.ANY)
    return pl.pallas_call(
        functools.partial(hold_kernel, count),
        out_shape=[jax.ShapeDtypeStruct(a.shape, a.dtype) for a in arrays],
        in_specs=[anywhere] * (count + len(until)),
        out_specs=[pl.BlockSpec(memory_space=pltpu.VMEM)] * count,
        scratch_shapes=[pltpu.SemaphoreType.DMA((count,))],
        compiler_params=pltpu.CompilerParams(vmem_limit_bytes=40 * MIB),
        cost_estimate=pl.CostEstimate(flops=1, bytes_accessed=0, transcendentals=0),
        name="hold",
    )(*[in_hbm(a) for a in arrays], *until)


def gather(keys, values, axis):
    count = lax.axis_size(axis)

    def spread(held, bit):
        pairs = [(i, i ^ (1 << bit)) for i in range(count)]
        return {r ^ (1 << bit): lax.ppermute(a, axis, pairs) for r, a in held.items()}

    bits = list(range(1, count.bit_length() - 1))
    k_held, v_held = {0: keys}, {0: values}
    for k_bit, v_bit in zip(bits, bits[::-1]):
        k_held.update(spread(k_held, k_bit))
        v_held.update(spread(v_held, v_bit))
    until = [k_held[1 << bits[0]], v_held[1 << bits[-1]]]
    k_own, v_own = hold([keys, values], until)
    k_held.update(spread({**k_held, 0: k_own}, 0))
    v_held.update(spread({**v_held, 0: v_own}, 0))
    return [k_held[r] for r in range(count)], [v_held[r] for r in range(count)]


def share_kernel(roles, waited, z_ref, w_ref, *refs):
    operands = sum(1 + extra for _, extra in roles)
    out, tiles, sems = refs[operands + waited:]
    count, _, wide = tiles.shape
    for blocks, extra in roles:
        a_ref, arrived, refs = refs[0], refs[1:1 + extra], refs[1 + extra:]
        block = pick(z_ref[0], blocks)

        @pl.when(block >= 0)
        def _(block=block, a_ref=a_ref, arrived=arrived):
            def copy(j):
                place = pl.multiple_of((block * count + j) * wide, wide)
                return pltpu.make_async_copy(
                    w_ref.at[:, pl.ds(place, wide)], tiles.at[j], sems.at[j])

            def column(j, _):
                copy(j).wait()
                lanes = pl.ds(pl.multiple_of(j * wide, wide), wide)
                total = jnp.dot(a_ref[...], tiles[j], preferred_element_type=jnp.float32)
                if arrived:
                    total = total + jnp.concatenate(
                        [ref[:, lanes] for ref in arrived], axis=0).astype(jnp.float32)
                out[:, lanes] = total.astype(out.dtype)
                return 0

            for j in range(count):
                copy(j).start()
            lax.fori_loop(0, count, column, 0)


def share(roles, w_out, z, columns, after=()):
    tok, depth = roles[0][1].shape
    wide = min(columns, 256)
    count = columns // wide
    whole = pl.BlockSpec(memory_space=pltpu.VMEM)
    anywhere = pl.BlockSpec(memory_space=pl.ANY)
    operands = [a for _, attended, arrived in roles for a in (attended, *arrived)]
    return pl.pallas_call(
        functools.partial(share_kernel, [(b, len(arrived)) for b, _, arrived in roles], len(after)),
        out_shape=jax.ShapeDtypeStruct((tok, columns), jnp.bfloat16),
        grid_spec=pltpu.PrefetchScalarGridSpec(
            num_scalar_prefetch=1,
            grid=(),
            in_specs=[anywhere] + [whole] * len(operands) + [anywhere] * len(after),
            out_specs=whole,
            scratch_shapes=[
                pltpu.VMEM((count, depth, wide), w_out.dtype),
                pltpu.SemaphoreType.DMA((count,)),
            ],
        ),
        compiler_params=pltpu.CompilerParams(vmem_limit_bytes=40 * MIB),
        cost_estimate=pl.CostEstimate(flops=1, bytes_accessed=0, transcendentals=0),
        name="share",
    )(z, in_hbm(w_out), *operands, *after)


def own_kernel(chunks, waited, z_ref, w_ref, *refs):
    a_refs, outs, (tiles, sems) = refs[:chunks], refs[chunks + waited:-2], refs[-2:]
    count, _, wide = tiles.shape

    def copy(j):
        place = pl.multiple_of((z_ref[0] * count + j) * wide, wide)
        return pltpu.make_async_copy(w_ref.at[:, pl.ds(place, wide)], tiles.at[j], sems.at[j])

    def column(j, _):
        copy(j).wait()
        lanes = pl.ds(pl.multiple_of(j * wide, wide), wide)
        rows = jnp.concatenate([ref[...] for ref in a_refs], axis=0)
        total = jnp.dot(rows, tiles[j], preferred_element_type=jnp.float32)
        tok = outs[0].shape[0]
        for i, out in enumerate(outs):
            out[:, lanes] = total[i * tok:(i + 1) * tok]
        return 0

    for j in range(count):
        copy(j).start()
    lax.fori_loop(0, count, column, 0)


def own_columns(chunks, w_out, z, columns, after):
    tok, depth = chunks[0].shape
    wide = min(columns, 256)
    count = columns // wide
    whole = pl.BlockSpec(memory_space=pltpu.VMEM)
    anywhere = pl.BlockSpec(memory_space=pl.ANY)
    return pl.pallas_call(
        functools.partial(own_kernel, len(chunks), len(after)),
        out_shape=[jax.ShapeDtypeStruct((tok, columns), jnp.float32)] * len(chunks),
        grid_spec=pltpu.PrefetchScalarGridSpec(
            num_scalar_prefetch=1,
            grid=(),
            in_specs=[anywhere] + [whole] * len(chunks) + [anywhere] * len(after),
            out_specs=[whole] * len(chunks),
            scratch_shapes=[
                pltpu.VMEM((count, depth, wide), w_out.dtype),
                pltpu.SemaphoreType.DMA((count,)),
            ],
        ),
        compiler_params=pltpu.CompilerParams(vmem_limit_bytes=40 * MIB),
        cost_estimate=pl.CostEstimate(flops=1, bytes_accessed=0, transcendentals=0),
        name="own",
    )(z, in_hbm(w_out), *chunks, *after)


def finish_kernel(extra, chunk, order_ref, me_ref, *refs):
    out, summed, sem = refs[-3:]
    total = refs[0][...].astype(jnp.float32)
    for ref in refs[1:extra]:
        total = total + ref[...].astype(jnp.float32)
    summed[...] = total.astype(summed.dtype)
    tok = summed.shape[0]
    first = pl.multiple_of(block_place(chunk, order_ref, me_ref) * tok, tok)
    copy = pltpu.make_async_copy(summed, out.at[pl.ds(first, tok), :], sem)
    copy.start()
    copy.wait()


def finish(terms, order, me, chunk, whole_tok, out, after=()):
    tok, columns = terms[0].shape
    anywhere = pl.BlockSpec(memory_space=pl.ANY)
    before = [] if out is None else [out]
    return pl.pallas_call(
        functools.partial(finish_kernel, len(terms), chunk),
        out_shape=jax.ShapeDtypeStruct((whole_tok, columns), jnp.bfloat16),
        grid_spec=pltpu.PrefetchScalarGridSpec(
            num_scalar_prefetch=2,
            grid=(),
            in_specs=[pl.BlockSpec(memory_space=pltpu.VMEM)] * len(terms)
            + [anywhere] * len(before + list(after)),
            out_specs=anywhere,
            scratch_shapes=[pltpu.VMEM((tok, columns), jnp.bfloat16), pltpu.SemaphoreType.DMA],
        ),
        input_output_aliases={2 + len(terms): 0} if before else {},
        compiler_params=pltpu.CompilerParams(vmem_limit_bytes=40 * MIB),
        cost_estimate=pl.CostEstimate(flops=1, bytes_accessed=0, transcendentals=0),
        name="finish",
    )(order, me, *terms, *before, *after)


def swap(array, pairs):
    return lax.ppermute(array, "head", pairs)


def line_of_four(attended, w_out, z, order, me, columns, tok):
    outer, inner, back = [(0, 1), (3, 2)], [(1, 2), (2, 1)], [(1, 0), (2, 3)]
    far_end, near_end, last_end = (3, -1, -1, 0), (2, -1, -1, 1), (1, -1, -1, 2)
    far_on, near_on, home_on = (-1, 3, 0, -1), (-1, 2, 1, -1), (-1, 0, 3, -1)

    def part(roles, after=()):
        return share(roles, w_out, z, columns, after)

    split = tok // 4
    a0, far_0 = attended(0, [], far_end, [], split)
    a0, far_0b = attended(0, [], far_end, [a0], split)
    near_0 = part([(near_end, a0, [])])
    far_0, far_0b = swap(far_0, outer), swap(far_0b, outer)
    a1, far_1 = attended(1, [near_0, far_0], far_end)
    near_0, far_1 = swap(near_0, outer), swap(far_1, outer)
    step = part([(far_on, a0, [far_0, far_0b])], [a1])
    far_0 = swap(step, inner)
    step = part([(near_end, a1, []), (near_on, a0, [near_0])], [step])
    near_1, near_0 = swap(step, outer), swap(step, inner)
    step = part([(last_end, a0, []), (home_on, a0, [far_0])], [step])
    edge_0 = swap(step, outer + back)
    step = part([(last_end, a1, []), (far_on, a1, [far_1])], [step])
    last_1, far_1 = swap(step, outer), swap(step, inner)
    step = part([(near_on, a1, [near_1])], [step, near_0])
    near_1 = swap(step, inner)
    step = part([(home_on, a1, [far_1])], [step])
    home_1 = swap(step, back)
    own = own_columns([a0, a1], w_out, z, columns, [step])
    out = finish([own[0], near_0, edge_0], order, me, 0, tok, None)
    return finish([own[1], near_1, last_1, home_1], order, me, 1, tok, out)


def per_device(queries, keys, values, w_out, order):
    tok = queries.shape[0]
    half = tok // 2
    line = lax.axis_size("head")
    columns = w_out.shape[1] // line
    me = lax.axis_index("blk").astype(jnp.int32).reshape(1)
    z = lax.axis_index("head").astype(jnp.int32).reshape(1)
    k_pieces, v_pieces = gather(keys, values, "blk")

    def attended(chunk, after, blocks=None, before=(), rows=None):
        return attend(queries, k_pieces, v_pieces, w_out, order, me, z, chunk, half, after, blocks,
                      columns, before, rows)

    if line == 4:
        return line_of_four(attended, w_out, z, order, me, columns, tok)
    outs = []
    for c in range(2):
        sums = jnp.dot(attended(c, [])[0], w_out, preferred_element_type=jnp.float32)
        outs.append(lax.psum_scatter(
            sums.astype(jnp.bfloat16), "head", scatter_dimension=1, tiled=True))
    swapped = block_place(0, order, me) == 1
    outs = [jnp.where(swapped, outs[1 - c], outs[c]) for c in range(2)]
    return jnp.concatenate(outs, axis=0)


def solution(mesh):
    return jax.shard_map(
        per_device,
        mesh=mesh,
        in_specs=(P("blk", "head"), P("blk", "head"), P("blk", "head"), P("head", None), P()),
        out_specs=P("blk", "head"),
        check_vma=False,
    )
```

```python
import functools
import math

import jax
import jax.numpy as jnp
from jax import lax
from jax.experimental import pallas as pl
from jax.experimental.pallas import tpu as pltpu
from jax.sharding import PartitionSpec as P

HD = 128
NT = (((1,), (1,)), ((), ()))
MIB = 2 ** 20
STEP = 4
LIMIT = 64.0
JOINT = 1024


def in_hbm(array):
    return pltpu.with_memory_space_constraint(array, pltpu.HBM)


def block_place(chunk, order_ref, me_ref):
    own = 2 * me_ref[0]
    return jnp.where(order_ref[own] > order_ref[own + 1], 1 - chunk, chunk)


def pick(z, options):
    value = jnp.int32(options[-1])
    for i in range(len(options) - 1):
        value = jnp.where(z == i, jnp.int32(options[i]), value)
    return value


def attend_kernel(half, chunk, start, pieces, packed, heads, waited, before, blocks_by_z,
                  order_ref, me_ref, z_ref, q_ref, w_ref, *refs):
    if packed:
        k_all, v_all, *refs = refs
    else:
        k_refs, v_refs, refs = refs[:pieces], refs[pieces:2 * pieces], refs[2 * pieces:]
    done_refs, refs = refs[:before], refs[before + waited:]
    if blocks_by_z:
        o_ref, far_ref, *refs, tiles, tile_sems = refs
        count, _, wide_tile = tiles.shape
        block = pick(z_ref[0], blocks_by_z)

        def tile_copy(j):
            place = pl.multiple_of((block * count + j) * wide_tile, wide_tile)
            return pltpu.make_async_copy(
                w_ref.at[:, pl.ds(place, wide_tile)], tiles.at[j], tile_sems.at[j])
    else:
        o_ref, *refs = refs
    if not packed:
        k_all, v_all, *refs = refs
    inv, q_all, v_wide, acc, top, above, sems = refs
    blocks = order_ref.shape[0]
    per = blocks // pieces
    tile = q_all.shape[0]
    width = o_ref.shape[1] // heads
    group = width // HD
    joint = math.gcd(group, JOINT // tile)
    mine = pl.ds(o_ref.shape[0] - tile, tile)
    shard = per * half
    factor = HD ** (-0.5) * math.log2(math.e)
    own = block_place(chunk, order_ref, me_ref)
    me = me_ref[0]
    head = pl.program_id(0)
    lanes = pl.ds(pl.multiple_of(head * HD, HD), HD)

    def copies():
        source = pl.ds(pl.multiple_of(own * half + start, math.gcd(half, start or half)), tile)
        pairs = [(q_ref.at[source, :], q_all)]
        for r in range(0 if packed else pieces):
            here = pl.ds(r * shard, shard)
            pairs += [(k_refs[r], k_all.at[here, :]), (v_refs[r], v_all.at[here, :])]
        return [pltpu.make_async_copy(src, dst, sems.at[i]) for i, (src, dst) in enumerate(pairs)]

    @pl.when(head == 0)
    def _():
        for copy in copies():
            copy.start()
        if blocks_by_z:
            @pl.when(block >= 0)
            def _():
                for j in range(count):
                    tile_copy(j).start()

        def invert(b, _):
            inv[order_ref[b]] = jnp.bitwise_xor(b // per, me) * per + lax.rem(b, per)
            return 0

        lax.fori_loop(0, blocks, invert, 0)
        v_wide[:, HD:] = jnp.ones((v_wide.shape[0], HD), v_wide.dtype)
        for ref in done_refs:
            o_ref[:ref.shape[0], :] = ref[...]
        for copy in copies()[:1 if packed else 3]:
            copy.wait()

    v_wide[:shard, :HD] = v_all[:shard, lanes]
    earlier = order_ref[me * per + own]

    def keys_of(blocks_in):
        rows = [pl.ds(pl.multiple_of(b * half, half), half) for b in blocks_in]
        return (jnp.concatenate([k_all[r, lanes] for r in rows], axis=0),
                jnp.concatenate([v_wide[r, :] for r in rows], axis=0))

    def over_tiles(k_cat, use):
        def scores(g):
            q_cat = jnp.concatenate([
                q_all[:, pl.ds(pl.multiple_of(head * width + i * HD, HD), HD)]
                for i in range(g, g + joint)], axis=0)
            return lax.dot_general(q_cat, k_cat, NT, preferred_element_type=jnp.float32)

        score = scores(0)
        for g in range(0, group, joint):
            ahead = scores(g + joint) if g + joint < group else None
            use(pl.ds(g * tile, joint * tile), score)
            score = ahead

    def diagonal():
        k_cat, v_cat = keys_of([own])
        query = lax.rem(lax.broadcasted_iota(jnp.int32, (joint * tile, half), 0), tile) + start
        seen = lax.broadcasted_iota(jnp.int32, (joint * tile, half), 1) <= query

        def use(rows, score):
            score = jnp.where(seen, score, -1e30)
            peak = jnp.max(score, axis=1, keepdims=True)
            weight = jnp.exp2((score - peak) * factor)
            top[rows, :] = jnp.broadcast_to(peak, (joint * tile, HD))
            acc[rows, :] = jnp.dot(weight.astype(jnp.bfloat16), v_cat,
                                   preferred_element_type=jnp.float32)

        over_tiles(k_cat, use)

    def wide(array, count):
        return jnp.concatenate([array] * (count * half // HD), axis=1)

    def step(places):
        k_cat, v_cat = keys_of(places)
        count = len(places)

        def use(rows, score):
            power = (score - wide(top[rows, :], count)) * factor
            across = pl.ds(0, count * half)
            above[:, across] = jnp.maximum(
                above[:, across], jnp.max(power.reshape(-1, 8, power.shape[1]), axis=0))
            acc[rows, :] = acc[rows, :] + jnp.dot(
                jnp.exp2(power).astype(jnp.bfloat16), v_cat, preferred_element_type=jnp.float32)

        over_tiles(k_cat, use)

    def full_step(n, _):
        step([inv[STEP * n + i] for i in range(STEP)])
        return 0

    def careful_step(n, _):
        k_cat, v_cat = keys_of([inv[n]])

        def one(g, _):
            at = pl.ds(pl.multiple_of(head * width + g * HD, HD), HD)
            rows = pl.ds(pl.multiple_of(g * tile, tile), tile)
            score = lax.dot_general(q_all[:, at], k_cat, NT, preferred_element_type=jnp.float32)
            old = top[rows, :]
            peak = jnp.maximum(old, jnp.max(score, axis=1, keepdims=True))
            top[rows, :] = peak
            weight = jnp.exp2((score - wide(peak, 1)) * factor)
            shrink = jnp.exp2((old - peak) * factor)
            acc[rows, :] = acc[rows, :] * jnp.concatenate([shrink, shrink], axis=1) + jnp.dot(
                weight.astype(jnp.bfloat16), v_cat, preferred_element_type=jnp.float32)
            return 0

        lax.fori_loop(0, group, one, 0)
        return 0

    diagonal()

    @pl.when(head == 0)
    def _():
        for copy in copies()[3:]:
            copy.wait()

    v_wide[shard:, :HD] = v_all[shard:, lanes]
    above[...] = jnp.zeros_like(above)
    lax.fori_loop(0, earlier // STEP, full_step, 0)
    for rest in range(1, STEP):
        @pl.when(lax.rem(earlier, STEP) == rest)
        def _():
            step([inv[earlier - rest + i] for i in range(rest)])

    @pl.when(jnp.max(above[...]) > LIMIT)
    def _():
        diagonal()
        lax.fori_loop(0, earlier, careful_step, 0)

    for g in range(group):
        part = acc[g * tile:(g + 1) * tile, :]
        at = pl.ds(pl.multiple_of(head * width + g * HD, HD), HD)
        o_ref[mine, at] = (part[:, :HD] / part[:, HD:]).astype(o_ref.dtype)
    if not blocks_by_z:
        return

    @pl.when(jnp.logical_and(head == heads - 1, block >= 0))
    def _():
        def column(j, _):
            tile_copy(j).wait()
            across = pl.ds(pl.multiple_of(j * wide_tile, wide_tile), wide_tile)
            far_ref[:, across] = jnp.dot(
                o_ref[mine, :], tiles[j], preferred_element_type=jnp.float32).astype(far_ref.dtype)
            return 0

        lax.fori_loop(0, count, column, 0)


def attend(queries, k_pieces, v_pieces, w_out, order, me, z, chunk, half, after=(), blocks=None,
           columns=0, before=(), tok=None, packed=()):
    tok = tok or half
    start = sum(a.shape[0] for a in before)
    pieces = len(k_pieces)
    shard, kv_width = k_pieces[0].shape
    heads = kv_width // HD
    depth = queries.shape[1]
    keys = shard * pieces
    rows = depth // heads // HD * tok
    anywhere = pl.BlockSpec(memory_space=pl.ANY)
    whole = pl.BlockSpec(memory_space=pltpu.VMEM)
    out_shape = [jax.ShapeDtypeStruct((start + tok, depth), jnp.bfloat16)]
    scratch = [
        pltpu.SMEM((order.shape[0],), jnp.int32),
        pltpu.VMEM((tok, depth), jnp.bfloat16),
        pltpu.VMEM((keys, 2 * HD), jnp.bfloat16),
        pltpu.VMEM((rows, 2 * HD), jnp.float32),
        pltpu.VMEM((rows, HD), jnp.float32),
        pltpu.VMEM((8, STEP * half), jnp.float32),
        pltpu.SemaphoreType.DMA((2 * pieces + 1,)),
    ]
    if blocks:
        wide = min(columns, 256)
        out_shape.append(jax.ShapeDtypeStruct((tok, columns), jnp.bfloat16))
        scratch += [
            pltpu.VMEM((columns // wide, depth, wide), w_out.dtype),
            pltpu.SemaphoreType.DMA((columns // wide,)),
        ]
    if packed:
        given = [whole] * 2
        operands = list(packed)
    else:
        given = [anywhere] * (2 * pieces)
        operands = [in_hbm(k_pieces[0]), *k_pieces[1:], in_hbm(v_pieces[0]), *v_pieces[1:]]
        out_shape += [jax.ShapeDtypeStruct((keys, kv_width), jnp.bfloat16)] * 2
    return pl.pallas_call(
        functools.partial(attend_kernel, half, chunk, start, pieces, bool(packed), heads,
                          len(after), len(before), blocks),
        out_shape=out_shape,
        grid_spec=pltpu.PrefetchScalarGridSpec(
            num_scalar_prefetch=3,
            grid=(heads,),
            in_specs=[anywhere] * 2 + given + [whole] * len(before) + [anywhere] * len(after),
            out_specs=[whole] * len(out_shape),
            scratch_shapes=scratch,
        ),
        compiler_params=pltpu.CompilerParams(vmem_limit_bytes=44 * MIB),
        cost_estimate=pl.CostEstimate(flops=1, bytes_accessed=0, transcendentals=0),
        name="attend",
    )(in_hbm(order), me, z, in_hbm(queries), in_hbm(w_out), *operands, *before, *after)


def hold_kernel(count, *refs):
    outs, sems = refs[-count - 1:-1], refs[-1]
    copies = [pltpu.make_async_copy(refs[i], outs[i], sems.at[i]) for i in range(count)]
    for copy in copies:
        copy.start()
    for copy in copies:
        copy.wait()


def hold(arrays, until):
    count = len(arrays)
    anywhere = pl.BlockSpec(memory_space=pl.ANY)
    return pl.pallas_call(
        functools.partial(hold_kernel, count),
        out_shape=[jax.ShapeDtypeStruct(a.shape, a.dtype) for a in arrays],
        in_specs=[anywhere] * (count + len(until)),
        out_specs=[pl.BlockSpec(memory_space=pltpu.VMEM)] * count,
        scratch_shapes=[pltpu.SemaphoreType.DMA((count,))],
        compiler_params=pltpu.CompilerParams(vmem_limit_bytes=40 * MIB),
        cost_estimate=pl.CostEstimate(flops=1, bytes_accessed=0, transcendentals=0),
        name="hold",
    )(*[in_hbm(a) for a in arrays], *until)


def gather(keys, values, axis):
    count = lax.axis_size(axis)

    def spread(held, bit):
        pairs = [(i, i ^ (1 << bit)) for i in range(count)]
        return {r ^ (1 << bit): lax.ppermute(a, axis, pairs) for r, a in held.items()}

    bits = list(range(1, count.bit_length() - 1))
    k_held, v_held = {0: keys}, {0: values}
    for k_bit, v_bit in zip(bits, bits[::-1]):
        k_held.update(spread(k_held, k_bit))
        v_held.update(spread(v_held, v_bit))
    until = [k_held[1 << bits[0]], v_held[1 << bits[-1]]]
    k_own, v_own = hold([keys, values], until)
    k_held.update(spread({**k_held, 0: k_own}, 0))
    v_held.update(spread({**v_held, 0: v_own}, 0))
    return [k_held[r] for r in range(count)], [v_held[r] for r in range(count)]


def share_kernel(roles, waited, z_ref, w_ref, *refs):
    operands = sum(1 + extra for _, extra in roles)
    out, tiles, sems = refs[operands + waited:]
    count, _, wide = tiles.shape
    for blocks, extra in roles:
        a_ref, arrived, refs = refs[0], refs[1:1 + extra], refs[1 + extra:]
        block = pick(z_ref[0], blocks)

        @pl.when(block >= 0)
        def _(block=block, a_ref=a_ref, arrived=arrived):
            def copy(j):
                place = pl.multiple_of((block * count + j) * wide, wide)
                return pltpu.make_async_copy(
                    w_ref.at[:, pl.ds(place, wide)], tiles.at[j], sems.at[j])

            def column(j, _):
                copy(j).wait()
                lanes = pl.ds(pl.multiple_of(j * wide, wide), wide)
                total = jnp.dot(a_ref[...], tiles[j], preferred_element_type=jnp.float32)
                if arrived:
                    total = total + jnp.concatenate(
                        [ref[:, lanes] for ref in arrived], axis=0).astype(jnp.float32)
                out[:, lanes] = total.astype(out.dtype)
                return 0

            for j in range(count):
                copy(j).start()
            lax.fori_loop(0, count, column, 0)


def share(roles, w_out, z, columns, after=()):
    tok, depth = roles[0][1].shape
    wide = min(columns, 256)
    count = columns // wide
    whole = pl.BlockSpec(memory_space=pltpu.VMEM)
    anywhere = pl.BlockSpec(memory_space=pl.ANY)
    operands = [a for _, attended, arrived in roles for a in (attended, *arrived)]
    return pl.pallas_call(
        functools.partial(share_kernel, [(b, len(arrived)) for b, _, arrived in roles], len(after)),
        out_shape=jax.ShapeDtypeStruct((tok, columns), jnp.bfloat16),
        grid_spec=pltpu.PrefetchScalarGridSpec(
            num_scalar_prefetch=1,
            grid=(),
            in_specs=[anywhere] + [whole] * len(operands) + [anywhere] * len(after),
            out_specs=whole,
            scratch_shapes=[
                pltpu.VMEM((count, depth, wide), w_out.dtype),
                pltpu.SemaphoreType.DMA((count,)),
            ],
        ),
        compiler_params=pltpu.CompilerParams(vmem_limit_bytes=40 * MIB),
        cost_estimate=pl.CostEstimate(flops=1, bytes_accessed=0, transcendentals=0),
        name="share",
    )(z, in_hbm(w_out), *operands, *after)


def own_kernel(chunks, waited, z_ref, w_ref, *refs):
    a_refs, outs, (tiles, sems) = refs[:chunks], refs[chunks + waited:-2], refs[-2:]
    count, _, wide = tiles.shape

    def copy(j):
        place = pl.multiple_of((z_ref[0] * count + j) * wide, wide)
        return pltpu.make_async_copy(w_ref.at[:, pl.ds(place, wide)], tiles.at[j], sems.at[j])

    def column(j, _):
        copy(j).wait()
        lanes = pl.ds(pl.multiple_of(j * wide, wide), wide)
        rows = jnp.concatenate([ref[...] for ref in a_refs], axis=0)
        total = jnp.dot(rows, tiles[j], preferred_element_type=jnp.float32)
        tok = outs[0].shape[0]
        for i, out in enumerate(outs):
            out[:, lanes] = total[i * tok:(i + 1) * tok]
        return 0

    for j in range(count):
        copy(j).start()
    lax.fori_loop(0, count, column, 0)


def own_columns(chunks, w_out, z, columns, after):
    tok, depth = chunks[0].shape
    wide = min(columns, 256)
    count = columns // wide
    whole = pl.BlockSpec(memory_space=pltpu.VMEM)
    anywhere = pl.BlockSpec(memory_space=pl.ANY)
    return pl.pallas_call(
        functools.partial(own_kernel, len(chunks), len(after)),
        out_shape=[jax.ShapeDtypeStruct((tok, columns), jnp.float32)] * len(chunks),
        grid_spec=pltpu.PrefetchScalarGridSpec(
            num_scalar_prefetch=1,
            grid=(),
            in_specs=[anywhere] + [whole] * len(chunks) + [anywhere] * len(after),
            out_specs=[whole] * len(chunks),
            scratch_shapes=[
                pltpu.VMEM((count, depth, wide), w_out.dtype),
                pltpu.SemaphoreType.DMA((count,)),
            ],
        ),
        compiler_params=pltpu.CompilerParams(vmem_limit_bytes=40 * MIB),
        cost_estimate=pl.CostEstimate(flops=1, bytes_accessed=0, transcendentals=0),
        name="own",
    )(z, in_hbm(w_out), *chunks, *after)


def finish_kernel(extra, chunk, order_ref, me_ref, *refs):
    out, summed, sem = refs[-3:]
    total = refs[0][...].astype(jnp.float32)
    for ref in refs[1:extra]:
        total = total + ref[...].astype(jnp.float32)
    summed[...] = total.astype(summed.dtype)
    tok = summed.shape[0]
    first = pl.multiple_of(block_place(chunk, order_ref, me_ref) * tok, tok)
    copy = pltpu.make_async_copy(summed, out.at[pl.ds(first, tok), :], sem)
    copy.start()
    copy.wait()


def finish(terms, order, me, chunk, whole_tok, out, after=()):
    tok, columns = terms[0].shape
    anywhere = pl.BlockSpec(memory_space=pl.ANY)
    before = [] if out is None else [out]
    return pl.pallas_call(
        functools.partial(finish_kernel, len(terms), chunk),
        out_shape=jax.ShapeDtypeStruct((whole_tok, columns), jnp.bfloat16),
        grid_spec=pltpu.PrefetchScalarGridSpec(
            num_scalar_prefetch=2,
            grid=(),
            in_specs=[pl.BlockSpec(memory_space=pltpu.VMEM)] * len(terms)
            + [anywhere] * len(before + list(after)),
            out_specs=anywhere,
            scratch_shapes=[pltpu.VMEM((tok, columns), jnp.bfloat16), pltpu.SemaphoreType.DMA],
        ),
        input_output_aliases={2 + len(terms): 0} if before else {},
        compiler_params=pltpu.CompilerParams(vmem_limit_bytes=40 * MIB),
        cost_estimate=pl.CostEstimate(flops=1, bytes_accessed=0, transcendentals=0),
        name="finish",
    )(order, me, *terms, *before, *after)


def swap(array, pairs):
    return lax.ppermute(array, "head", pairs)


def line_of_four(attended, w_out, z, order, me, columns, tok):
    outer, inner, back = [(0, 1), (3, 2)], [(1, 2), (2, 1)], [(1, 0), (2, 3)]
    far_end, near_end, last_end = (3, -1, -1, 0), (2, -1, -1, 1), (1, -1, -1, 2)
    far_on, near_on, home_on = (-1, 3, 0, -1), (-1, 2, 1, -1), (-1, 0, 3, -1)

    def part(roles, after=()):
        return share(roles, w_out, z, columns, after)

    split = tok // 4
    a0, far_0, *packed = attended(0, [], far_end, [], split)
    a0, far_0b = attended(0, [], far_end, [a0], split, packed)
    near_0 = part([(near_end, a0, [])])
    far_0, far_0b = swap(far_0, outer), swap(far_0b, outer)
    a1, far_1 = attended(1, [near_0, far_0], far_end, packed=packed)
    near_0, far_1 = swap(near_0, outer), swap(far_1, outer)
    step = part([(far_on, a0, [far_0, far_0b])], [a1])
    far_0 = swap(step, inner)
    step = part([(near_end, a1, []), (near_on, a0, [near_0])], [step])
    near_1, near_0 = swap(step, outer), swap(step, inner)
    step = part([(last_end, a0, []), (home_on, a0, [far_0])], [step])
    edge_0 = swap(step, outer + back)
    step = part([(last_end, a1, []), (far_on, a1, [far_1])], [step])
    last_1, far_1 = swap(step, outer), swap(step, inner)
    step = part([(near_on, a1, [near_1])], [step, near_0])
    near_1 = swap(step, inner)
    step = part([(home_on, a1, [far_1])], [step])
    home_1 = swap(step, back)
    own = own_columns([a0, a1], w_out, z, columns, [step])
    out = finish([own[0], near_0, edge_0], order, me, 0, tok, None)
    return finish([own[1], near_1, last_1, home_1], order, me, 1, tok, out)


def per_device(queries, keys, values, w_out, order):
    tok = queries.shape[0]
    half = tok // 2
    line = lax.axis_size("head")
    columns = w_out.shape[1] // line
    me = lax.axis_index("blk").astype(jnp.int32).reshape(1)
    z = lax.axis_index("head").astype(jnp.int32).reshape(1)
    k_pieces, v_pieces = gather(keys, values, "blk")

    def attended(chunk, after, blocks=None, before=(), rows=None, packed=()):
        return attend(queries, k_pieces, v_pieces, w_out, order, me, z, chunk, half, after, blocks,
                      columns, before, rows, packed)

    if line == 4:
        return line_of_four(attended, w_out, z, order, me, columns, tok)
    outs = []
    for c in range(2):
        sums = jnp.dot(attended(c, [])[0], w_out, preferred_element_type=jnp.float32)
        outs.append(lax.psum_scatter(
            sums.astype(jnp.bfloat16), "head", scatter_dimension=1, tiled=True))
    swapped = block_place(0, order, me) == 1
    outs = [jnp.where(swapped, outs[1 - c], outs[c]) for c in range(2)]
    return jnp.concatenate(outs, axis=0)


def solution(mesh):
    return jax.shard_map(
        per_device,
        mesh=mesh,
        in_specs=(P("blk", "head"), P("blk", "head"), P("blk", "head"), P("head", None), P()),
        out_specs=P("blk", "head"),
        check_vma=False,
    )
```
